32 devices in a mesh: dp: 8 (over z, y), seq: 4 (over x, core).
Axes of the slice: x: 2, y: 2, z: 4, core: 2. Of those that a mesh axis runs over, the one named last changes fastest.
Arguments:
- inputs: bfloat16 [24, 2048, 512], P('dp', 'seq'), may hold values from -6 to 6
- gains: float32 [1, 2, 512], replicated, may hold values from 0.5 to 1.5
- w_qkv: bfloat16 [1, 512, 1536], replicated, may hold values from -0.125 to 0.125
- w_out: bfloat16 [1, 512, 512], replicated, may hold values from -1 to 1
- ffn_weight: bfloat16 [1, 2, 2048, 512], P(None, None, ('dp', 'seq')), may hold values from -0.25 to 0.25
- omega: bfloat16 [1, 8, 256, 64], replicated, may hold values from -5 to 5
- cotangent: bfloat16 [24, 2048, 512], P('dp', 'seq'), may hold values from -6 to 6
Outputs:
- outputs: bfloat16 [24, 2048, 512], P('dp', 'seq')
- grad_inputs: float32 [24, 2048, 512], P('dp', 'seq')
- grad_gains: float32 [1, 2, 512], replicated
- grad_w_qkv: float32 [1, 512, 1536], replicated
- grad_w_out: float32 [1, 512, 512], replicated
- grad_ffn: float32 [1, 2, 2048, 512], P(None, None, ('dp', 'seq'))
The draws below stay inside these ranges and needn't reach their ends.
All inputs are finite; a program needn't handle non-finite values.
Results may differ from the reference program's by a relative error of at most 0.017.
Values may be sent and summed in bfloat16 or wider, within the bound.
No kernel may reach another device: no remote copies, remote signals or barrier semaphores. Data moves between devices by JAX's collectives and lax.ppermute only.
A program may use at most 320 MiB of HBM per device.

```python
import math
import jax
import jax.numpy as jnp
from jax import lax

HEADS = 8
HD = 64
D = 512
FEATS = 256
FF = 2048
LAYERS = 1
LENGTH = 2048
BATCH = 24
N_SEQ = 4


def steps_of(own_key, shape, cuts, least, largest):
    factor_of = 1.0
    for dim, parts in cuts:
        draws = jax.random.uniform(jax.random.fold_in(jax.random.fold_in(own_key, 6), dim), (parts,), jnp.float32, least / len(cuts), largest / len(cuts))
        factor_of = factor_of * jnp.repeat(jnp.exp(draws), shape[dim] // parts).reshape((-1,) + (1,) * (len(shape) - 1 - dim))
    return factor_of


def normal_values(key, shape, scale, most, shards=(), kind=jnp.bfloat16):
    array = jax.random.normal(key, shape, jnp.float32) * scale
    if len(shards) > 0:
        array = steps_of(key, shape, shards, -0.22, 0.18) * array
    return jnp.clip(array, min=-most, max=most).astype(kind)


def setup_inputs(seed: int = 0) -> dict:
    key_list = jax.random.split(jax.random.key(seed), 8)
    inputs = normal_values(key_list[0], (BATCH, LENGTH, D), 1.0, 6.0, ((0, 8), (1, 4)))
    gains = jnp.clip(1.0 + 0.1 * jax.random.normal(key_list[1], (LAYERS, 2, D), jnp.float32), 0.5, 1.5)
    w_qkv = normal_values(key_list[2], (LAYERS, D, 3 * D), (4 * D) ** -0.5, 0.125)
    w_out = normal_values(key_list[3], (LAYERS, D, D), (D // 16) ** -0.5, 1.0)
    ffn_weight = normal_values(key_list[4], (LAYERS, 2, FF, D), D ** -0.5, 0.25, ((2, 32),))
    omega = normal_values(key_list[5], (LAYERS, HEADS, FEATS, HD), 1.0, 5.0)
    cotangent = normal_values(key_list[6], (BATCH, LENGTH, D), 1.0, 6.0, ((0, 8), (1, 4)))
    return dict(inputs=inputs, gains=gains, w_qkv=w_qkv, w_out=w_out, ffn_weight=ffn_weight, omega=omega, cotangent=cotangent)


epsilon = 1e-05
highest = lax.Precision.HIGHEST

@jax.custom_vjp
def low(v):
    return lax.optimization_barrier(v.astype(jnp.bfloat16)).astype(jnp.float32)

@jax.custom_vjp
def low_back(v):
    return v

def low_keep(v):
    return (low(v), None)

def low_pass(kept, grad):
    return (grad,)

def back_keep(v):
    return (v, None)

def back_low(kept, grad):
    return (low(grad),)
low.defvjp(low_keep, low_pass)
low_back.defvjp(back_keep, back_low)

def layer_norm(values, gain_row):
    center = values - lax.optimization_barrier(jnp.mean(values, axis=-1, keepdims=True))
    spread = lax.optimization_barrier(jnp.mean(center * center, axis=-1, keepdims=True))
    return center * lax.rsqrt(spread + epsilon) * gain_row

def feature_map(projected, queries):
    head_dim = queries.shape[-1]
    feature_scale = head_dim ** (-0.25)
    energy = lax.optimization_barrier(jnp.sum(queries * queries, axis=-1, keepdims=True))
    return jnp.exp(feature_scale * projected - 0.5 * feature_scale * feature_scale * energy) / math.sqrt(projected.shape[-1])

def gelu_exact(values):
    return jax.nn.gelu(values, approximate=False)

def causal_mask(block_len):
    positions = jnp.arange(block_len)
    return (positions[:, None] >= positions[None, :]).astype(jnp.float32)

def attention_branch(stream, gain_row, w_qkv, w_out, omega_layer):
    length_all, model_width = stream.shape
    head_count, feature_count, head_dim = omega_layer.shape
    block_len = length_all // N_SEQ
    hidden_low = low(layer_norm(stream, gain_row))
    qkv_low = low(low_back(jnp.dot(hidden_low, w_qkv, precision=highest)))
    queries = qkv_low[:, :model_width].reshape(length_all, head_count, head_dim)
    key_rows = qkv_low[:, model_width:2 * model_width].reshape(length_all, head_count, head_dim)
    value_rows = qkv_low[:, 2 * model_width:].reshape(length_all, head_count, head_dim)
    proj_q = low_back(jnp.einsum('thd,hfd->thf', queries, omega_layer, precision=highest))
    proj_k = low_back(jnp.einsum('thd,hfd->thf', key_rows, omega_layer, precision=highest))
    phi_q = low(feature_map(proj_q, queries))
    phi_k = low(feature_map(proj_k, key_rows))
    causal = causal_mask(block_len)

    def block_step(carried, pieces):
        prev_state, prev_norm = carried
        block_q, block_k, block_v = pieces
        scores = low_back(jnp.einsum('thf,shf->hts', block_q, block_k, precision=highest) * causal[None])
        numerator = low_back(jnp.einsum('hts,shd->thd', low(scores), block_v, precision=highest) + jnp.einsum('thf,hfd->thd', block_q, prev_state, precision=highest))
        denominator = lax.optimization_barrier(jnp.sum(scores, axis=-1)).T + jnp.einsum('thf,hf->th', block_q, prev_norm, precision=highest)
        local_state = jnp.einsum('thf,thd->hfd', block_k, block_v, precision=highest)
        local_norm = lax.optimization_barrier(jnp.sum(block_k, axis=0))
        return ((prev_state + local_state, prev_norm + local_norm), numerator / denominator[:, :, None])
    start = (jnp.zeros((head_count, feature_count, head_dim), jnp.float32), jnp.zeros((head_count, feature_count), jnp.float32))
    pieces = (phi_q.reshape(N_SEQ, block_len, head_count, feature_count), phi_k.reshape(N_SEQ, block_len, head_count, feature_count), value_rows.reshape(N_SEQ, block_len, head_count, head_dim))
    _, mixed_heads = lax.scan(jax.checkpoint(block_step), start, pieces)
    mixed_low = low(mixed_heads.reshape(length_all, model_width))
    return low_back(jnp.dot(mixed_low, w_out, precision=highest))

def ffn_branch(stream, gain_row, weight_pair):
    hidden_low = low(layer_norm(stream, gain_row))
    pre_act = low_back(jnp.einsum('tc,jc->tj', hidden_low, weight_pair[0], precision=highest))
    act_low = low(gelu_exact(pre_act))
    return low_back(jnp.dot(act_low, weight_pair[1], precision=highest))

def sequence_forward(params, omega_all, sequence):
    gains, w_qkv, w_out, ffn_weight = params
    stream = sequence
    for layer_index in range(LAYERS):
        stream = stream + attention_branch(stream, gains[layer_index, 0], w_qkv[layer_index], w_out[layer_index], omega_all[layer_index])
        stream = stream + ffn_branch(stream, gains[layer_index, 1], ffn_weight[layer_index])
    return stream

def reference(inputs, gains, w_qkv, w_out, ffn_weight, omega, cotangent):
    params = (gains.astype(jnp.float32), w_qkv.astype(jnp.float32), w_out.astype(jnp.float32), ffn_weight.astype(jnp.float32))
    omega_all = omega.astype(jnp.float32)

    def forward(weights, sequences):
        return lax.map(jax.checkpoint(lambda sequence: sequence_forward(weights, omega_all, sequence)), sequences)
    result_out, pullback = jax.vjp(forward, params, inputs.astype(jnp.float32))
    grad_params, grad_inputs = pullback(cotangent.astype(jnp.float32))
    return (result_out.astype(jnp.bfloat16), grad_inputs, grad_params[0], grad_params[1], grad_params[2], grad_params[3])
```

```python
import functools
import math

import jax
import jax.numpy as jnp
from jax import lax
from jax.experimental import pallas as pl
from jax.experimental.pallas import tpu as pltpu
from jax.sharding import PartitionSpec as P

epsilon = 1e-05
bf16 = jnp.bfloat16
f32 = jnp.float32
AXES = ("dp", "seq")
MIB = 2**20
A_ROWS = 48


def nn(a, b):
    return lax.dot_general(a, b, (((1,), (0,)), ((), ())), preferred_element_type=f32)


def nt(a, b):
    return lax.dot_general(a, b, (((1,), (1,)), ((), ())), preferred_element_type=f32)


def tn(a, b):
    return lax.dot_general(a, b, (((0,), (0,)), ((), ())), preferred_element_type=f32)


def lanes_of(shape):
    return lax.broadcasted_iota(jnp.int32, shape, len(shape) - 1)


def params(mib=56):
    return pltpu.CompilerParams(vmem_limit_bytes=mib * MIB)


def cost(flops, nbytes, trans=0):
    return pl.CostEstimate(flops=int(flops), bytes_accessed=int(nbytes), transcendentals=int(trans))


def const_block(shape):
    return pl.BlockSpec(shape, lambda *_: (0,) * len(shape))


def stacked_call(kernel, grid, in_specs, out_specs, out_shapes, stacked, before, args, scratch, estimate):
    n_in = len(args)
    aliases = {}
    extra = []
    if before is not None:
        for at, (flag, buffer) in enumerate(zip(stacked, before)):
            if flag:
                aliases[n_in + len(extra)] = at
                extra.append(buffer)
    n_extra = len(extra)

    def body(*refs):
        kernel(*refs[:n_in], *refs[n_in + n_extra :])

    return pl.pallas_call(
        body,
        grid=grid,
        in_specs=list(in_specs) + [pl.BlockSpec(memory_space=pl.ANY)] * n_extra,
        out_specs=out_specs,
        out_shape=out_shapes,
        scratch_shapes=scratch,
        input_output_aliases=aliases,
        compiler_params=params(),
        cost_estimate=estimate,
    )(*args, *extra)


def normed(values):
    center = values - jnp.mean(values, axis=-1, keepdims=True)
    spread = jnp.mean(center * center, axis=-1, keepdims=True)
    scale = lax.rsqrt(spread + epsilon)
    return center * scale, scale


def norm_back(grad, xhat, scale, gain):
    gy = grad * gain
    return scale * (
        gy - jnp.mean(gy, axis=-1, keepdims=True) - xhat * jnp.mean(gy * xhat, axis=-1, keepdims=True)
    )


def causal_tile(rows):
    return lax.broadcasted_iota(jnp.int32, (rows, rows), 0) >= lax.broadcasted_iota(
        jnp.int32, (rows, rows), 1
    )


def feature_weights(omega):
    heads, feats, hd = omega.shape
    pairs = omega.reshape(heads // 2, 2, feats, hd)
    ones = jnp.full((heads // 2, feats, hd), -1.0, omega.dtype)
    zeros = jnp.zeros_like(ones)
    even = jnp.concatenate([pairs[:, 0], ones, ones, zeros], axis=-1)
    odd = jnp.concatenate([ones, pairs[:, 1], zeros, ones], axis=-1)
    return jnp.stack([even, odd], axis=1).reshape(heads, feats, 4 * hd)


def features_kernel(hd, x_ref, gains_ref, w_ref, wf_ref, qkv_ref, phiq_ref, phik_ref, h1_ref, state_ref, qkv_scr):
    pair = pl.program_id(0)
    width = 2 * hd
    model = x_ref.shape[-1]
    s = hd ** (-0.25)
    feats = wf_ref.shape[1]

    @pl.when(pair == 0)
    def _():
        xhat, _ = normed(x_ref[0].astype(f32))
        hidden = (xhat * gains_ref[0:1, :]).astype(bf16)
        h1_ref[0] = hidden
        for part in range(3):
            cols = slice(part * model, (part + 1) * model)
            made = nn(hidden, w_ref[:, cols]).astype(bf16)
            qkv_ref[0, :, cols] = made
            qkv_scr[part] = made

    column = pl.ds(pl.multiple_of(pair * width, width), width)
    rows = x_ref.shape[1]
    low = lanes_of((rows, width)) < hd

    def phi_pair(part, out_ref):
        points = qkv_scr[part, :, column].astype(f32)
        energy = points * points * (0.5 * s)
        high = energy.astype(bf16).astype(f32)
        rest = (energy - high).astype(bf16)
        turned = pltpu.roll(high, hd, 1)
        made = []
        for odd in range(2):
            first = jnp.where(low, turned, points) if odd else jnp.where(low, points, turned)
            left = jnp.concatenate([first.astype(bf16), rest], axis=1)
            proj = nt(left, wf_ref[odd])
            phi = jnp.exp2(proj * (s * math.log2(math.e)) - 0.5 * math.log2(feats))
            phi_low = phi.astype(bf16)
            out_ref[0, :, odd * feats : (odd + 1) * feats] = phi_low
            made.append(phi_low)
        return made

    phi_pair(0, phiq_ref)
    even_k, odd_k = phi_pair(1, phik_ref)
    values = qkv_scr[2, :, column]
    state_ref[0, 0:hd, :] = tn(values, even_k)[0:hd].astype(bf16)
    state_ref[0, hd:width, :] = tn(values, odd_k)[hd:width].astype(bf16)
    sums = jnp.concatenate(
        [
            jnp.sum(even_k.astype(f32), axis=0, keepdims=True),
            jnp.sum(odd_k.astype(f32), axis=0, keepdims=True),
            jnp.zeros((14, feats), f32),
        ],
        axis=0,
    )
    state_ref[0, width : width + 16, :] = sums.astype(bf16)


def features_call(index, inputs, gains, w_qkv, wf, before, hd):
    batch, rows, model = inputs.shape
    heads, feats, _ = wf.shape
    pairs = heads // 2
    width = 2 * hd
    n_rows = width + 16
    return stacked_call(
        functools.partial(features_kernel, hd),
        (pairs,),
        [
            pl.BlockSpec((1, rows, model), lambda p: (index, 0, 0)),
            const_block(gains.shape),
            const_block(w_qkv.shape),
            pl.BlockSpec((2, feats, 4 * hd), lambda p: (p, 0, 0)),
        ],
        [
            pl.BlockSpec((1, rows, 3 * model), lambda p: (index, 0, 0)),
            pl.BlockSpec((1, rows, 2 * feats), lambda p: (index, 0, p)),
            pl.BlockSpec((1, rows, 2 * feats), lambda p: (index, 0, p)),
            pl.BlockSpec((1, rows, model), lambda p: (index, 0, 0)),
            pl.BlockSpec((1, n_rows, feats), lambda p: (p, 0, 0)),
        ],
        [
            jax.ShapeDtypeStruct((batch, rows, 3 * model), bf16),
            jax.ShapeDtypeStruct((batch, rows, heads * feats), bf16),
            jax.ShapeDtypeStruct((batch, rows, heads * feats), bf16),
            jax.ShapeDtypeStruct((batch, rows, model), bf16),
            jax.ShapeDtypeStruct((pairs, n_rows, feats), bf16),
        ],
        (True, True, True, True, False),
        before,
        (inputs, gains, w_qkv, wf),
        [pltpu.VMEM((3, rows, model), bf16)],
        cost(2 * rows * model * 3 * model + 4 * heads * rows * 256 * feats, 8 * MIB, 2 * rows * heads * feats),
    )


def state_block(state_refs, place, pair, hd):
    if len(state_refs) == 1:
        total = state_refs[0][0].astype(f32)
    else:
        near, got, other = state_refs
        mine = jnp.where(pair // got.half == place["core"], 1.0, 0.0)
        total = (
            got.ref[0].astype(f32) * mine
            + other.ref[0].astype(f32) * (1.0 - mine)
            + near[0].astype(f32) * place["near"]
        )
    feats = total.shape[-1]
    width = 2 * hd
    zeros = jnp.zeros((hd, feats), bf16)
    low = total.astype(bf16)
    even_norm = jnp.broadcast_to(total[width : width + 1], (hd, feats)).astype(bf16)
    odd_norm = jnp.broadcast_to(total[width + 1 : width + 2], (hd, feats)).astype(bf16)
    even = jnp.concatenate([low[0:hd], zeros, even_norm, zeros], axis=0)
    odd = jnp.concatenate([zeros, low[hd:width], zeros, odd_norm], axis=0)
    return even, odd


class Half:
    def __init__(self, ref, half):
        self.ref = ref
        self.half = half


def state_refs_of(refs, pairs):
    if len(refs) == 1:
        return refs
    return refs[0], Half(refs[1], pairs // 2), Half(refs[2], pairs // 2)


def place_of(backward):
    seq = lax.axis_index("seq")
    core = lax.rem(seq, 2)
    near = jnp.where(core == (0 if backward else 1), 1.0, 0.0)
    return {"core": core, "near": near}


def state_specs(states, pairs):
    shape = (1,) + states[0].shape[1:]
    specs = [pl.BlockSpec(shape, lambda p: (p, 0, 0))]
    if len(states) > 1:
        specs += [pl.BlockSpec(shape, lambda p: (lax.rem(p, pairs // 2), 0, 0))] * 2
    return specs


def mix_kernel(hd, n_states, tile, *refs):
    x_ref, gains_ref, wout_ref, phiq_ref, phik_ref, v_ref = refs[:6]
    state_refs = refs[6 : 6 + n_states]
    scores_ref, mixed_ref, rden_ref, x1_ref, h2_ref, mixed_scr = refs[6 + n_states :]
    pair = pl.program_id(0)
    pairs = pl.num_programs(0)
    width = 2 * hd
    rows = x_ref.shape[1]
    feats = phiq_ref.shape[-1] // 2
    tiles = rows // tile
    column = pl.ds(pl.multiple_of(pair * width, width), width)
    even_state, odd_state = state_block(
        state_refs_of(state_refs, wout_ref.shape[0] // width), place_of(False), pair, hd
    )
    both_state = jnp.concatenate([even_state, odd_state], axis=1)
    low = lanes_of((rows, width)) < hd
    values = v_ref[0].astype(f32)
    ones = jnp.where(low, 1.0, 0.0)
    sides = [
        jnp.concatenate([jnp.where(low, values, 0.0), ones], axis=1).astype(bf16),
        jnp.concatenate([jnp.where(low, 0.0, values), 1.0 - ones], axis=1).astype(bf16),
    ]
    causal = causal_tile(tile)
    for at in range(tiles):
        here = slice(at * tile, (at + 1) * tile)
        end = (at + 1) * tile
        total = nt(phiq_ref[0, here, :], both_state)
        for odd in range(2):
            cols = slice(odd * feats, (odd + 1) * feats)
            made = nt(phiq_ref[0, here, cols], phik_ref[0, 0:end, cols])
            last = jnp.where(causal, made[:, at * tile : end], 0.0)
            made = last if at == 0 else jnp.concatenate([made[:, : at * tile], last], axis=1)
            made = made.astype(bf16)
            scores_ref[0, odd, here, 0:end] = made
            total = total + nn(made, sides[odd][0:end])
        rden = 1.0 / total[:, width:]
        mixed = (total[:, :width] * rden).astype(bf16)
        rden_ref[0, here, :] = rden
        mixed_ref[0, here, :] = mixed
        mixed_scr[here, column] = mixed

    @pl.when(pair == pairs - 1)
    def _():
        x1 = x_ref[0].astype(f32) + nn(mixed_scr[...], wout_ref[...])
        x1_ref[0] = x1
        xhat, _ = normed(x1)
        h2_ref[0] = (xhat * gains_ref[1:2, :]).astype(bf16)


def mix_call(index, inputs, gains, w_out, phi_q, phi_k, qkv, states, before, hd):
    batch, rows, model = inputs.shape
    width = 2 * hd
    pairs = model // width
    heads = 2 * pairs
    feats = phi_q.shape[-1] // heads
    tile = min(256, rows)
    return stacked_call(
        functools.partial(mix_kernel, hd, len(states), tile),
        (pairs,),
        [
            pl.BlockSpec((1, rows, model), lambda p: (index, 0, 0)),
            const_block(gains.shape),
            const_block(w_out.shape),
            pl.BlockSpec((1, rows, 2 * feats), lambda p: (index, 0, p)),
            pl.BlockSpec((1, rows, 2 * feats), lambda p: (index, 0, p)),
            pl.BlockSpec((1, rows, width), lambda p: (index, 0, 2 * pairs + p)),
        ]
        + state_specs(states, pairs),
        [
            pl.BlockSpec((1, 2, rows, rows), lambda p: (index, p, 0, 0)),
            pl.BlockSpec((1, rows, width), lambda p: (index, 0, p)),
            pl.BlockSpec((1, rows, width), lambda p: (index, 0, p)),
            pl.BlockSpec((1, rows, model), lambda p: (index, 0, 0)),
            pl.BlockSpec((1, rows, model), lambda p: (index, 0, 0)),
        ],
        [
            jax.ShapeDtypeStruct((batch, heads, rows, rows), bf16),
            jax.ShapeDtypeStruct((batch, rows, model), bf16),
            jax.ShapeDtypeStruct((batch, rows, model), f32),
            jax.ShapeDtypeStruct((batch, rows, model), f32),
            jax.ShapeDtypeStruct((batch, rows, model), bf16),
        ],
        (True,) * 5,
        before,
        (inputs, gains, w_out, phi_q, phi_k, qkv) + tuple(states),
        [pltpu.VMEM((rows, model), bf16)],
        cost(heads * 2 * rows * rows * 512 + 2 * rows * model * model, 12 * MIB),
    )


def ffn_kernel(n_weights, copies, groups, batch, split_out, *refs):
    h2_ref, gf_ref, x1_ref = refs[:3]
    weights = refs[3 : 3 + n_weights]
    n_out = 6 if split_out else 4
    outs = refs[3 + n_weights : 3 + n_weights + n_out]
    out_ref, gh2_ref = outs[:2]
    up_scr, down_scr, act_scr, pre_scr, sems = refs[3 + n_weights + n_out :]
    step = pl.program_id(0)
    n_blocks = pl.num_programs(0) - batch
    block = act_scr.shape[-1] // n_blocks
    rows = h2_ref.shape[1]
    model = h2_ref.shape[2]
    started = [
        pltpu.make_async_copy(src(weights), dst(up_scr, down_scr), sems.at[at])
        for at, (src, dst, _) in enumerate(copies)
    ]

    @pl.when(step == 0)
    def _():
        for copy in started:
            copy.start()

    for group in range(groups):

        @pl.when(step == group * (n_blocks // groups))
        def _():
            for copy, (_, _, own) in zip(started, copies):
                if own == group:
                    copy.wait()

    @pl.when(step < n_blocks)
    def _():
        if split_out:
            up = up_scr[step // 4, lax.rem(step, 4)].reshape(block, model)
            down = down_scr[step // 4, lax.rem(step, 4)].reshape(block, model)
        else:
            up = up_scr[step]
            down = down_scr[step]
        cols = pl.ds(pl.multiple_of(step * block, block), block)
        grad_up = jnp.zeros((block, model), f32)
        grad_down = jnp.zeros((block, model), f32)
        for b in range(batch):
            pre = nt(h2_ref[b], up)
            part = 0.5 * lax.erf(pre * math.sqrt(0.5)) + 0.5
            act = (pre * part).astype(bf16)
            act_scr[b, :, cols] = act
            slope = part + pre * (
                jnp.exp2(pre * pre * (-0.5 * math.log2(math.e))) * (1.0 / math.sqrt(2.0 * math.pi))
            )
            grad_pre = (nt(gf_ref[b], down) * slope).astype(bf16)
            pre_scr[b, :, cols] = grad_pre
            grad_down = grad_down + tn(act, gf_ref[b])
            grad_up = grad_up + tn(grad_pre, h2_ref[b])
        if split_out:
            up_low = grad_up.astype(bf16).reshape(4, block // 4, model)
            down_low = grad_down.astype(bf16).reshape(4, block // 4, model)
            for half in range(2):

                @pl.when(step // 4 == half)
                def _():
                    a_ref, b_ref = outs[2 + 2 * half : 4 + 2 * half]
                    a_ref[0] = up_low[:, :A_ROWS]
                    b_ref[:, 0, 0 : block // 4 - A_ROWS] = up_low[:, A_ROWS:]
                    b_ref[:, 0, block // 4 - A_ROWS :] = down_low
        else:
            outs[2][0] = grad_up.astype(bf16)
            outs[3][0] = grad_down.astype(bf16)

    @pl.when(step >= n_blocks)
    def _():
        b = step - n_blocks
        hidden = n_blocks * block
        down = down_scr[...].reshape(hidden, model)
        out_ref[0] = (x1_ref[0] + nn(act_scr[b], down)).astype(bf16)
        up = up_scr[...].reshape(hidden, model)
        gh2_ref[0] = nn(pre_scr[b], up)


def ffn_call(h2, gf, x1, weights, copies, groups, scratch_dims, split_out):
    batch, rows, model = h2.shape
    hidden = math.prod(scratch_dims)
    block = min(256, hidden)
    n_blocks = hidden // block
    late = lambda j: (jnp.clip(j - n_blocks, 0, batch - 1), 0, 0)
    out_specs = [pl.BlockSpec((1, rows, model), late), pl.BlockSpec((1, rows, model), late)]
    out_shapes = [
        jax.ShapeDtypeStruct((batch, rows, model), bf16),
        jax.ShapeDtypeStruct((batch, rows, model), f32),
    ]
    if split_out:
        unit = scratch_dims[-1]
        b_rows = 2 * unit - A_ROWS
        for half in range(2):
            out_specs.append(
                pl.BlockSpec((1, 4, A_ROWS, model), lambda j, h=half: (jnp.clip(j - 4 * h, 0, 3), 0, 0, 0))
            )
            out_shapes.append(jax.ShapeDtypeStruct((4, 4, A_ROWS, model), bf16))
            out_specs.append(
                pl.BlockSpec((4, 1, b_rows, model), lambda j, h=half: (0, jnp.clip(j - 4 * h, 0, 3), 0, 0))
            )
            out_shapes.append(jax.ShapeDtypeStruct((4, 4, b_rows, model), bf16))
    else:
        for _ in range(2):
            out_specs.append(pl.BlockSpec((1, block, model), lambda j: (jnp.minimum(j, n_blocks - 1), 0, 0)))
            out_shapes.append(jax.ShapeDtypeStruct((n_blocks, block, model), bf16))
    return pl.pallas_call(
        functools.partial(ffn_kernel, len(weights), copies, groups, batch, split_out),
        grid=(n_blocks + batch,),
        in_specs=[
            const_block(h2.shape),
            const_block(gf.shape),
            pl.BlockSpec((1, rows, model), late),
        ]
        + [pl.BlockSpec(memory_space=pl.ANY)] * len(weights),
        out_specs=out_specs,
        out_shape=out_shapes,
        scratch_shapes=[
            pltpu.VMEM(scratch_dims + (model,), bf16),
            pltpu.VMEM(scratch_dims + (model,), bf16),
            pltpu.VMEM((batch, rows, hidden), bf16),
            pltpu.VMEM((batch, rows, hidden), bf16),
            pltpu.SemaphoreType.DMA((len(copies),)),
        ],
        compiler_params=params(),
        cost_estimate=cost(12 * batch * rows * hidden * model, 18 * MIB, 2 * batch * rows * hidden),
    )(h2, gf, x1, *weights)


def query_back_kernel(hd, n_states, tile, *refs):
    (
        gh2_ref,
        x1_ref,
        cot_ref,
        mixed_ref,
        rden_ref,
        wout_ref,
        gains_ref,
        phiq_ref,
        phik_ref,
        q_ref,
        v_ref,
        wf_ref,
    ) = refs[:12]
    state_refs = refs[12 : 12 + n_states]
    g1_ref, ga_ref, gcol_ref, gn_ref, gs_ref, gq_ref, gstate_ref, side_scr = refs[12 + n_states :]
    pair = pl.program_id(0)
    width = 2 * hd
    rows = x1_ref.shape[1]
    model = x1_ref.shape[2]
    pairs = model // width
    feats = phiq_ref.shape[-1] // 2
    s = hd ** (-0.25)
    low = lanes_of((rows, width)) < hd
    inner = lax.rem(lanes_of((rows, width)), hd)

    @pl.when(pair == 0)
    def _():
        xhat, scale = normed(x1_ref[0])
        grad = gh2_ref[0]
        g1 = cot_ref[0].astype(f32) + norm_back(grad, xhat, scale, gains_ref[1:2, :])
        g1_ref[0] = g1
        gcol_ref[0] = tn((grad * xhat).astype(bf16), jnp.ones((rows, 128), bf16))
        ga = g1.astype(bf16)
        ga_ref[0] = ga
        gn_full = nt(ga, wout_ref[...]) * rden_ref[0]
        gn_low = gn_full.astype(bf16)
        gn_ref[0] = gn_low
        product = gn_full * mixed_ref[0].astype(f32)
        high = product.astype(bf16)
        rest = (product - high.astype(f32)).astype(bf16)
        same = lax.div(lax.rem(lax.broadcasted_iota(jnp.int32, (2 * width, width), 0), width), hd) == lax.div(
            lax.broadcasted_iota(jnp.int32, (2 * width, width), 1), hd
        )
        minus = jnp.where(same, -1.0, 0.0).astype(bf16)
        for at in range(pairs):
            cols = slice(at * width, (at + 1) * width)
            gd = nn(jnp.concatenate([high[:, cols], rest[:, cols]], axis=1), minus)
            gd_high = gd.astype(bf16).astype(f32)
            gdx = jnp.where(inner == 0, gd_high, jnp.where(inner == 1, gd - gd_high, 0.0))
            side_scr[at] = jnp.concatenate([gn_low[:, cols], gdx.astype(bf16)], axis=1)

    side = side_scr[pair]
    even_state, odd_state = state_block(state_refs_of(state_refs, pairs), place_of(False), pair, hd)
    states = [even_state, odd_state]
    values = v_ref[0].astype(f32)
    ones = jnp.where(inner < 2, 1.0, 0.0)
    sides = [
        jnp.concatenate([jnp.where(low, values, 0.0), jnp.where(low, ones, 0.0)], axis=1).astype(bf16),
        jnp.concatenate([jnp.where(low, 0.0, values), jnp.where(low, 0.0, ones)], axis=1).astype(bf16),
    ]
    causal = causal_tile(tile)
    low_tile = low[0:tile]
    for at in range(rows // tile):
        here = slice(at * tile, (at + 1) * tile)
        end = (at + 1) * tile
        back = []
        for odd in range(2):
            cols = slice(odd * feats, (odd + 1) * feats)
            made = nt(side[here], sides[odd][0:end])
            last = jnp.where(causal, made[:, at * tile : end], 0.0)
            made = last if at == 0 else jnp.concatenate([made[:, : at * tile], last], axis=1)
            made = made.astype(bf16)
            gs_ref[0, odd, here, 0:end] = made
            grad_phi = nn(side[here], states[odd]) + nn(made, phik_ref[0, 0:end, cols])
            grad_proj = (grad_phi * phiq_ref[0, here, cols].astype(f32)).astype(bf16)
            back.append(nn(grad_proj, wf_ref[odd]))
        along = jnp.where(low_tile, back[0][:, :width], back[1][:, :width])
        total = jnp.where(low_tile, back[0][:, width:], back[1][:, width:])
        gq_ref[0, here, :] = (s * along + (s * s) * q_ref[0, here, :].astype(f32) * total).astype(bf16)
    even = tn(side, phiq_ref[0, :, :feats])
    odd = tn(side, phiq_ref[0, :, feats:])
    gstate_ref[0, 0:hd] = even[0:hd].astype(bf16)
    gstate_ref[0, hd:width] = odd[hd:width].astype(bf16)
    norms = jnp.concatenate(
        [
            even[width : width + 1] + even[width + 1 : width + 2],
            odd[width + hd : width + hd + 1] + odd[width + hd + 1 : width + hd + 2],
            jnp.zeros((14, feats), f32),
        ],
        axis=0,
    )
    gstate_ref[0, width : width + 16] = norms.astype(bf16)


def query_back_call(index, gh2, x1, cot, mixed, rden, w_out, gains, phi_q, phi_k, qkv, wf, states, before, hd):
    batch, rows, model = x1.shape
    width = 2 * hd
    pairs = model // width
    heads = 2 * pairs
    feats = phi_q.shape[-1] // heads
    tile = min(256, rows)
    whole = pl.BlockSpec((1, rows, model), lambda p: (index, 0, 0))
    phi_spec = pl.BlockSpec((1, rows, 2 * feats), lambda p: (index, 0, p))
    n_rows = width + 16
    return stacked_call(
        functools.partial(query_back_kernel, hd, len(states), tile),
        (pairs,),
        [
            whole,
            whole,
            whole,
            whole,
            whole,
            const_block(w_out.shape),
            const_block(gains.shape),
            phi_spec,
            phi_spec,
            pl.BlockSpec((1, rows, width), lambda p: (index, 0, p)),
            pl.BlockSpec((1, rows, width), lambda p: (index, 0, 2 * pairs + p)),
            pl.BlockSpec((2, feats, 4 * hd), lambda p: (p, 0, 0)),
        ]
        + state_specs(states, pairs),
        [
            whole,
            whole,
            pl.BlockSpec((1, model, 128), lambda p: (index, 0, 0)),
            whole,
            pl.BlockSpec((1, 2, rows, rows), lambda p: (index, p, 0, 0)),
            pl.BlockSpec((1, rows, width), lambda p: (index, 0, p)),
            pl.BlockSpec((1, n_rows, feats), lambda p: (p, 0, 0)),
        ],
        [
            jax.ShapeDtypeStruct((batch, rows, model), f32),
            jax.ShapeDtypeStruct((batch, rows, model), bf16),
            jax.ShapeDtypeStruct((batch, model, 128), f32),
            jax.ShapeDtypeStruct((batch, rows, model), bf16),
            jax.ShapeDtypeStruct((batch, heads, rows, rows), bf16),
            jax.ShapeDtypeStruct((batch, rows, model), bf16),
            jax.ShapeDtypeStruct((pairs, n_rows, feats), bf16),
        ],
        (True,) * 6 + (False,),
        before,
        (gh2, x1, cot, mixed, rden, w_out, gains, phi_q, phi_k, qkv, qkv, wf) + tuple(states),
        [pltpu.VMEM((pairs, rows, 2 * width), bf16)],
        cost(heads * 2 * rows * (rows * 512 + 4 * 65536), 18 * MIB),
    )


def key_back_kernel(hd, n_states, tile, *refs):
    gs_ref, scores_ref, phiq_ref, phik_ref, gn_ref, k_ref, v_ref, wf_ref = refs[:8]
    state_refs = refs[8 : 8 + n_states]
    gk_ref, gv_ref = refs[8 + n_states :]
    pair = pl.program_id(0)
    width = 2 * hd
    rows = k_ref.shape[1]
    feats = phiq_ref.shape[-1] // 2
    tiles = rows // tile
    s = hd ** (-0.25)
    states = state_block(state_refs_of(state_refs, pl.num_programs(0)), place_of(True), pair, hd)
    both = jnp.concatenate([states[0][0:width], states[1][0:width]], axis=1)
    low = lanes_of((tile, width)) < hd
    inner = lax.rem(lanes_of((tile, width)), hd)
    one = jnp.where(inner == 0, 1.0, 0.0).astype(bf16)
    gn_pair = gn_ref[0].astype(f32)
    low_all = lanes_of((rows, width)) < hd
    gn_sides = [
        jnp.where(low_all, gn_pair, 0.0).astype(bf16),
        jnp.where(low_all, 0.0, gn_pair).astype(bf16),
    ]
    for at in range(tiles):
        here = slice(at * tile, (at + 1) * tile)
        start = at * tile
        side = jnp.concatenate([v_ref[0, here, :], one], axis=1)
        grad_v = nt(phik_ref[0, here, :], both)
        back = []
        for odd in range(2):
            cols = slice(odd * feats, (odd + 1) * feats)
            grad_phi = nn(side, states[odd]) + tn(gs_ref[0, odd, start:, here], phiq_ref[0, start:, cols])
            grad_proj = (grad_phi * phik_ref[0, here, cols].astype(f32)).astype(bf16)
            back.append(nn(grad_proj, wf_ref[odd]))
            grad_v = grad_v + tn(scores_ref[0, odd, start:, here], gn_sides[odd][start:])
        along = jnp.where(low, back[0][:, :width], back[1][:, :width])
        total = jnp.where(low, back[0][:, width:], back[1][:, width:])
        gk_ref[0, here, :] = (s * along + (s * s) * k_ref[0, here, :].astype(f32) * total).astype(bf16)
        gv_ref[0, here, :] = grad_v.astype(bf16)


def key_back_call(index, gs, scores, phi_q, phi_k, gn, qkv, wf, states, before, hd):
    batch, rows, model = gn.shape
    width = 2 * hd
    pairs = model // width
    heads = 2 * pairs
    feats = phi_q.shape[-1] // heads
    tile = min(256, rows)
    square = pl.BlockSpec((1, 2, rows, rows), lambda p: (index, p, 0, 0))
    phi_spec = pl.BlockSpec((1, rows, 2 * feats), lambda p: (index, 0, p))
    narrow = pl.BlockSpec((1, rows, width), lambda p: (index, 0, p))
    return stacked_call(
        functools.partial(key_back_kernel, hd, len(states), tile),
        (pairs,),
        [
            square,
            square,
            phi_spec,
            phi_spec,
            narrow,
            pl.BlockSpec((1, rows, width), lambda p: (index, 0, pairs + p)),
            pl.BlockSpec((1, rows, width), lambda p: (index, 0, 2 * pairs + p)),
            pl.BlockSpec((2, feats, 4 * hd), lambda p: (p, 0, 0)),
        ]
        + state_specs(states, pairs),
        [narrow, narrow],
        [jax.ShapeDtypeStruct((batch, rows, model), bf16)] * 2,
        (True, True),
        before,
        (gs, scores, phi_q, phi_k, gn, qkv, qkv, wf) + tuple(states),
        [],
        cost(heads * 2 * rows * (rows * 512 + 4 * 65536), 14 * MIB),
    )


def inputs_back_kernel(gq_ref, gk_ref, gv_ref, w_ref, x_ref, g1_ref, gains_ref, out_ref):
    model = gq_ref.shape[2]
    grad = nt(gq_ref[0], w_ref[:, :model])
    grad = grad + nt(gk_ref[0], w_ref[:, model : 2 * model])
    grad = grad + nt(gv_ref[0], w_ref[:, 2 * model :])
    xhat, scale = normed(x_ref[0].astype(f32))
    out_ref[0] = g1_ref[0] + norm_back(grad, xhat, scale, gains_ref[0:1, :])


def inputs_back_call(gq, gk, gv, w_qkv, inputs, g1, gains):
    batch, rows, model = gq.shape
    whole = pl.BlockSpec((1, rows, model), lambda b: (b, 0, 0))
    return pl.pallas_call(
        inputs_back_kernel,
        grid=(batch,),
        in_specs=[whole, whole, whole, const_block(w_qkv.shape), whole, whole, const_block(gains.shape)],
        out_specs=whole,
        out_shape=jax.ShapeDtypeStruct((batch, rows, model), f32),
        compiler_params=params(),
        cost_estimate=cost(6 * batch * rows * model * model, 14 * MIB),
    )(gq, gk, gv, w_qkv, inputs, g1, gains)


def position():
    dp = lax.axis_index("dp")
    seq = lax.axis_index("seq")
    z, y = dp // 2, lax.rem(dp, 2)
    x, core = seq // 2, lax.rem(seq, 2)
    return core * 16 + z * 4 + y * 2 + x


def weight_kernel(n_products, has_column, pieces, *refs):
    n_in = 2 * n_products + has_column
    ins = refs[:n_in]
    outs = refs[n_in:-1]
    acc = refs[-1]
    step = pl.program_id(0)
    model = acc.shape[0]
    parts = [tn(ins[2 * at][0], ins[2 * at + 1][0]) for at in range(n_products)]
    if has_column:
        parts.append(ins[-1][0])

    @pl.when(step == 0)
    def _():
        for at, part in enumerate(parts):
            acc[:, at * model : at * model + part.shape[1]] = part

    @pl.when(step > 0)
    def _():
        for at, part in enumerate(parts):
            acc[:, at * model : at * model + part.shape[1]] += part

    @pl.when(step == pl.num_programs(0) - 1)
    def _():
        if not pieces:
            outs[0][...] = acc[...]
            return
        rows = model // 32
        cut = 3 * 128
        here = position()
        for half in range(2):
            a_ref, b_ref = outs[2 * half : 2 * half + 2]
            for z in range(4):
                for plane in range(4):
                    owner = here ^ (half * 16 + z * 4 + plane)
                    taken = acc[pl.ds(pl.multiple_of(owner * rows, rows), rows), :].astype(bf16)
                    a_ref[z, plane] = taken[:, :cut]
                    b_ref[plane, z] = taken[:, cut:]


def weight_call(products, column, pieces):
    batch, rows, model = products[0][0].shape
    whole = pl.BlockSpec((1, rows, model), lambda b: (b, 0, 0))
    args = [a for pair in products for a in pair]
    in_specs = [whole] * len(args)
    total = model * len(products)
    if column is not None:
        args.append(column)
        in_specs.append(pl.BlockSpec((1,) + column.shape[1:], lambda b: (b, 0, 0)))
        total += column.shape[2]
    if pieces:
        shapes = [(4, 4, model // 32, 384), (4, 4, model // 32, total - 384)] * 2
        kind = bf16
    else:
        shapes = [(model, total)]
        kind = f32
    return pl.pallas_call(
        functools.partial(weight_kernel, len(products), int(column is not None), pieces),
        grid=(batch,),
        in_specs=in_specs,
        out_specs=[const_block(shape) for shape in shapes],
        out_shape=[jax.ShapeDtypeStruct(shape, kind) for shape in shapes],
        scratch_shapes=[pltpu.VMEM((model, total), f32)],
        compiler_params=params(),
        cost_estimate=cost(2 * batch * rows * model * total, 10 * MIB),
    )(*args)


def swap(array, core=0, z=0, plane=0):
    mask = z * 8 + (plane // 2) * 4 + (plane % 2) * 2 + core
    return lax.ppermute(array, AXES, [(i, i ^ mask) for i in range(32)])


def gather_pieces(a_own, b_own):
    a_plane = jnp.stack([a_own] + [swap(a_own, plane=p) for p in (1, 2, 3)])
    b_line = jnp.stack([b_own] + [swap(b_own, z=z) for z in (1, 2, 3)])
    a_all = [a_plane] + [swap(a_plane, z=z) for z in (1, 2, 3)]
    b_all = [b_line] + [swap(b_line, plane=p) for p in (1, 2, 3)]
    return a_all, b_all


def summed(*arrays):
    return functools.reduce(lambda a, b: a + b, [a.astype(f32) for a in arrays])


def scatter_pieces(a_near, b_near, a_far, b_far):
    a_got, b_got = swap(a_far, core=1), swap(b_far, core=1)
    a_sum = [summed(a_near[z], a_got[z]).astype(bf16) for z in range(4)]
    b_sum = [summed(b_near[p], b_got[p]).astype(bf16) for p in range(4)]
    a_line = summed(a_sum[0], *[swap(a_sum[z], z=z) for z in (1, 2, 3)]).astype(bf16)
    b_plane = summed(b_sum[0], *[swap(b_sum[p], plane=p) for p in (1, 2, 3)]).astype(bf16)
    a_own = summed(a_line[0], *[swap(a_line[p], plane=p) for p in (1, 2, 3)])
    b_own = summed(b_plane[0], *[swap(b_plane[z], z=z) for z in (1, 2, 3)])
    return a_own, b_own


def share_pieces(a_own, b_own):
    a_all, b_all = gather_pieces(a_own, b_own)
    a_near = jnp.stack(a_all)
    b_near = jnp.stack(b_all, axis=1)
    near = jnp.concatenate([a_near, b_near], axis=-1)
    return jnp.stack([near, swap(near, core=1)])


def assemble_kernel(early_ref, late_ref, wqkv_ref, gains_ref, gw_ref, gwout_ref, ggain_ref, col_scr):
    rows = early_ref.shape[3]
    model = gwout_ref.shape[0]
    here = position()
    for core in range(2):
        for z in range(4):
            for plane in range(4):
                owner = here ^ (core * 16 + z * 4 + plane)
                at = pl.ds(pl.multiple_of(owner * rows, rows), rows)
                early = early_ref[core, z, plane].astype(f32)
                late = late_ref[core, z, plane].astype(f32)
                gwout_ref[at, :] = early[:, :model]
                gw_ref[at, 0:model] = early[:, model : 2 * model]
                col_scr[at, :] = early[:, 2 * model :]
                gw_ref[at, model:] = late
    gain_rows(gw_ref, col_scr, wqkv_ref, gains_ref, ggain_ref)


def gain_rows(gw_ref, col_ref, wqkv_ref, gains_ref, ggain_ref):
    along = jnp.sum(gw_ref[...] * wqkv_ref[...].astype(f32), axis=1, keepdims=True)
    wide = jnp.broadcast_to(along, col_ref.shape)
    ggain_ref[0:1, :] = wide.T[0:1, :] / gains_ref[0:1, :]
    ggain_ref[1:2, :] = col_ref[...].T[0:1, :]


def assemble_call(early, late, w_qkv, gains):
    model = w_qkv.shape[0]
    return pl.pallas_call(
        assemble_kernel,
        out_shape=[
            jax.ShapeDtypeStruct(w_qkv.shape, f32),
            jax.ShapeDtypeStruct((model, model), f32),
            jax.ShapeDtypeStruct(gains.shape, f32),
        ],
        scratch_shapes=[pltpu.VMEM((model, 128), f32)],
        compiler_params=params(),
    )(early, late, w_qkv, gains)


def gains_kernel(gw_ref, col_ref, wqkv_ref, gains_ref, ggain_ref):
    gain_rows(gw_ref, col_ref, wqkv_ref, gains_ref, ggain_ref)


def exchange_states(local, backward, fast):
    if not fast:
        everything = lax.all_gather(local, "seq").astype(f32)
        count, place = lax.axis_size("seq"), lax.axis_index("seq")
        at = jnp.arange(count)
        wanted = (at > place) if backward else (at < place)
        total = jnp.sum(jnp.where(wanted[:, None, None, None], everything, 0.0), axis=0)
        return (total.astype(bf16),)
    near = swap(local, core=1)
    half = local.shape[0] // 2
    core = lax.rem(lax.axis_index("seq"), 2)
    total = (local.astype(f32) + near.astype(f32)).astype(bf16)
    mine = jnp.where(core == 0, total[:half], total[half:])
    from_x = 1 if backward else 0
    pairs = [(i, i ^ 2) for i in range(32) if (i >> 1) & 1 == from_x]
    got = lax.ppermute(mine, AXES, pairs)
    other = swap(got, core=1)
    return near, got, other


def ffn_weights_fast(ffn_weight):
    shard = ffn_weight[0]
    unit = shard.shape[1]
    flat = shard.reshape(2 * unit, shard.shape[2])
    a_near, b_near = gather_pieces(flat[:A_ROWS], flat[A_ROWS:])
    a_far = [swap(a, core=1) for a in a_near]
    b_far = [swap(b, core=1) for b in b_near]
    weights = a_far + b_far + a_near + b_near
    copies = []
    tail = unit - A_ROWS
    for group in range(2):
        base = 8 * group
        for z in range(4):
            copies.append(
                (
                    lambda w, i=base + z: w[i],
                    lambda up, down, g=group, z=z: up.at[g, z, :, 0:A_ROWS],
                    group,
                )
            )
        for p in range(4):
            copies.append(
                (
                    lambda w, i=base + 4 + p: w[i].at[:, 0:tail],
                    lambda up, down, g=group, p=p: up.at[g, :, p, A_ROWS:unit],
                    group,
                )
            )
            copies.append(
                (
                    lambda w, i=base + 4 + p: w[i].at[:, tail:],
                    lambda up, down, g=group, p=p: down.at[g, :, p],
                    group,
                )
            )
    return weights, copies, 2, (2, 4, 4, unit)


def ffn_weights_plain(ffn_weight):
    pair = lax.all_gather(ffn_weight[0], AXES, axis=1, tiled=True)
    hidden, model = pair.shape[1:]
    block = min(256, hidden)
    blocks = pair.reshape(2, hidden // block, block, model)
    copies = [
        (lambda w: w[0].at[0], lambda up, down: up, 0),
        (lambda w: w[0].at[1], lambda up, down: down, 0),
    ]
    return [blocks], copies, 1, (hidden // block, block)


def on_device(inputs, gains, w_qkv, w_out, ffn_weight, omega, cotangent):
    batch, rows, model = inputs.shape
    hd = omega.shape[-1]
    fast = lax.axis_size("dp") == 8 and lax.axis_size("seq") == 4 and ffn_weight.shape[2] == 64
    gain_pair, wqkv, wout = gains[0], w_qkv[0], w_out[0]
    wf = feature_weights(omega[0])
    if fast:
        weights, copies, groups, dims = ffn_weights_fast(ffn_weight)
    else:
        weights, copies, groups, dims = ffn_weights_plain(ffn_weight)

    before = None
    carried = []
    for b in range(batch):
        before = features_call(b, inputs, gain_pair, wqkv, wf, before, hd)
        carried.append(exchange_states(before[4], False, fast))
    qkv, phi_q, phi_k, h1 = before[:4]
    before = None
    for b in range(batch):
        before = mix_call(b, inputs, gain_pair, wout, phi_q, phi_k, qkv, carried[b], before, hd)
    scores, mixed, rden, x1, h2 = before
    result = ffn_call(h2, cotangent, x1, weights, copies, groups, dims, fast)
    outputs, gh2 = result[:2]
    if fast:
        a_far, b_far, a_near, b_near = result[2:]
        a_own, b_own = scatter_pieces(a_near, b_near, a_far, b_far)
        unit = ffn_weight.shape[2]
        grad_ffn = jnp.concatenate([a_own, b_own], axis=0).reshape(1, 2, unit, model)
    else:
        both = jnp.stack([g.reshape(-1, model) for g in result[2:]])
        grad_ffn = lax.psum_scatter(both, AXES, scatter_dimension=1, tiled=True).astype(f32)[None]

    before = None
    later = []
    for b in range(batch):
        before = query_back_call(
            b, gh2, x1, cotangent, mixed, rden, wout, gain_pair, phi_q, phi_k, qkv, wf, carried[b], before, hd
        )
        later.append(exchange_states(before[6], True, fast))
    g1, ga, gcol, gn, gs, gq = before[:6]
    early = weight_call([(mixed, ga), (h1, gq)], gcol, fast)
    before = None
    for b in range(batch):
        before = key_back_call(b, gs, scores, phi_q, phi_k, gn, qkv, wf, later[b], before, hd)
    gk, gv = before
    late = weight_call([(h1, gk), (h1, gv)], None, fast)
    grad_inputs = inputs_back_call(gq, gk, gv, wqkv, inputs, g1, gain_pair)
    if fast:
        early_own = scatter_pieces(*early[:2], *early[2:])
        late_own = scatter_pieces(*late[:2], *late[2:])
        early_all = share_pieces(*[a.astype(bf16) for a in early_own])
        late_all = share_pieces(*[a.astype(bf16) for a in late_own])
        grad_wqkv, grad_wout, grad_gains = assemble_call(early_all, late_all, wqkv, gain_pair)
    else:
        early_sum, late_sum = lax.psum((early[0], late[0]), AXES)
        grad_wout = early_sum[:, :model]
        grad_wqkv = jnp.concatenate([early_sum[:, model : 2 * model], late_sum], axis=1)
        grad_gains = pl.pallas_call(
            gains_kernel,
            out_shape=jax.ShapeDtypeStruct(gain_pair.shape, f32),
            compiler_params=params(),
        )(grad_wqkv, early_sum[:, 2 * model :], wqkv, gain_pair)
    return (outputs, grad_inputs, grad_gains[None], grad_wqkv[None], grad_wout[None], grad_ffn)


def solution(mesh):
    in_specs = (
        P("dp", "seq", None),
        P(),
        P(),
        P(),
        P(None, None, ("dp", "seq"), None),
        P(),
        P("dp", "seq", None),
    )
    out_specs = (
        P("dp", "seq", None),
        P("dp", "seq", None),
        P(),
        P(),
        P(),
        P(None, None, ("dp", "seq"), None),
    )
    return jax.shard_map(
        on_device, mesh=mesh, in_specs=in_specs, out_specs=out_specs, check_vma=False
    )
```

```python
import functools
import math

import jax
import jax.numpy as jnp
from jax import lax
from jax.experimental import pallas as pl
from jax.experimental.pallas import tpu as pltpu
from jax.sharding import PartitionSpec as P

epsilon = 1e-05
bf16 = jnp.bfloat16
f32 = jnp.float32
AXES = ("dp", "seq")
MIB = 2**20


def nn(a, b):
    return lax.dot_general(a, b, (((1,), (0,)), ((), ())), preferred_element_type=f32)


def nt(a, b):
    return lax.dot_general(a, b, (((1,), (1,)), ((), ())), preferred_element_type=f32)


def tn(a, b):
    return lax.dot_general(a, b, (((0,), (0,)), ((), ())), preferred_element_type=f32)


def lanes_of(shape):
    return lax.broadcasted_iota(jnp.int32, shape, len(shape) - 1)


def params(mib=56):
    return pltpu.CompilerParams(vmem_limit_bytes=mib * MIB)


def cost(flops, nbytes, trans=0):
    return pl.CostEstimate(flops=int(flops), bytes_accessed=int(nbytes), transcendentals=int(trans))


def const_block(shape):
    return pl.BlockSpec(shape, lambda *_: (0,) * len(shape))


def stacked_call(kernel, grid, in_specs, out_specs, out_shapes, stacked, before, args, scratch, estimate, after=()):
    n_in = len(args)
    aliases = {}
    extra = list(after)
    if before is not None:
        for at, (flag, buffer) in enumerate(zip(stacked, before)):
            if flag:
                aliases[n_in + len(extra)] = at
                extra.append(buffer)
    n_extra = len(extra)

    def body(*refs):
        kernel(*refs[:n_in], *refs[n_in + n_extra :])

    return pl.pallas_call(
        body,
        grid=grid,
        in_specs=list(in_specs) + [pl.BlockSpec(memory_space=pl.ANY)] * n_extra,
        out_specs=out_specs,
        out_shape=out_shapes,
        scratch_shapes=scratch,
        input_output_aliases=aliases,
        compiler_params=params(),
        cost_estimate=estimate,
    )(*args, *extra)


def normed(values):
    center = values - jnp.mean(values, axis=-1, keepdims=True)
    spread = jnp.mean(center * center, axis=-1, keepdims=True)
    scale = lax.rsqrt(spread + epsilon)
    return center * scale, scale


def norm_back(grad, xhat, scale, gain):
    gy = grad * gain
    return scale * (
        gy - jnp.mean(gy, axis=-1, keepdims=True) - xhat * jnp.mean(gy * xhat, axis=-1, keepdims=True)
    )


def causal_tile(rows):
    return lax.broadcasted_iota(jnp.int32, (rows, rows), 0) >= lax.broadcasted_iota(
        jnp.int32, (rows, rows), 1
    )


def feature_weights(omega, odd):
    ones = jnp.full(omega.shape, -1.0, omega.dtype)
    zeros = jnp.zeros_like(ones)
    parts = [ones, omega, zeros, ones] if odd else [omega, ones, ones, zeros]
    return jnp.concatenate(parts, axis=1)


def features_kernel(hd, x_ref, gains_ref, w_ref, omega_ref, qkv_ref, phiq_ref, phik_ref, h1_ref, state_ref, qkv_scr):
    pair = pl.program_id(0)
    width = 2 * hd
    model = x_ref.shape[-1]
    s = hd ** (-0.25)
    feats = omega_ref.shape[1]

    @pl.when(pair == 0)
    def _():
        xhat, _ = normed(x_ref[0].astype(f32))
        hidden = (xhat * gains_ref[0:1, :]).astype(bf16)
        h1_ref[0] = hidden
        for part in range(3):
            cols = slice(part * model, (part + 1) * model)
            made = nn(hidden, w_ref[:, cols]).astype(bf16)
            qkv_ref[0, :, cols] = made
            qkv_scr[part] = made

    column = pl.ds(pl.multiple_of(pair * width, width), width)
    rows = x_ref.shape[1]
    low = lanes_of((rows, width)) < hd
    weights = [feature_weights(omega_ref[odd], odd) for odd in range(2)]

    def phi_pair(part, out_ref):
        points = qkv_scr[part, :, column].astype(f32)
        energy = points * points * (0.5 * s)
        high = energy.astype(bf16).astype(f32)
        rest = (energy - high).astype(bf16)
        turned = pltpu.roll(high, hd, 1)
        made = []
        for odd in range(2):
            first = jnp.where(low, turned, points) if odd else jnp.where(low, points, turned)
            left = jnp.concatenate([first.astype(bf16), rest], axis=1)
            proj = nt(left, weights[odd])
            phi = jnp.exp2(proj * (s * math.log2(math.e)) - 0.5 * math.log2(feats))
            phi_low = phi.astype(bf16)
            out_ref[0, :, odd * feats : (odd + 1) * feats] = phi_low
            made.append(phi_low)
        return made

    phi_pair(0, phiq_ref)
    even_k, odd_k = phi_pair(1, phik_ref)
    values = qkv_scr[2, :, column]
    state_ref[0, 0:hd, :] = tn(values, even_k)[0:hd].astype(bf16)
    state_ref[0, hd:width, :] = tn(values, odd_k)[hd:width].astype(bf16)
    sums = jnp.concatenate(
        [
            jnp.sum(even_k.astype(f32), axis=0, keepdims=True),
            jnp.sum(odd_k.astype(f32), axis=0, keepdims=True),
            jnp.zeros((14, feats), f32),
        ],
        axis=0,
    )
    state_ref[0, width : width + 16, :] = sums.astype(bf16)


def features_call(index, at, count, inputs, gains, w_qkv, omega, before, after=()):
    batch, rows, model = inputs.shape
    heads, feats, hd = omega.shape
    pairs = heads // 2
    width = 2 * hd
    n_rows = width + 16
    phi_spec = pl.BlockSpec((1, rows, 2 * feats), lambda p: (index, 0, p))
    return stacked_call(
        functools.partial(features_kernel, hd),
        (pairs,),
        [
            pl.BlockSpec((1, rows, model), lambda p: (index, 0, 0)),
            const_block(gains.shape),
            const_block(w_qkv.shape),
            pl.BlockSpec((2, feats, hd), lambda p: (p, 0, 0)),
        ],
        [
            pl.BlockSpec((1, rows, 3 * model), lambda p: (index, 0, 0)),
            phi_spec,
            phi_spec,
            pl.BlockSpec((1, rows, model), lambda p: (index, 0, 0)),
            pl.BlockSpec((1, n_rows, feats), lambda p: (at * pairs + p, 0, 0)),
        ],
        [
            jax.ShapeDtypeStruct((batch, rows, 3 * model), bf16),
            jax.ShapeDtypeStruct((batch, rows, heads * feats), bf16),
            jax.ShapeDtypeStruct((batch, rows, heads * feats), bf16),
            jax.ShapeDtypeStruct((batch, rows, model), bf16),
            jax.ShapeDtypeStruct((count * pairs, n_rows, feats), bf16),
        ],
        (True, True, True, True, at > 0),
        before,
        (inputs, gains, w_qkv, omega),
        [pltpu.VMEM((3, rows, model), bf16)],
        cost(2 * rows * model * 3 * model + 4 * heads * rows * 256 * feats, 9 * MIB, 2 * rows * heads * feats),
        after,
    )


def state_block(state_refs, backward, pair, hd, first, count):
    if len(state_refs) == 1:
        total = state_refs[0][0].astype(f32)
    else:
        near, got, other = state_refs
        core = lax.rem(lax.axis_index("seq"), 2)
        own_half = (first + pair) // (count // 2) == core
        own = jnp.where(own_half, 1.0, 0.0)
        beside = jnp.where(core == (0 if backward else 1), 1.0, 0.0)
        total = (
            got[0].astype(f32) * own + other[0].astype(f32) * (1.0 - own) + near[0].astype(f32) * beside
        )
    feats = total.shape[-1]
    width = 2 * hd
    zeros = jnp.zeros((hd, feats), bf16)
    low = total.astype(bf16)
    even_norm = jnp.broadcast_to(total[width : width + 1], (hd, feats)).astype(bf16)
    odd_norm = jnp.broadcast_to(total[width + 1 : width + 2], (hd, feats)).astype(bf16)
    even = jnp.concatenate([low[0:hd], zeros, even_norm, zeros], axis=0)
    odd = jnp.concatenate([zeros, low[hd:width], zeros, odd_norm], axis=0)
    return even, odd


def state_specs(carried, pairs):
    states, at, count = carried
    shape = (1,) + states[0].shape[1:]
    first = at * pairs
    specs = [pl.BlockSpec(shape, lambda g: (first + g, 0, 0))]
    if len(states) > 1:
        specs += [pl.BlockSpec(shape, lambda g: (lax.rem(first + g, count // 2), 0, 0))] * 2
    return specs


def mix_kernel(hd, n_states, first, count, tile, *refs):
    x_ref, gains_ref, wout_ref, phiq_ref, phik_ref, v_ref = refs[:6]
    state_refs = refs[6 : 6 + n_states]
    mixed_ref, rden_ref, x1_ref, h2_ref, mixed_scr = refs[6 + n_states :]
    step = pl.program_id(0)
    width = 2 * hd
    pairs = wout_ref.shape[0] // width
    pair = lax.rem(step, pairs)
    rows = x_ref.shape[1]
    feats = phiq_ref.shape[-1] // 2
    column = pl.ds(pl.multiple_of(pair * width, width), width)
    even_state, odd_state = state_block(state_refs, False, step, hd, first, count)
    both_state = jnp.concatenate([even_state, odd_state], axis=1)
    low = lanes_of((rows, width)) < hd
    values = v_ref[0].astype(f32)
    ones = jnp.where(low, 1.0, 0.0)
    sides = [
        jnp.concatenate([jnp.where(low, values, 0.0), ones], axis=1).astype(bf16),
        jnp.concatenate([jnp.where(low, 0.0, values), 1.0 - ones], axis=1).astype(bf16),
    ]
    causal = causal_tile(tile)
    for at in range(rows // tile):
        here = slice(at * tile, (at + 1) * tile)
        end = (at + 1) * tile
        total = nt(phiq_ref[0, here, :], both_state)
        for odd in range(2):
            cols = slice(odd * feats, (odd + 1) * feats)
            made = masked(nt(phiq_ref[0, here, cols], phik_ref[0, 0:end, cols]), causal, at, tile)
            total = total + nn(made, sides[odd][0:end])
        rden = 1.0 / total[:, width:]
        mixed = (total[:, :width] * rden).astype(bf16)
        rden_ref[0, here, :] = rden
        mixed_ref[0, here, :] = mixed
        mixed_scr[here, column] = mixed

    @pl.when(pair == pairs - 1)
    def _():
        x1 = x_ref[0].astype(f32) + nn(mixed_scr[...], wout_ref[...])
        x1_ref[0] = x1
        xhat, _ = normed(x1)
        h2_ref[0] = (xhat * gains_ref[1:2, :]).astype(bf16)


def masked(made, causal, at, tile):
    last = jnp.where(causal, made[:, at * tile :], 0.0)
    if at > 0:
        last = jnp.concatenate([made[:, : at * tile], last], axis=1)
    return last.astype(bf16)


def mix_call(index, members, inputs, gains, w_out, phi_q, phi_k, qkv, carried, before, hd, after=()):
    batch, rows, model = inputs.shape
    width = 2 * hd
    pairs = model // width
    states, at, count = carried
    heads = 2 * pairs
    feats = phi_q.shape[-1] // heads
    tile = min(256, rows)
    whole = pl.BlockSpec((1, rows, model), lambda g: (index + g // pairs, 0, 0))
    narrow = pl.BlockSpec((1, rows, width), lambda g: (index + g // pairs, 0, lax.rem(g, pairs)))
    phi_spec = pl.BlockSpec((1, rows, 2 * feats), lambda g: (index + g // pairs, 0, lax.rem(g, pairs)))
    return stacked_call(
        functools.partial(mix_kernel, hd, len(states), at * pairs, count, tile),
        (members * pairs,),
        [
            whole,
            const_block(gains.shape),
            const_block(w_out.shape),
            phi_spec,
            phi_spec,
            pl.BlockSpec((1, rows, width), lambda g: (index + g // pairs, 0, 2 * pairs + lax.rem(g, pairs))),
        ]
        + state_specs(carried, pairs),
        [narrow, narrow, whole, whole],
        [
            jax.ShapeDtypeStruct((batch, rows, model), bf16),
            jax.ShapeDtypeStruct((batch, rows, model), f32),
            jax.ShapeDtypeStruct((batch, rows, model), f32),
            jax.ShapeDtypeStruct((batch, rows, model), bf16),
        ],
        (True,) * 4,
        before,
        (inputs, gains, w_out, phi_q, phi_k, qkv) + tuple(states),
        [pltpu.VMEM((rows, model), bf16)],
        cost(members * (heads * 2 * rows * rows * 512 + 2 * rows * model * model), members * 9 * MIB),
        after,
    )


def ffn_kernel(groups, batch, hd, *refs):
    h2_ref, gf_ref, x1_ref, mixed_ref, rden_ref, phiq_ref, wout_ref, gains_ref = refs[:8]
    weights = refs[8 : 8 + groups]
    act_ref, pre_ref, g1_ref, ga_ref, gain_ref, side_ref, gstate_ref = refs[8 + groups : 15 + groups]
    up_scr, down_scr, pre_scr, sems = refs[15 + groups :]
    step = pl.program_id(0)
    n_blocks = pl.num_programs(0) - batch
    each = n_blocks // groups
    block = act_ref.shape[-1]
    rows = h2_ref.shape[1]
    model = h2_ref.shape[2]
    shards, unit = up_scr.shape[1:3]
    taken = block // unit
    started = []
    for group in range(groups):
        started.append(pltpu.make_async_copy(weights[group].at[:, 0], up_scr.at[group], sems.at[2 * group]))
        started.append(pltpu.make_async_copy(weights[group].at[:, 1], down_scr.at[group], sems.at[2 * group + 1]))

    @pl.when(step == 0)
    def _():
        for copy in started:
            copy.start()

    for group in range(groups):

        @pl.when(step == group * each)
        def _():
            started[2 * group].wait()
            started[2 * group + 1].wait()

    @pl.when(step < n_blocks)
    def _():
        here = pl.ds(pl.multiple_of(lax.rem(step, each) * taken, taken), taken)
        up = up_scr[step // each, here].reshape(block, model)
        down = down_scr[step // each, here].reshape(block, model)
        cols = pl.ds(pl.multiple_of(step * block, block), block)
        for b in range(batch):
            pre = nt(h2_ref[b], up)
            part = 0.5 * lax.erf(pre * math.sqrt(0.5)) + 0.5
            act_ref[b] = (pre * part).astype(bf16)
            slope = part + pre * (
                jnp.exp2(pre * pre * (-0.5 * math.log2(math.e))) * (1.0 / math.sqrt(2.0 * math.pi))
            )
            grad_pre = (nt(gf_ref[b], down) * slope).astype(bf16)
            pre_ref[b] = grad_pre
            pre_scr[b, :, cols] = grad_pre

    @pl.when(step >= n_blocks)
    def _():
        b = step - n_blocks
        grad = nn(pre_scr[b], up_scr[...].reshape(n_blocks * block, model))
        xhat, scale = normed(x1_ref[0])
        g1 = gf_ref[b].astype(f32) + norm_back(grad, xhat, scale, gains_ref[1:2, :])
        g1_ref[0] = g1
        gain = jnp.sum(grad * xhat, axis=0, keepdims=True)

        @pl.when(b == 0)
        def _():
            gain_ref[...] = jnp.zeros_like(gain_ref)

        gain_ref[0:1] += gain
        ga = g1.astype(bf16)
        ga_ref[0] = ga
        gn_full = nt(ga, wout_ref[...]) * rden_ref[0]
        gn_low = gn_full.astype(bf16)
        product = gn_full * mixed_ref[0].astype(f32)
        high = product.astype(bf16)
        rest = (product - high.astype(f32)).astype(bf16)
        width = 2 * hd
        same = lax.div(lax.rem(lax.broadcasted_iota(jnp.int32, (2 * width, width), 0), width), hd) == lax.div(
            lax.broadcasted_iota(jnp.int32, (2 * width, width), 1), hd
        )
        minus = jnp.where(same, -1.0, 0.0).astype(bf16)
        inner = lax.rem(lanes_of((rows, width)), hd)
        feats = phiq_ref.shape[-1] // (model // hd)
        for at in range(model // width):
            cols = slice(at * width, (at + 1) * width)
            gd = nn(jnp.concatenate([high[:, cols], rest[:, cols]], axis=1), minus)
            gd_high = gd.astype(bf16).astype(f32)
            gdx = jnp.where(inner == 0, gd_high, jnp.where(inner == 1, gd - gd_high, 0.0))
            side = jnp.concatenate([gn_low[:, cols], gdx.astype(bf16)], axis=1)
            side_ref[0, at] = side
            even = tn(side, phiq_ref[0, :, 2 * at * feats : (2 * at + 1) * feats])
            odd = tn(side, phiq_ref[0, :, (2 * at + 1) * feats : (2 * at + 2) * feats])
            gstate_ref[at, 0:hd] = even[0:hd].astype(bf16)
            gstate_ref[at, hd:width] = odd[hd:width].astype(bf16)
            norms = jnp.concatenate(
                [
                    even[width : width + 1] + even[width + 1 : width + 2],
                    odd[width + hd : width + hd + 1] + odd[width + hd + 1 : width + hd + 2],
                    jnp.zeros((14, feats), f32),
                ],
                axis=0,
            )
            gstate_ref[at, width : width + 16] = norms.astype(bf16)


def ffn_call(h2, gf, x1, mixed, rden, phi_q, w_out, gains, weights, hd):
    batch, rows, model = h2.shape
    groups = len(weights)
    shards, _, unit, _ = weights[0].shape
    hidden = groups * shards * unit
    block = min(512, shards * unit)
    n_blocks = hidden // block
    pairs = model // (2 * hd)
    feats = phi_q.shape[-1] // (2 * pairs)
    n_rows = 2 * hd + 16
    here = lambda j: jnp.clip(j - n_blocks, 0, batch - 1)
    late = pl.BlockSpec((1, rows, model), lambda j: (here(j), 0, 0))
    wide = pl.BlockSpec((batch, rows, block), lambda j: (0, 0, jnp.minimum(j, n_blocks - 1)))
    scratch = (groups, shards, unit, model)
    return pl.pallas_call(
        functools.partial(ffn_kernel, groups, batch, hd),
        grid=(n_blocks + batch,),
        in_specs=[
            const_block(h2.shape),
            const_block(gf.shape),
            late,
            late,
            late,
            pl.BlockSpec((1, rows, phi_q.shape[-1]), lambda j: (here(j), 0, 0)),
            const_block(w_out.shape),
            const_block(gains.shape),
        ]
        + [pl.BlockSpec(memory_space=pl.ANY)] * groups,
        out_specs=[
            wide,
            wide,
            late,
            late,
            const_block((16, model)),
            pl.BlockSpec((1, pairs, rows, 4 * hd), lambda j: (here(j), 0, 0, 0)),
            pl.BlockSpec((pairs, n_rows, feats), lambda j: (here(j), 0, 0)),
        ],
        out_shape=[
            jax.ShapeDtypeStruct((batch, rows, hidden), bf16),
            jax.ShapeDtypeStruct((batch, rows, hidden), bf16),
            jax.ShapeDtypeStruct((batch, rows, model), f32),
            jax.ShapeDtypeStruct((batch, rows, model), bf16),
            jax.ShapeDtypeStruct((16, model), f32),
            jax.ShapeDtypeStruct((batch, pairs, rows, 4 * hd), bf16),
            jax.ShapeDtypeStruct((batch * pairs, n_rows, feats), bf16),
        ],
        scratch_shapes=[
            pltpu.VMEM(scratch, bf16),
            pltpu.VMEM(scratch, bf16),
            pltpu.VMEM((batch, rows, hidden), bf16),
            pltpu.SemaphoreType.DMA((2 * groups,)),
        ],
        compiler_params=params(),
        cost_estimate=cost(6 * batch * rows * hidden * model, 30 * MIB, 2 * batch * rows * hidden),
    )(h2, gf, x1, mixed, rden, phi_q, w_out, gains, *weights)


def row_owner(far, first, second):
    seq = lax.axis_index("seq")
    y, x = lax.rem(lax.axis_index("dp"), 2), seq // 2
    core = lax.rem(seq, 2) ^ far
    turned = core == 1
    y = y ^ jnp.where(turned, second, first)
    x = x ^ jnp.where(turned, first, second)
    return core * 4 + y * 2 + x


EXTRA = 16


def ffn_weight_kernel(groups, fast, n_after, *refs):
    act_ref, pre_ref, gf_ref, h2_ref, gain_ref, mixed_any, ga_any = refs[:7]
    outs = refs[7 + n_after : 9 + n_after]
    mixed_scr, ga_scr, sum_scr, sems = refs[9 + n_after :]
    step = pl.program_id(0)
    n_blocks = pl.num_programs(0) - 1
    batch, rows, block = act_ref.shape
    model = gf_ref.shape[2]
    copies = [
        pltpu.make_async_copy(mixed_any, mixed_scr, sems.at[0]),
        pltpu.make_async_copy(ga_any, ga_scr, sems.at[1]),
    ]

    @pl.when(step == 0)
    def _():
        for copy in copies:
            copy.start()

    @pl.when(step < n_blocks)
    def _():
        down = tn(act_ref[...].reshape(batch * rows, block), gf_ref[...].reshape(batch * rows, model)).astype(bf16)
        up = tn(pre_ref[...].reshape(batch * rows, block), h2_ref[...].reshape(batch * rows, model)).astype(bf16)
        if not fast:
            outs[0][0, 0] = up
            outs[0][0, 1] = down
            return
        unit = block // 8
        held = outs[0].shape[0] // 2
        for group in range(groups):

            @pl.when(step == group)
            def _():
                out = outs[group // 2]
                first = (group % 2) * held
                for at in range(8):
                    row = first + 2 * at * unit
                    here = slice(at * unit, (at + 1) * unit)
                    out[row : row + unit] = up[here]
                    out[row + unit : row + 2 * unit] = down[here]

    @pl.when(step == n_blocks)
    def _():
        for copy in copies:
            copy.wait()
        total = tn(mixed_scr[...].reshape(batch * rows, model), ga_scr[...].reshape(batch * rows, model))
        if not fast:
            outs[1][...] = total
            return
        sum_scr[...] = total
        piece = model // 8
        held = outs[0].shape[0] // 2
        gain = gain_ref[...].astype(bf16)
        for far in range(2):
            for first in range(2):
                for second in range(2):
                    owner = row_owner(far, first, second)
                    taken = sum_scr[pl.ds(pl.multiple_of(owner * piece, piece), piece), :].astype(bf16)
                    out = outs[0 if far else 1]
                    row = (first + 1) * held - (2 - second) * (piece + EXTRA)
                    out[row : row + piece] = taken
                    out[row + piece : row + piece + EXTRA] = gain


def ffn_weight_call(act, pre, gf, h2, gain, mixed, ga, weights, fast, after=()):
    batch, rows, model = h2.shape
    groups = len(weights)
    shards, _, unit, _ = weights[0].shape
    hidden = act.shape[-1]
    block = min(512, shards * unit)
    n_blocks = hidden // block
    wide = pl.BlockSpec((batch, rows, block), lambda j: (0, 0, jnp.minimum(j, n_blocks - 1)))
    if fast:
        shape = (4 * shards * unit + 4 * (model // 8 + EXTRA), model)
        out_specs = [const_block(shape)] * 2
        out_shapes = [jax.ShapeDtypeStruct(shape, bf16)] * 2
    else:
        out_specs = [
            pl.BlockSpec((1, 2, block, model), lambda j: (jnp.minimum(j, n_blocks - 1), 0, 0, 0)),
            const_block((model, model)),
        ]
        out_shapes = [
            jax.ShapeDtypeStruct((n_blocks, 2, block, model), bf16),
            jax.ShapeDtypeStruct((model, model), f32),
        ]
    anywhere = pl.BlockSpec(memory_space=pl.ANY)
    return pl.pallas_call(
        functools.partial(ffn_weight_kernel, groups, fast, len(after)),
        grid=(n_blocks + 1,),
        in_specs=[wide, wide, const_block(gf.shape), const_block(h2.shape), const_block(gain.shape), anywhere, anywhere]
        + [anywhere] * len(after),
        out_specs=out_specs,
        out_shape=out_shapes,
        scratch_shapes=[
            pltpu.VMEM(mixed.shape, bf16),
            pltpu.VMEM(ga.shape, bf16),
            pltpu.VMEM((model, model), f32),
            pltpu.SemaphoreType.DMA((2,)),
        ],
        compiler_params=params(),
        cost_estimate=cost(4 * batch * rows * hidden * model, 22 * MIB),
    )(act, pre, gf, h2, gain, mixed, ga, *after)


def attention_back_kernel(hd, n_prev, n_later, spots, tile, *refs):
    side_ref, phiq_ref, phik_ref, q_ref, k_ref, v_ref, omega_ref = refs[:7]
    prev_refs = refs[7 : 7 + n_prev]
    later_refs = refs[7 + n_prev : 7 + n_prev + n_later]
    out_ref, scores_scr, back_scr = refs[7 + n_prev + n_later :]
    pair = pl.program_id(0)
    width = 2 * hd
    rows = q_ref.shape[1]
    feats = phiq_ref.shape[-1] // 2
    tiles = rows // tile
    s = hd ** (-0.25)
    low = lanes_of((rows, width)) < hd
    low_tile = low[0:tile]
    inner = lax.rem(lanes_of((rows, width)), hd)
    weights = [feature_weights(omega_ref[odd], odd) for odd in range(2)]
    prev = state_block(prev_refs, False, pair, hd, *spots[0])
    later = state_block(later_refs, True, pair, hd, *spots[1])
    both = jnp.concatenate([later[0][0:width], later[1][0:width]], axis=1)
    side = side_ref[0, 0]
    values = v_ref[0].astype(f32)
    ones = jnp.where(inner < 2, 1.0, 0.0)
    sides = [
        jnp.concatenate([jnp.where(low, values, 0.0), jnp.where(low, ones, 0.0)], axis=1).astype(bf16),
        jnp.concatenate([jnp.where(low, 0.0, values), jnp.where(low, 0.0, ones)], axis=1).astype(bf16),
    ]
    one = jnp.where(inner == 0, 1.0, 0.0).astype(bf16)
    gn_pair = side[:, :width].astype(f32)
    gn_sides = [jnp.where(low, gn_pair, 0.0).astype(bf16), jnp.where(low, 0.0, gn_pair).astype(bf16)]
    causal = causal_tile(tile)

    def to_points(back, point_ref, here):
        along = jnp.where(low_tile, back[0][:, :width], back[1][:, :width])
        total = jnp.where(low_tile, back[0][:, width:], back[1][:, width:])
        return (s * along + (s * s) * point_ref[0, here, :].astype(f32) * total).astype(bf16)

    for at in range(tiles):
        here = slice(at * tile, (at + 1) * tile)
        end = (at + 1) * tile
        back = []
        for odd in range(2):
            cols = slice(odd * feats, (odd + 1) * feats)
            scores_scr[odd, here, 0:end] = masked(
                nt(phiq_ref[0, here, cols], phik_ref[0, 0:end, cols]), causal, at, tile
            )
            made = masked(nt(side[here], sides[odd][0:end]), causal, at, tile)
            back_scr[odd, here, 0:end] = made
            grad_phi = nn(side[here], prev[odd]) + nn(made, phik_ref[0, 0:end, cols])
            grad_proj = (grad_phi * phiq_ref[0, here, cols].astype(f32)).astype(bf16)
            back.append(nn(grad_proj, weights[odd]))
        out_ref[0, 0, here, :] = to_points(back, q_ref, here)
    for at in range(tiles):
        here = slice(at * tile, (at + 1) * tile)
        start = at * tile
        beside = jnp.concatenate([v_ref[0, here, :], one[here]], axis=1)
        grad_v = nt(phik_ref[0, here, :], both)
        back = []
        for odd in range(2):
            cols = slice(odd * feats, (odd + 1) * feats)
            grad_phi = nn(beside, later[odd]) + tn(back_scr[odd, start:, here], phiq_ref[0, start:, cols])
            grad_proj = (grad_phi * phik_ref[0, here, cols].astype(f32)).astype(bf16)
            back.append(nn(grad_proj, weights[odd]))
            grad_v = grad_v + tn(scores_scr[odd, start:, here], gn_sides[odd][start:])
        out_ref[0, 1, here, :] = to_points(back, k_ref, here)
        out_ref[0, 2, here, :] = grad_v.astype(bf16)


def attention_back_call(index, side, phi_q, phi_k, qkv, omega, carried, later, before, after=()):
    batch, pairs, rows, wide = side.shape
    heads, feats, hd = omega.shape
    width = 2 * hd
    model = pairs * width
    tile = min(256, rows)
    phi_spec = pl.BlockSpec((1, rows, 2 * feats), lambda p: (index, 0, p))
    spots = tuple((at * pairs, count) for _, at, count in (carried, later))

    def part(n):
        return pl.BlockSpec((1, rows, width), lambda p: (index, 0, n * pairs + p))

    return stacked_call(
        functools.partial(attention_back_kernel, hd, len(carried[0]), len(later[0]), spots, tile),
        (pairs,),
        [
            pl.BlockSpec((1, 1, rows, wide), lambda p: (index, p, 0, 0)),
            phi_spec,
            phi_spec,
            part(0),
            part(1),
            part(2),
            pl.BlockSpec((2, feats, hd), lambda p: (p, 0, 0)),
        ]
        + state_specs(carried, pairs)
        + state_specs(later, pairs),
        [pl.BlockSpec((1, 3, rows, width), lambda p: (index, 0, 0, p))],
        [jax.ShapeDtypeStruct((batch, 3, rows, model), bf16)],
        (True,),
        before,
        (side, phi_q, phi_k, qkv, qkv, qkv, omega) + tuple(carried[0]) + tuple(later[0]),
        [pltpu.VMEM((2, rows, rows), bf16), pltpu.VMEM((2, rows, rows), bf16)],
        cost(heads * 2 * rows * (rows * 1024 + 6 * 65536), 12 * MIB),
        after,
    )


def qkv_weight_kernel(fast, n_after, *refs):
    h1_ref, grad_ref = refs[:2]
    outs = refs[2 + n_after :]
    batch, rows, model = h1_ref.shape
    total = tn(h1_ref[...].reshape(batch * rows, model), grad_ref[...].reshape(batch * rows, model))
    if not fast:
        outs[0][...] = total
        return
    far_ref, low_ref, high_ref, sum_scr = outs
    sum_scr[...] = total
    piece = model // 8
    for far in range(2):
        for first in range(2):
            for second in range(2):
                owner = row_owner(far, first, second)
                taken = sum_scr[pl.ds(pl.multiple_of(owner * piece, piece), piece), :].astype(bf16)
                if far:
                    far_ref[2 * first + second, 0] = taken
                else:
                    (high_ref if first else low_ref)[second, 0] = taken


def qkv_weight_call(h1, grads, fast, after=()):
    batch, rows, model = h1.shape
    if fast:
        sizes = (4, 2, 2)
        out_specs = [pl.BlockSpec((n, 1, model // 8, model), lambda p: (0, p, 0, 0)) for n in sizes]
        out_shapes = [jax.ShapeDtypeStruct((n, 3, model // 8, model), bf16) for n in sizes]
    else:
        out_specs = [pl.BlockSpec((model, model), lambda p: (0, p))]
        out_shapes = [jax.ShapeDtypeStruct((model, 3 * model), f32)]
    return pl.pallas_call(
        functools.partial(qkv_weight_kernel, fast, len(after)),
        grid=(3,),
        in_specs=[const_block(h1.shape), pl.BlockSpec((batch, 1, rows, model), lambda p: (0, p, 0, 0))]
        + [pl.BlockSpec(memory_space=pl.ANY)] * len(after),
        out_specs=out_specs,
        out_shape=out_shapes,
        scratch_shapes=[pltpu.VMEM((model, model), f32)] if fast else [],
        compiler_params=params(),
        cost_estimate=cost(6 * batch * rows * model * model, 8 * MIB),
    )(h1, grads, *after)


def finish_kernel(groups, *refs):
    grads_ref, w_ref, x_ref, g1_ref, gains_ref, act_ref, x1_ref = refs[:7]
    weights = refs[7 : 7 + groups]
    grad_ref, out_ref, token_ref, down_scr, sems = refs[7 + groups :]
    copies = [
        pltpu.make_async_copy(weights[group].at[:, 1], down_scr.at[group], sems.at[group]) for group in range(groups)
    ]
    for copy in copies:
        copy.start()
    model = x_ref.shape[2]
    grad = nt(grads_ref[0, 0], w_ref[:, :model])
    for part in (1, 2):
        grad = grad + nt(grads_ref[0, part], w_ref[:, part * model : (part + 1) * model])
    xhat, scale = normed(x_ref[0].astype(f32))
    grad_ref[0] = g1_ref[0] + norm_back(grad, xhat, scale, gains_ref[0:1, :])
    token_ref[...] = jnp.zeros_like(token_ref)
    for copy in copies:
        copy.wait()
    down = down_scr[...].reshape(act_ref.shape[2], model)
    out_ref[0] = (x1_ref[0] + nn(act_ref[0], down)).astype(bf16)


def finish_call(index, grads, w_qkv, inputs, g1, gains, act, x1, weights, before, after=()):
    batch, rows, model = inputs.shape
    hidden = act.shape[2]
    groups = len(weights)
    shards, _, unit, _ = weights[0].shape
    one = lambda j: (index, 0, 0)
    whole = pl.BlockSpec((1, rows, model), one)
    return stacked_call(
        functools.partial(finish_kernel, groups),
        (1,),
        [
            pl.BlockSpec((1, 3, rows, model), lambda j: (index, 0, 0, 0)),
            const_block(w_qkv.shape),
            whole,
            whole,
            const_block(gains.shape),
            pl.BlockSpec((1, rows, hidden), one),
            whole,
        ]
        + [pl.BlockSpec(memory_space=pl.ANY)] * groups,
        [whole, whole, const_block((8, 128))],
        [
            jax.ShapeDtypeStruct((batch, rows, model), f32),
            jax.ShapeDtypeStruct((batch, rows, model), bf16),
            jax.ShapeDtypeStruct((8, 128), f32),
        ],
        (True, True, False),
        before,
        (grads, w_qkv, inputs, g1, gains, act, x1) + tuple(weights),
        [pltpu.VMEM((groups, shards, unit, model), bf16), pltpu.SemaphoreType.DMA((groups,))],
        cost(2 * rows * model * (3 * model + hidden), 12 * MIB),
        after,
    )


CORE = (1, 1)
GATHER = ((16, 8), (8, 16), (2, 4), (4, 2))
PLANE = ((4, 2), (2, 4))
LINE = ((16, 8), (8, 16))


def swap(array, masks):
    return lax.ppermute(array, AXES, [(i, i ^ masks[i & 1]) for i in range(32)])


def summed(*arrays):
    return functools.reduce(lambda a, b: a + b, [a.astype(f32) for a in arrays])


def summed_low(*arrays):
    return summed(*arrays).astype(bf16)


def exchange_states(local, backward, fast):
    if not fast:
        everything = lax.all_gather(local, "seq").astype(f32)
        count, place = lax.axis_size("seq"), lax.axis_index("seq")
        at = jnp.arange(count)
        wanted = (at > place) if backward else (at < place)
        total = jnp.sum(jnp.where(wanted[:, None, None, None], everything, 0.0), axis=0)
        return (total.astype(bf16),)
    near = swap(local, CORE)
    core = lax.rem(lax.axis_index("seq"), 2)
    half = local.shape[0] // 2
    mine = jnp.where(core == 0, summed_low(local[:half], near[:half]), summed_low(local[half:], near[half:]))
    from_x = 1 if backward else 0
    pairs = [(i, i ^ 2) for i in range(32) if (i >> 1) & 1 == from_x]
    got = lax.ppermute(mine, AXES, pairs)
    other = swap(got, CORE)
    return near, got, other


def assemble_kernel(near_ref, ahead_ref, far_ref, wqkv_ref, gains_ref, gw_ref, gwout_ref, ggain_ref):
    model = gwout_ref.shape[0]
    rows = model // 8
    for far in range(2):
        for first in range(2):
            for second in range(2):
                owner = row_owner(far, first, second)
                at = pl.ds(pl.multiple_of(owner * rows, rows), rows)
                if far:
                    piece = far_ref[2 * first + second]
                else:
                    piece = (ahead_ref if first else near_ref)[second]
                for part in range(3):
                    gw_ref[at, part * model : (part + 1) * model] = piece[part * rows : (part + 1) * rows].astype(f32)
                gwout_ref[at, :] = piece[3 * rows : 4 * rows].astype(f32)

                @pl.when(owner == 0)
                def _():
                    ggain_ref[1:2, :] = piece[4 * rows : 4 * rows + EXTRA].astype(f32)[0:1]

    ggain_ref[0:1, :] = first_gain(gw_ref, wqkv_ref, gains_ref)


def first_gain(gw_ref, wqkv_ref, gains_ref):
    along = jnp.sum(gw_ref[...] * wqkv_ref[...].astype(f32), axis=1, keepdims=True)
    return jnp.broadcast_to(along, (along.shape[0], 128)).T[0:1, :] / gains_ref[0:1, :]


def assemble_call(near, ahead, far, w_qkv, gains):
    model = w_qkv.shape[0]
    return pl.pallas_call(
        assemble_kernel,
        out_shape=[
            jax.ShapeDtypeStruct(w_qkv.shape, f32),
            jax.ShapeDtypeStruct((model, model), f32),
            jax.ShapeDtypeStruct(gains.shape, f32),
        ],
        compiler_params=params(),
    )(near, ahead, far, w_qkv, gains)


def gains_kernel(gw_ref, gain_ref, wqkv_ref, gains_ref, ggain_ref):
    ggain_ref[0:1, :] = first_gain(gw_ref, wqkv_ref, gains_ref)
    ggain_ref[1:2, :] = gain_ref[0:1, :]


def halves(array):
    cut = array.shape[0] // 2
    return array[:cut], array[cut:]


def gather_shards(shard):
    held = shard[None]
    steps = []
    for masks in GATHER:
        got = swap(held, masks)
        steps.append(got)
        low, held = held, jnp.concatenate([held, got])
    return [swap(low, CORE), swap(got, CORE), low, got], steps


def scatter_sums(far, near, n_shard, n_piece):
    got = swap(far, CORE)
    steps = [got]
    (low, high), (got_low, got_high) = halves(near), halves(got)
    low, high = summed_low(low, got_low), summed_low(high, got_high)
    for at, masks in enumerate(reversed(GATHER)):
        got = swap(high, masks)
        steps.append(got)
        shards = (8 >> at) * n_shard
        shard, shard_got = low[:shards], got[:shards]
        piece, piece_got = low[shards:], got[shards:]
        if at == 3:
            return summed(shard, shard_got), summed_low(piece, piece_got), steps
        (shard_low, shard_high), (got_low, got_high) = halves(shard), halves(shard_got)
        if at == 0:
            (low_p, high_p), (low_g, high_g) = halves(piece), halves(piece_got)
        else:
            low_p, low_g = piece, piece_got
            high_p, high_g = piece, piece_got
        low = summed_low(jnp.concatenate([shard_low, low_p]), jnp.concatenate([got_low, low_g]))
        high = summed_low(jnp.concatenate([shard_high, high_p]), jnp.concatenate([got_high, high_g]))


def on_device(inputs, gains, w_qkv, w_out, ffn_weight, omega, cotangent):
    batch, rows, model = inputs.shape
    heads, feats, hd = omega.shape[1:]
    fast = lax.axis_size("dp") == 8 and lax.axis_size("seq") == 4 and batch == 3
    gain_pair, wqkv, wout, omegas = gains[0], w_qkv[0], w_out[0], omega[0]
    pairs = heads // 2
    unit = ffn_weight.shape[2]

    def only_fast(*arrays):
        return arrays if fast else ()

    if fast:
        weights, steps = gather_shards(ffn_weight[0])
        groups = [(0, 2), (2, 1)]
    else:
        pair = lax.all_gather(ffn_weight[0], AXES, axis=1, tiled=True)
        hidden = pair.shape[1]
        block = min(512, hidden)
        weights = [jnp.swapaxes(pair.reshape(2, hidden // block, block, model), 0, 1)]
        steps = [None] * 4
        groups = [(0, batch)]

    before = None
    carried = []
    for first, members in groups:
        for at in range(members):
            b = first + at
            waits = []
            if fast and b > 0:
                waits.append(steps[b - 1])
            if fast and b == 2:
                waits.append(carried[0][0][0])
            before = features_call(b, at, members, inputs, gain_pair, wqkv, omegas, before, tuple(waits))
        carried.append((exchange_states(before[4], False, fast), 0, members * pairs))
    qkv, phi_q, phi_k, h1 = before[:4]
    before = None
    for (first, members), sums in zip(groups, carried):
        waits = only_fast(steps[2], carried[-1][0][0]) if first == 0 else ()
        before = mix_call(
            first, members, inputs, gain_pair, wout, phi_q, phi_k, qkv, sums, before, hd, waits
        )
    mixed, rden, x1, h2 = before
    carried = [(sums, at, members * pairs) for (first, members), (sums, _, _) in zip(groups, carried) for at in range(members)]

    act, pre, g1, ga, gain, side, gstate = ffn_call(
        h2, cotangent, x1, mixed, rden, phi_q, wout, gain_pair, weights, hd
    )
    sums = exchange_states(gstate, True, fast)
    far, near = ffn_weight_call(act, pre, cotangent, h2, gain, mixed, ga, weights, fast, only_fast(sums[0]))
    if fast:
        shard, piece, steps = scatter_sums(far, near, 2 * unit, model // 8 + EXTRA)
        grad_ffn = shard.reshape(1, 2, unit, model)
    else:
        both = jnp.swapaxes(far, 0, 1).reshape(2, -1, model)
        grad_ffn = lax.psum_scatter(both, AXES, scatter_dimension=1, tiled=True).astype(f32)[None]

    before = None
    for b in range(batch):
        waits = only_fast(steps[b - 1]) if b > 0 else ()
        before = attention_back_call(
            b, side, phi_q, phi_k, qkv, omegas, carried[b], (sums, b, batch * pairs), before, waits
        )
    (grads,) = before
    late = qkv_weight_call(h1, grads, fast, only_fast(steps[2]))

    before = None
    tokens = []
    for b in range(batch):
        before = finish_call(b, grads, wqkv, inputs, g1, gain_pair, act, x1, weights, before)
        tokens.append(before[2][0, 0])
    grad_inputs, outputs = before[:2]
    if fast:
        far, low, high = [a.reshape(a.shape[0], -1, model) for a in late]
        got_low, got_high = halves(swap(far, CORE))
        high = summed_low(high, got_high)
        low = summed_low(low, got_low)
        got = swap(high, PLANE[0])
        high = summed(low[1], got[1])
        low = summed_low(low[0], got[0])
        low = summed_low(low, swap((high + tokens[0]).astype(bf16), PLANE[1]))
        for at, masks in enumerate(LINE):
            low = (summed(low, swap(low, masks)) + tokens[1 + at]).astype(bf16)
        low = jnp.concatenate([low, piece])
        near = jnp.stack([low, swap(low, PLANE[1])])
        ahead = swap(near, PLANE[0])
        far = swap(jnp.concatenate([near, ahead]), CORE)
        grad_wqkv, grad_wout, grad_gains = assemble_call(near, ahead, far, wqkv, gain_pair)
    else:
        grad_wqkv, grad_wout, gain = lax.psum((late[0], near, gain), AXES)
        grad_gains = pl.pallas_call(
            gains_kernel,
            out_shape=jax.ShapeDtypeStruct(gain_pair.shape, f32),
            compiler_params=params(),
        )(grad_wqkv, gain, wqkv, gain_pair)
    return (outputs, grad_inputs, grad_gains[None], grad_wqkv[None], grad_wout[None], grad_ffn)


def solution(mesh):
    in_specs = (
        P("dp", "seq", None),
        P(),
        P(),
        P(),
        P(None, None, ("dp", "seq"), None),
        P(),
        P("dp", "seq", None),
    )
    out_specs = (
        P("dp", "seq", None),
        P("dp", "seq", None),
        P(),
        P(),
        P(),
        P(None, None, ("dp", "seq"), None),
    )
    return jax.shard_map(
        on_device, mesh=mesh, in_specs=in_specs, out_specs=out_specs, check_vma=False
    )
```

```python
import functools
import math

import jax
import jax.numpy as jnp
from jax import lax
from jax.experimental import pallas as pl
from jax.experimental.pallas import tpu as pltpu
from jax.sharding import PartitionSpec as P

epsilon = 1e-05
bf16 = jnp.bfloat16
f32 = jnp.float32
AXES = ("dp", "seq")
MIB = 2**20


def nn(a, b):
    return lax.dot_general(a, b, (((1,), (0,)), ((), ())), preferred_element_type=f32)


def nt(a, b):
    return lax.dot_general(a, b, (((1,), (1,)), ((), ())), preferred_element_type=f32)


def tn(a, b):
    return lax.dot_general(a, b, (((0,), (0,)), ((), ())), preferred_element_type=f32)


def lanes_of(shape):
    return lax.broadcasted_iota(jnp.int32, shape, len(shape) - 1)


def params(mib=63):
    return pltpu.CompilerParams(vmem_limit_bytes=mib * MIB)


def cost(flops, nbytes, trans=0):
    return pl.CostEstimate(flops=int(flops), bytes_accessed=int(nbytes), transcendentals=int(trans))


def in_hbm(arrays):
    return [pltpu.with_memory_space_constraint(a, pltpu.HBM) for a in arrays]


def const_block(shape):
    return pl.BlockSpec(shape, lambda *_: (0,) * len(shape))


def stacked_call(kernel, grid, in_specs, out_specs, out_shapes, stacked, before, args, scratch, estimate, after=()):
    n_in = len(args)
    aliases = {}
    extra = list(after)
    if before is not None:
        for at, (flag, buffer) in enumerate(zip(stacked, before)):
            if flag:
                aliases[n_in + len(extra)] = at
                extra.append(buffer)
    n_extra = len(extra)

    def body(*refs):
        kernel(*refs[:n_in], *refs[n_in + n_extra :])

    return pl.pallas_call(
        body,
        grid=grid,
        in_specs=list(in_specs) + [pl.BlockSpec(memory_space=pltpu.HBM)] * n_extra,
        out_specs=out_specs,
        out_shape=out_shapes,
        scratch_shapes=scratch,
        input_output_aliases=aliases,
        compiler_params=params(),
        cost_estimate=estimate,
    )(*args, *in_hbm(extra))


def normed(values):
    center = values - jnp.mean(values, axis=-1, keepdims=True)
    spread = jnp.mean(center * center, axis=-1, keepdims=True)
    scale = lax.rsqrt(spread + epsilon)
    return center * scale, scale


def norm_back(grad, xhat, scale, gain):
    gy = grad * gain
    return scale * (
        gy - jnp.mean(gy, axis=-1, keepdims=True) - xhat * jnp.mean(gy * xhat, axis=-1, keepdims=True)
    )


def causal_tile(rows):
    return lax.broadcasted_iota(jnp.int32, (rows, rows), 0) >= lax.broadcasted_iota(
        jnp.int32, (rows, rows), 1
    )


def feature_weights(omega, odd):
    ones = jnp.full(omega.shape, -1.0, omega.dtype)
    zeros = jnp.zeros_like(ones)
    parts = [ones, omega, zeros, ones] if odd else [omega, ones, ones, zeros]
    return jnp.concatenate(parts, axis=0)


PER = 2


def features_kernel(hd, x_ref, gains_ref, w_ref, omega_ref, qkv_ref, phiq_ref, phik_ref, h1_ref, state_ref, qkv_scr):
    step = pl.program_id(0)
    width = 2 * hd
    rows, model = x_ref.shape[1:]
    s = hd ** (-0.25)
    feats = omega_ref.shape[2]

    @pl.when(step == 0)
    def _():
        xhat, _ = normed(x_ref[0].astype(f32))
        hidden = (xhat * gains_ref[0:1, :]).astype(bf16)
        h1_ref[0] = hidden
        for part in range(3):
            cols = slice(part * model, (part + 1) * model)
            made = nn(hidden, w_ref[:, cols]).astype(bf16)
            qkv_ref[0, :, cols] = made
            qkv_scr[part] = made

    low = lanes_of((rows, width)) < hd
    lefts = []
    for at in range(PER):
        column = pl.ds(pl.multiple_of((step * PER + at) * width, width), width)
        for part in range(2):
            points = qkv_scr[part, :, column].astype(f32)
            energy = points * points * (0.5 * s)
            high = energy.astype(bf16).astype(f32)
            rest = (energy - high).astype(bf16)
            turned = pltpu.roll(high, hd, 1)
            for odd in range(2):
                first = jnp.where(low, turned, points) if odd else jnp.where(low, points, turned)
                lefts.append((at, part, odd, jnp.concatenate([first.astype(bf16), rest], axis=1)))
    made = {}
    for at, part, odd, left in lefts:
        proj = nn(left, feature_weights(omega_ref[2 * at + odd], odd))
        phi = jnp.exp2(proj * (s * math.log2(math.e)) - 0.5 * math.log2(feats)).astype(bf16)
        head = 2 * at + odd
        (phik_ref if part else phiq_ref)[0, :, head * feats : (head + 1) * feats] = phi
        if part:
            made[at, odd] = phi
    for at in range(PER):
        column = pl.ds(pl.multiple_of((step * PER + at) * width, width), width)
        values = qkv_scr[2, :, column]
        state_ref[at, 0:hd, :] = tn(values, made[at, 0])[0:hd].astype(bf16)
        state_ref[at, hd:width, :] = tn(values, made[at, 1])[hd:width].astype(bf16)
        sums = jnp.concatenate(
            [
                jnp.sum(made[at, 0].astype(f32), axis=0, keepdims=True),
                jnp.sum(made[at, 1].astype(f32), axis=0, keepdims=True),
                jnp.zeros((14, feats), f32),
            ],
            axis=0,
        )
        state_ref[at, width : width + 16, :] = sums.astype(bf16)


def features_call(index, at, count, inputs, gains, w_qkv, omega, before, after=()):
    batch, rows, model = inputs.shape
    heads, hd, feats = omega.shape
    pairs = heads // 2
    steps = pairs // PER
    n_rows = 2 * hd + 16
    phi_spec = pl.BlockSpec((1, rows, 2 * PER * feats), lambda g: (index, 0, g))
    return stacked_call(
        functools.partial(features_kernel, hd),
        (steps,),
        [
            pl.BlockSpec((1, rows, model), lambda g: (index, 0, 0)),
            const_block(gains.shape),
            const_block(w_qkv.shape),
            pl.BlockSpec((2 * PER, hd, feats), lambda g: (g, 0, 0)),
        ],
        [
            pl.BlockSpec((1, rows, 3 * model), lambda g: (index, 0, 0)),
            phi_spec,
            phi_spec,
            pl.BlockSpec((1, rows, model), lambda g: (index, 0, 0)),
            pl.BlockSpec((PER, n_rows, feats), lambda g: (at * steps + g, 0, 0)),
        ],
        [
            jax.ShapeDtypeStruct((batch, rows, 3 * model), bf16),
            jax.ShapeDtypeStruct((batch, rows, heads * feats), bf16),
            jax.ShapeDtypeStruct((batch, rows, heads * feats), bf16),
            jax.ShapeDtypeStruct((batch, rows, model), bf16),
            jax.ShapeDtypeStruct((count * pairs, n_rows, feats), bf16),
        ],
        (True, True, True, True, at > 0),
        before,
        (inputs, gains, w_qkv, omega),
        [pltpu.VMEM((3, rows, model), bf16)],
        cost(2 * rows * model * 3 * model + 4 * heads * rows * 256 * feats, 9 * MIB, 2 * rows * heads * feats),
        after,
    )


def state_block(state_refs, backward, at, step, hd, first, count):
    if len(state_refs) == 1:
        total = state_refs[0][at].astype(f32)
    else:
        near, got, other = state_refs
        core = lax.rem(lax.axis_index("seq"), 2)
        own_half = (first + step * PER + at) // (count // 2) == core
        own = jnp.where(own_half, 1.0, 0.0)
        beside = jnp.where(core == (0 if backward else 1), 1.0, 0.0)
        total = (
            got[at].astype(f32) * own + other[at].astype(f32) * (1.0 - own) + near[at].astype(f32) * beside
        )
    feats = total.shape[-1]
    width = 2 * hd
    zeros = jnp.zeros((hd, feats), bf16)
    low = total.astype(bf16)
    even_norm = jnp.broadcast_to(total[width : width + 1], (hd, feats)).astype(bf16)
    odd_norm = jnp.broadcast_to(total[width + 1 : width + 2], (hd, feats)).astype(bf16)
    even = jnp.concatenate([low[0:hd], zeros, even_norm, zeros], axis=0)
    odd = jnp.concatenate([zeros, low[hd:width], zeros, odd_norm], axis=0)
    return even, odd


def state_specs(carried, pairs):
    states, at, count = carried
    shape = (PER,) + states[0].shape[1:]
    first = at * pairs // PER
    specs = [pl.BlockSpec(shape, lambda g: (first + g, 0, 0))]
    if len(states) > 1:
        specs += [pl.BlockSpec(shape, lambda g: (lax.rem(first + g, count // 2 // PER), 0, 0))] * 2
    return specs


def mix_kernel(hd, n_states, first, count, tile, *refs):
    x_ref, gains_ref, wout_ref, phiq_ref, phik_ref, v_ref = refs[:6]
    state_refs = refs[6 : 6 + n_states]
    mixed_ref, rden_ref, x1_ref, h2_ref, mixed_scr = refs[6 + n_states :]
    step = pl.program_id(0)
    width = 2 * hd
    rows, model = x_ref.shape[1:]
    steps = model // width // PER
    feats = phiq_ref.shape[-1] // (2 * PER)
    causal = causal_tile(tile)
    low = lanes_of((rows, width)) < hd
    ones = jnp.where(low, 1.0, 0.0)
    spans = [(slice(at * tile, (at + 1) * tile), (at + 1) * tile) for at in range(rows // tile)]
    scores = {}
    for at in range(PER):
        for odd in range(2):
            cols = slice((2 * at + odd) * feats, (2 * at + odd + 1) * feats)
            for t, (here, end) in enumerate(spans):
                scores[at, odd, t] = masked(nt(phiq_ref[0, here, cols], phik_ref[0, 0:end, cols]), causal, t, tile)
    for at in range(PER):
        even, odd = state_block(state_refs, False, at, step, hd, first, count)
        both_state = jnp.concatenate([even, odd], axis=1)
        values = v_ref[0, :, at * width : (at + 1) * width].astype(f32)
        sides = [
            jnp.concatenate([jnp.where(low, values, 0.0), ones], axis=1).astype(bf16),
            jnp.concatenate([jnp.where(low, 0.0, values), 1.0 - ones], axis=1).astype(bf16),
        ]
        cols = slice(2 * at * feats, 2 * (at + 1) * feats)
        lanes = slice(at * width, (at + 1) * width)
        column = pl.ds(pl.multiple_of((lax.rem(step, steps) * PER + at) * width, width), width)
        for t, (here, end) in enumerate(spans):
            total = nt(phiq_ref[0, here, cols], both_state)
            for odd in range(2):
                total = total + nn(scores[at, odd, t], sides[odd][0:end])
            rden = 1.0 / total[:, width:]
            mixed = (total[:, :width] * rden).astype(bf16)
            rden_ref[0, here, lanes] = rden
            mixed_ref[0, here, lanes] = mixed
            mixed_scr[here, column] = mixed

    @pl.when(lax.rem(step, steps) == steps - 1)
    def _():
        x1 = x_ref[0].astype(f32) + nn(mixed_scr[...], wout_ref[...])
        x1_ref[0] = x1
        xhat, _ = normed(x1)
        h2_ref[0] = (xhat * gains_ref[1:2, :]).astype(bf16)


def masked(made, causal, at, tile):
    last = jnp.where(causal, made[:, at * tile :], 0.0)
    if at > 0:
        last = jnp.concatenate([made[:, : at * tile], last], axis=1)
    return last.astype(bf16)


def mix_call(index, members, inputs, gains, w_out, phi_q, phi_k, qkv, carried, before, hd, after=()):
    batch, rows, model = inputs.shape
    width = 2 * hd
    pairs = model // width
    steps = pairs // PER
    states, at, count = carried
    heads = 2 * pairs
    feats = phi_q.shape[-1] // heads
    tile = min(256, rows)
    whole = pl.BlockSpec((1, rows, model), lambda g: (index + g // steps, 0, 0))
    narrow = pl.BlockSpec((1, rows, PER * width), lambda g: (index + g // steps, 0, lax.rem(g, steps)))
    phi_spec = pl.BlockSpec((1, rows, 2 * PER * feats), lambda g: (index + g // steps, 0, lax.rem(g, steps)))
    return stacked_call(
        functools.partial(mix_kernel, hd, len(states), at * pairs, count, tile),
        (members * steps,),
        [
            whole,
            const_block(gains.shape),
            const_block(w_out.shape),
            phi_spec,
            phi_spec,
            pl.BlockSpec((1, rows, PER * width), lambda g: (index + g // steps, 0, 2 * steps + lax.rem(g, steps))),
        ]
        + state_specs(carried, pairs),
        [narrow, narrow, whole, whole],
        [
            jax.ShapeDtypeStruct((batch, rows, model), bf16),
            jax.ShapeDtypeStruct((batch, rows, model), f32),
            jax.ShapeDtypeStruct((batch, rows, model), f32),
            jax.ShapeDtypeStruct((batch, rows, model), bf16),
        ],
        (True,) * 4,
        before,
        (inputs, gains, w_out, phi_q, phi_k, qkv) + tuple(states),
        [pltpu.VMEM((rows, model), bf16)],
        cost(members * (heads * 2 * rows * rows * 512 + 2 * rows * model * model), members * 9 * MIB),
        after,
    )


def ffn_kernel(groups, batch, hd, *refs):
    h2_ref, gf_ref, x1_ref, mixed_ref, rden_ref, phiq_ref, wout_ref, gains_ref = refs[:8]
    weights = refs[8 : 8 + groups]
    act_ref, pre_ref, g1_ref, ga_ref, gain_ref, side_ref, gstate_ref = refs[8 + groups : 15 + groups]
    up_scr, down_scr, pre_scr, sems = refs[15 + groups :]
    step = pl.program_id(0)
    n_blocks = pl.num_programs(0) - batch
    each = n_blocks // groups
    block = act_ref.shape[-1]
    rows = h2_ref.shape[1]
    model = h2_ref.shape[2]
    shards, unit = up_scr.shape[1:3]
    taken = block // unit
    started = []
    for group in range(groups):
        started.append(pltpu.make_async_copy(weights[group].at[:, 0], up_scr.at[group], sems.at[2 * group]))
        started.append(pltpu.make_async_copy(weights[group].at[:, 1], down_scr.at[group], sems.at[2 * group + 1]))

    @pl.when(step == 0)
    def _():
        for copy in started:
            copy.start()

    for group in range(groups):

        @pl.when(step == group * each)
        def _():
            started[2 * group].wait()
            started[2 * group + 1].wait()

    @pl.when(step < n_blocks)
    def _():
        here = pl.ds(pl.multiple_of(lax.rem(step, each) * taken, taken), taken)
        up = up_scr[step // each, here].reshape(block, model)
        down = down_scr[step // each, here].reshape(block, model)
        cols = pl.ds(pl.multiple_of(step * block, block), block)
        for b in range(batch):
            pre = nt(h2_ref[b], up)
            part = 0.5 * lax.erf(pre * math.sqrt(0.5)) + 0.5
            act_ref[b] = (pre * part).astype(bf16)
            slope = part + pre * (
                jnp.exp2(pre * pre * (-0.5 * math.log2(math.e))) * (1.0 / math.sqrt(2.0 * math.pi))
            )
            grad_pre = (nt(gf_ref[b], down) * slope).astype(bf16)
            pre_ref[b] = grad_pre
            pre_scr[b, :, cols] = grad_pre

    @pl.when(step >= n_blocks)
    def _():
        b = step - n_blocks
        grad = nn(pre_scr[b], up_scr[...].reshape(n_blocks * block, model))
        xhat, scale = normed(x1_ref[0])
        g1 = gf_ref[b].astype(f32) + norm_back(grad, xhat, scale, gains_ref[1:2, :])
        g1_ref[0] = g1
        gain = jnp.sum(grad * xhat, axis=0, keepdims=True)

        @pl.when(b == 0)
        def _():
            gain_ref[...] = jnp.zeros_like(gain_ref)

        gain_ref[0:1] += gain
        ga = g1.astype(bf16)
        ga_ref[0] = ga
        gn_full = nt(ga, wout_ref[...]) * rden_ref[0]
        gn_low = gn_full.astype(bf16)
        product = gn_full * mixed_ref[0].astype(f32)
        high = product.astype(bf16)
        rest = (product - high.astype(f32)).astype(bf16)
        width = 2 * hd
        same = lax.div(lax.rem(lax.broadcasted_iota(jnp.int32, (2 * width, width), 0), width), hd) == lax.div(
            lax.broadcasted_iota(jnp.int32, (2 * width, width), 1), hd
        )
        minus = jnp.where(same, -1.0, 0.0).astype(bf16)
        inner = lax.rem(lanes_of((rows, width)), hd)
        feats = phiq_ref.shape[-1] // (model // hd)
        for at in range(model // width):
            cols = slice(at * width, (at + 1) * width)
            gd = nn(jnp.concatenate([high[:, cols], rest[:, cols]], axis=1), minus)
            gd_high = gd.astype(bf16).astype(f32)
            gdx = jnp.where(inner == 0, gd_high, jnp.where(inner == 1, gd - gd_high, 0.0))
            side = jnp.concatenate([gn_low[:, cols], gdx.astype(bf16)], axis=1)
            side_ref[0, at] = side
            even = tn(side, phiq_ref[0, :, 2 * at * feats : (2 * at + 1) * feats])
            odd = tn(side, phiq_ref[0, :, (2 * at + 1) * feats : (2 * at + 2) * feats])
            gstate_ref[at, 0:hd] = even[0:hd].astype(bf16)
            gstate_ref[at, hd:width] = odd[hd:width].astype(bf16)
            norms = jnp.concatenate(
                [
                    even[width : width + 1] + even[width + 1 : width + 2],
                    odd[width + hd : width + hd + 1] + odd[width + hd + 1 : width + hd + 2],
                    jnp.zeros((14, feats), f32),
                ],
                axis=0,
            )
            gstate_ref[at, width : width + 16] = norms.astype(bf16)


def ffn_call(h2, gf, x1, mixed, rden, phi_q, w_out, gains, weights, hd):
    batch, rows, model = h2.shape
    groups = len(weights)
    shards, _, unit, _ = weights[0].shape
    hidden = groups * shards * unit
    block = min(512, shards * unit)
    n_blocks = hidden // block
    pairs = model // (2 * hd)
    feats = phi_q.shape[-1] // (2 * pairs)
    n_rows = 2 * hd + 16
    here = lambda j: jnp.clip(j - n_blocks, 0, batch - 1)
    late = pl.BlockSpec((1, rows, model), lambda j: (here(j), 0, 0))
    wide = pl.BlockSpec((batch, rows, block), lambda j: (0, 0, jnp.minimum(j, n_blocks - 1)))
    scratch = (groups, shards, unit, model)
    return pl.pallas_call(
        functools.partial(ffn_kernel, groups, batch, hd),
        grid=(n_blocks + batch,),
        in_specs=[
            const_block(h2.shape),
            const_block(gf.shape),
            late,
            late,
            late,
            pl.BlockSpec((1, rows, phi_q.shape[-1]), lambda j: (here(j), 0, 0)),
            const_block(w_out.shape),
            const_block(gains.shape),
        ]
        + [pl.BlockSpec(memory_space=pl.ANY)] * groups,
        out_specs=[
            wide,
            wide,
            late,
            late,
            const_block((16, model)),
            pl.BlockSpec((1, pairs, rows, 4 * hd), lambda j: (here(j), 0, 0, 0)),
            pl.BlockSpec((pairs, n_rows, feats), lambda j: (here(j), 0, 0)),
        ],
        out_shape=[
            jax.ShapeDtypeStruct((batch, rows, hidden), bf16),
            jax.ShapeDtypeStruct((batch, rows, hidden), bf16),
            jax.ShapeDtypeStruct((batch, rows, model), f32),
            jax.ShapeDtypeStruct((batch, rows, model), bf16),
            jax.ShapeDtypeStruct((16, model), f32),
            jax.ShapeDtypeStruct((batch, pairs, rows, 4 * hd), bf16),
            jax.ShapeDtypeStruct((batch * pairs, n_rows, feats), bf16),
        ],
        scratch_shapes=[
            pltpu.VMEM(scratch, bf16),
            pltpu.VMEM(scratch, bf16),
            pltpu.VMEM((batch, rows, hidden), bf16),
            pltpu.SemaphoreType.DMA((2 * groups,)),
        ],
        compiler_params=params(),
        cost_estimate=cost(6 * batch * rows * hidden * model, 30 * MIB, 2 * batch * rows * hidden),
    )(h2, gf, x1, mixed, rden, phi_q, w_out, gains, *weights)


def row_owner(far, first, second):
    seq = lax.axis_index("seq")
    y, x = lax.rem(lax.axis_index("dp"), 2), seq // 2
    core = lax.rem(seq, 2) ^ far
    turned = core == 1
    y = y ^ jnp.where(turned, second, first)
    x = x ^ jnp.where(turned, first, second)
    return core * 4 + y * 2 + x


EXTRA = 16


def ffn_weight_kernel(groups, fast, n_after, *refs):
    act_ref, pre_ref, gf_ref, h2_ref, gain_ref, mixed_any, ga_any = refs[:7]
    outs = refs[7 + n_after : 9 + n_after]
    mixed_scr, ga_scr, sum_scr, sems = refs[9 + n_after :]
    step = pl.program_id(0)
    n_blocks = pl.num_programs(0) - 1
    batch, rows, block = act_ref.shape
    model = gf_ref.shape[2]
    copies = [
        pltpu.make_async_copy(mixed_any, mixed_scr, sems.at[0]),
        pltpu.make_async_copy(ga_any, ga_scr, sems.at[1]),
    ]

    @pl.when(step == 0)
    def _():
        for copy in copies:
            copy.start()

    @pl.when(step < n_blocks)
    def _():
        down = tn(act_ref[...].reshape(batch * rows, block), gf_ref[...].reshape(batch * rows, model)).astype(bf16)
        up = tn(pre_ref[...].reshape(batch * rows, block), h2_ref[...].reshape(batch * rows, model)).astype(bf16)
        if not fast:
            outs[0][0, 0] = up
            outs[0][0, 1] = down
            return
        unit = block // 8
        held = outs[0].shape[0] // 2
        for group in range(groups):

            @pl.when(step == group)
            def _():
                out = outs[group // 2]
                first = (group % 2) * held
                for at in range(8):
                    row = first + 2 * at * unit
                    here = slice(at * unit, (at + 1) * unit)
                    out[row : row + unit] = up[here]
                    out[row + unit : row + 2 * unit] = down[here]

    @pl.when(step == n_blocks)
    def _():
        for copy in copies:
            copy.wait()
        total = tn(mixed_scr[...].reshape(batch * rows, model), ga_scr[...].reshape(batch * rows, model))
        if not fast:
            outs[1][...] = total
            return
        sum_scr[...] = total
        piece = model // 8
        held = outs[0].shape[0] // 2
        gain = gain_ref[...].astype(bf16)
        for far in range(2):
            for first in range(2):
                for second in range(2):
                    owner = row_owner(far, first, second)
                    taken = sum_scr[pl.ds(pl.multiple_of(owner * piece, piece), piece), :].astype(bf16)
                    out = outs[0 if far else 1]
                    row = (first + 1) * held - (2 - second) * (piece + EXTRA)
                    out[row : row + piece] = taken
                    out[row + piece : row + piece + EXTRA] = gain


def ffn_weight_call(act, pre, gf, h2, gain, mixed, ga, weights, fast, after=()):
    batch, rows, model = h2.shape
    groups = len(weights)
    shards, _, unit, _ = weights[0].shape
    hidden = act.shape[-1]
    block = min(512, shards * unit)
    n_blocks = hidden // block
    wide = pl.BlockSpec((batch, rows, block), lambda j: (0, 0, jnp.minimum(j, n_blocks - 1)))
    if fast:
        shape = (4 * shards * unit + 4 * (model // 8 + EXTRA), model)
        out_specs = [const_block(shape)] * 2
        out_shapes = [jax.ShapeDtypeStruct(shape, bf16)] * 2
    else:
        out_specs = [
            pl.BlockSpec((1, 2, block, model), lambda j: (jnp.minimum(j, n_blocks - 1), 0, 0, 0)),
            const_block((model, model)),
        ]
        out_shapes = [
            jax.ShapeDtypeStruct((n_blocks, 2, block, model), bf16),
            jax.ShapeDtypeStruct((model, model), f32),
        ]
    anywhere = pl.BlockSpec(memory_space=pl.ANY)
    return pl.pallas_call(
        functools.partial(ffn_weight_kernel, groups, fast, len(after)),
        grid=(n_blocks + 1,),
        in_specs=[wide, wide, const_block(gf.shape), const_block(h2.shape), const_block(gain.shape), anywhere, anywhere]
        + [anywhere] * len(after),
        out_specs=out_specs,
        out_shape=out_shapes,
        scratch_shapes=[
            pltpu.VMEM(mixed.shape, bf16),
            pltpu.VMEM(ga.shape, bf16),
            pltpu.VMEM((model, model), f32),
            pltpu.SemaphoreType.DMA((2,)),
        ],
        compiler_params=params(),
        cost_estimate=cost(4 * batch * rows * hidden * model, 22 * MIB),
    )(act, pre, gf, h2, gain, mixed, ga, *in_hbm(after))


def attention_back_kernel(hd, n_prev, n_later, spots, tile, *refs):
    side_ref, phiq_ref, phik_ref, q_ref, k_ref, v_ref, omega_ref = refs[:7]
    prev_refs = refs[7 : 7 + n_prev]
    later_refs = refs[7 + n_prev : 7 + n_prev + n_later]
    (out_ref,) = refs[7 + n_prev + n_later :]
    step = pl.program_id(0)
    width = 2 * hd
    rows = q_ref.shape[1]
    feats = phiq_ref.shape[-1] // (2 * PER)
    tiles = rows // tile
    s = hd ** (-0.25)
    low = lanes_of((rows, width)) < hd
    low_tile = low[0:tile]
    inner = lax.rem(lanes_of((rows, width)), hd)
    ones = jnp.where(inner < 2, 1.0, 0.0)
    one = jnp.where(inner == 0, 1.0, 0.0).astype(bf16)
    causal = causal_tile(tile)
    spans = [(slice(t * tile, (t + 1) * tile), (t + 1) * tile) for t in range(tiles)]
    heads = [(at, odd) for at in range(PER) for odd in range(2)]
    each = [(at, odd, t) for at, odd in heads for t in range(tiles)]
    cols = {(at, odd): slice((2 * at + odd) * feats, (2 * at + odd + 1) * feats) for at, odd in heads}
    lanes = [slice(at * width, (at + 1) * width) for at in range(PER)]

    def column(made, at, odd, t):
        return jnp.concatenate([made[at, odd, i][:, t * tile : (t + 1) * tile] for i in range(t, tiles)], axis=0)

    made, scores, weights, value_sides = {}, {}, {}, {}
    for at in range(PER):
        values = v_ref[0, :, lanes[at]].astype(f32)
        value_sides[at, 0] = jnp.concatenate(
            [jnp.where(low, values, 0.0), jnp.where(low, ones, 0.0)], axis=1
        ).astype(bf16)
        value_sides[at, 1] = jnp.concatenate(
            [jnp.where(low, 0.0, values), jnp.where(low, 0.0, ones)], axis=1
        ).astype(bf16)
    for at, odd, t in each:
        here, end = spans[t]
        made[at, odd, t] = masked(nt(side_ref[0, at, here], value_sides[at, odd][0:end]), causal, t, tile)
    for at, odd, t in each:
        here, end = spans[t]
        scores[at, odd, t] = masked(
            nt(phiq_ref[0, here, cols[at, odd]], phik_ref[0, 0:end, cols[at, odd]]), causal, t, tile
        )
    prev = [state_block(prev_refs, False, at, step, hd, *spots[0]) for at in range(PER)]
    later = [state_block(later_refs, True, at, step, hd, *spots[1]) for at in range(PER)]
    for at, odd in heads:
        weights[at, odd] = feature_weights(omega_ref[2 * at + odd], odd)
    proj_q, proj_k = {}, {}
    for at, odd, t in each:
        here, end = spans[t]
        grad_phi = nn(side_ref[0, at, here], prev[at][odd]) + nn(made[at, odd, t], phik_ref[0, 0:end, cols[at, odd]])
        proj_q[at, odd, t] = (grad_phi * phiq_ref[0, here, cols[at, odd]].astype(f32)).astype(bf16)
    for at, odd, t in each:
        here = spans[t][0]
        beside = jnp.concatenate([v_ref[0, here, lanes[at]], one[here]], axis=1)
        grad_phi = nn(beside, later[at][odd]) + tn(column(made, at, odd, t), phiq_ref[0, t * tile :, cols[at, odd]])
        proj_k[at, odd, t] = (grad_phi * phik_ref[0, here, cols[at, odd]].astype(f32)).astype(bf16)
    back_q = {key: nt(proj_q[key], weights[key[:2]]) for key in each}
    back_k = {key: nt(proj_k[key], weights[key[:2]]) for key in each}
    for at in range(PER):
        both = jnp.concatenate([later[at][0][0:width], later[at][1][0:width]], axis=1)
        gn_pair = side_ref[0, at, :, 0:width].astype(f32)
        gn_sides = [jnp.where(low, gn_pair, 0.0).astype(bf16), jnp.where(low, 0.0, gn_pair).astype(bf16)]
        for t in range(tiles):
            here = spans[t][0]
            grad_v = nt(phik_ref[0, here, 2 * at * feats : 2 * (at + 1) * feats], both)
            for odd in range(2):
                grad_v = grad_v + tn(column(scores, at, odd, t), gn_sides[odd][t * tile :])
            out_ref[0, 2, here, lanes[at]] = grad_v.astype(bf16)
    for part, back, points_ref in ((0, back_q, q_ref), (1, back_k, k_ref)):
        for at in range(PER):
            for t in range(tiles):
                here = spans[t][0]
                even, odd = back[at, 0, t], back[at, 1, t]
                along = jnp.where(low_tile, even[:, :width], odd[:, :width])
                total = jnp.where(low_tile, even[:, width:], odd[:, width:])
                points = points_ref[0, here, lanes[at]].astype(f32)
                out_ref[0, part, here, lanes[at]] = (s * along + (s * s) * points * total).astype(bf16)


def attention_back_call(index, side, phi_q, phi_k, qkv, omega, carried, later, before, after=()):
    batch, pairs, rows, wide = side.shape
    heads, hd, feats = omega.shape
    steps = pairs // PER
    model = pairs * 2 * hd
    tile = min(256, rows)
    phi_spec = pl.BlockSpec((1, rows, 2 * PER * feats), lambda g: (index, 0, g))
    spots = tuple((at * pairs, count) for _, at, count in (carried, later))

    def part(n):
        return pl.BlockSpec((1, rows, 2 * PER * hd), lambda g: (index, 0, n * steps + g))

    return stacked_call(
        functools.partial(attention_back_kernel, hd, len(carried[0]), len(later[0]), spots, tile),
        (steps,),
        [
            pl.BlockSpec((1, PER, rows, wide), lambda g: (index, g, 0, 0)),
            phi_spec,
            phi_spec,
            part(0),
            part(1),
            part(2),
            pl.BlockSpec((2 * PER, hd, feats), lambda g: (g, 0, 0)),
        ]
        + state_specs(carried, pairs)
        + state_specs(later, pairs),
        [pl.BlockSpec((1, 3, rows, 2 * PER * hd), lambda g: (index, 0, 0, g))],
        [jax.ShapeDtypeStruct((batch, 3, rows, model), bf16)],
        (True,),
        before,
        (side, phi_q, phi_k, qkv, qkv, qkv, omega) + tuple(carried[0]) + tuple(later[0]),
        [],
        cost(heads * 2 * rows * (rows * 1024 + 6 * 65536), 12 * MIB),
        after,
    )


def qkv_weight_kernel(fast, n_after, *refs):
    h1_ref, grad_ref = refs[:2]
    outs = refs[2 + n_after :]
    batch, rows, model = h1_ref.shape
    total = tn(h1_ref[...].reshape(batch * rows, model), grad_ref[...].reshape(batch * rows, model))
    if not fast:
        outs[0][...] = total
        return
    far_ref, low_ref, high_ref, sum_scr = outs
    sum_scr[...] = total
    piece = model // 8
    for far in range(2):
        for first in range(2):
            for second in range(2):
                owner = row_owner(far, first, second)
                taken = sum_scr[pl.ds(pl.multiple_of(owner * piece, piece), piece), :].astype(bf16)
                if far:
                    far_ref[2 * first + second, 0] = taken
                else:
                    (high_ref if first else low_ref)[second, 0] = taken


def qkv_weight_call(h1, grads, fast, after=()):
    batch, rows, model = h1.shape
    if fast:
        sizes = (4, 2, 2)
        out_specs = [pl.BlockSpec((n, 1, model // 8, model), lambda p: (0, p, 0, 0)) for n in sizes]
        out_shapes = [jax.ShapeDtypeStruct((n, 3, model // 8, model), bf16) for n in sizes]
    else:
        out_specs = [pl.BlockSpec((model, model), lambda p: (0, p))]
        out_shapes = [jax.ShapeDtypeStruct((model, 3 * model), f32)]
    return pl.pallas_call(
        functools.partial(qkv_weight_kernel, fast, len(after)),
        grid=(3,),
        in_specs=[const_block(h1.shape), pl.BlockSpec((batch, 1, rows, model), lambda p: (0, p, 0, 0))]
        + [pl.BlockSpec(memory_space=pl.ANY)] * len(after),
        out_specs=out_specs,
        out_shape=out_shapes,
        scratch_shapes=[pltpu.VMEM((model, model), f32)] if fast else [],
        compiler_params=params(),
        cost_estimate=cost(6 * batch * rows * model * model, 8 * MIB),
    )(h1, grads, *in_hbm(after))


def inputs_back_kernel(grads_ref, w_ref, x_ref, g1_ref, gains_ref, grad_ref):
    model = x_ref.shape[2]
    grad = nt(grads_ref[0, 0], w_ref[:, :model])
    for part in (1, 2):
        grad = grad + nt(grads_ref[0, part], w_ref[:, part * model : (part + 1) * model])
    xhat, scale = normed(x_ref[0].astype(f32))
    grad_ref[0] = g1_ref[0] + norm_back(grad, xhat, scale, gains_ref[0:1, :])


def inputs_back_call(index, grads, w_qkv, inputs, g1, gains, before, after=()):
    batch, rows, model = inputs.shape
    whole = pl.BlockSpec((1, rows, model), lambda j: (index, 0, 0))
    return stacked_call(
        inputs_back_kernel,
        (1,),
        [
            pl.BlockSpec((1, 3, rows, model), lambda j: (index, 0, 0, 0)),
            const_block(w_qkv.shape),
            whole,
            whole,
            const_block(gains.shape),
        ],
        [whole],
        [jax.ShapeDtypeStruct((batch, rows, model), f32)],
        (True,),
        before,
        (grads, w_qkv, inputs, g1, gains),
        [],
        cost(6 * rows * model * model, 6 * MIB),
        after,
    )


def outputs_kernel(groups, *refs):
    act_ref, x1_ref = refs[:2]
    weights = refs[2 : 2 + groups]
    out_ref, down_scr, sems = refs[2 + groups :]
    copies = [
        pltpu.make_async_copy(weights[group].at[:, 1], down_scr.at[group], sems.at[group]) for group in range(groups)
    ]
    for copy in copies:
        copy.start()
    for copy in copies:
        copy.wait()
    down = down_scr[...].reshape(act_ref.shape[2], x1_ref.shape[2])
    out_ref[0] = (x1_ref[0] + nn(act_ref[0], down)).astype(bf16)


def outputs_call(index, act, x1, weights, before, after=()):
    batch, rows, model = x1.shape
    hidden = act.shape[2]
    groups = len(weights)
    shards, _, unit, _ = weights[0].shape
    one = lambda j: (index, 0, 0)
    return stacked_call(
        functools.partial(outputs_kernel, groups),
        (1,),
        [pl.BlockSpec((1, rows, hidden), one), pl.BlockSpec((1, rows, model), one)]
        + [pl.BlockSpec(memory_space=pl.ANY)] * groups,
        [pl.BlockSpec((1, rows, model), one)],
        [jax.ShapeDtypeStruct((batch, rows, model), bf16)],
        (True,),
        before,
        (act, x1) + tuple(weights),
        [pltpu.VMEM((groups, shards, unit, model), bf16), pltpu.SemaphoreType.DMA((groups,))],
        cost(2 * rows * model * hidden, 6 * MIB),
        after,
    )


CORE = (1, 1)
GATHER = ((16, 8), (8, 16), (2, 4), (4, 2))
PLANE = ((4, 2), (2, 4))
LINE = ((16, 8), (8, 16))


def swap(array, masks):
    return lax.ppermute(array, AXES, [(i, i ^ masks[i & 1]) for i in range(32)])


def summed(*arrays):
    return functools.reduce(lambda a, b: a + b, [a.astype(f32) for a in arrays])


def summed_low(*arrays):
    return summed(*arrays).astype(bf16)


def gate(array, *deps):
    anywhere = pl.BlockSpec(memory_space=pltpu.HBM)
    return pl.pallas_call(
        lambda *refs: None,
        in_specs=[anywhere] * (1 + len(deps)),
        out_specs=anywhere,
        out_shape=jax.ShapeDtypeStruct(array.shape, array.dtype),
        input_output_aliases={0: 0},
    )(*in_hbm((array,) + deps))


def all_states(local, backward):
    everything = lax.all_gather(local, "seq").astype(f32)
    count, place = lax.axis_size("seq"), lax.axis_index("seq")
    at = jnp.arange(count)
    wanted = (at > place) if backward else (at < place)
    total = jnp.sum(jnp.where(wanted[:, None, None, None], everything, 0.0), axis=0)
    return (total.astype(bf16),)


def chip_half(local, near):
    core = lax.rem(lax.axis_index("seq"), 2)
    half = local.shape[0] // 2
    return jnp.where(core == 0, summed_low(local[:half], near[:half]), summed_low(local[half:], near[half:]))


def along_x(mine, backward):
    from_x = 1 if backward else 0
    return lax.ppermute(mine, AXES, [(i, i ^ 2) for i in range(32) if (i >> 1) & 1 == from_x])


def assemble_kernel(near_ref, ahead_ref, far_ref, wqkv_ref, gains_ref, gw_ref, gwout_ref, ggain_ref):
    model = gwout_ref.shape[0]
    rows = model // 8
    for far in range(2):
        for first in range(2):
            for second in range(2):
                owner = row_owner(far, first, second)
                at = pl.ds(pl.multiple_of(owner * rows, rows), rows)
                if far:
                    piece = far_ref[2 * first + second]
                else:
                    piece = (ahead_ref if first else near_ref)[second]
                for part in range(3):
                    gw_ref[at, part * model : (part + 1) * model] = piece[part * rows : (part + 1) * rows].astype(f32)
                gwout_ref[at, :] = piece[3 * rows : 4 * rows].astype(f32)

                @pl.when(owner == 0)
                def _():
                    ggain_ref[1:2, :] = piece[4 * rows : 4 * rows + EXTRA].astype(f32)[0:1]

    ggain_ref[0:1, :] = first_gain(gw_ref, wqkv_ref, gains_ref)


def first_gain(gw_ref, wqkv_ref, gains_ref):
    along = jnp.sum(gw_ref[...] * wqkv_ref[...].astype(f32), axis=1, keepdims=True)
    return jnp.broadcast_to(along, (along.shape[0], 128)).T[0:1, :] / gains_ref[0:1, :]


def assemble_call(near, ahead, far, w_qkv, gains):
    model = w_qkv.shape[0]
    return pl.pallas_call(
        assemble_kernel,
        out_shape=[
            jax.ShapeDtypeStruct(w_qkv.shape, f32),
            jax.ShapeDtypeStruct((model, model), f32),
            jax.ShapeDtypeStruct(gains.shape, f32),
        ],
        compiler_params=params(),
    )(near, ahead, far, w_qkv, gains)


def gains_kernel(gw_ref, gain_ref, wqkv_ref, gains_ref, ggain_ref):
    ggain_ref[0:1, :] = first_gain(gw_ref, wqkv_ref, gains_ref)
    ggain_ref[1:2, :] = gain_ref[0:1, :]


def halves(array):
    cut = array.shape[0] // 2
    return array[:cut], array[cut:]


def next_halves(low, got, n_shard, shards, whole_pieces):
    cut = shards * n_shard
    parts = []
    for at in range(2):
        rows = slice(at * cut // 2, (at + 1) * cut // 2)
        if whole_pieces:
            piece = slice(cut, None)
        else:
            half = (low.shape[0] - cut) // 2
            piece = slice(cut + at * half, cut + (at + 1) * half)
        parts.append(
            jnp.concatenate([summed_low(low[rows], got[rows]), summed_low(low[piece], got[piece])])
        )
    return parts


def planned(inputs, gains, w_qkv, w_out, shard, omega, cotangent):
    batch, rows, model = inputs.shape
    heads, hd, _ = omega.shape
    pairs = heads // 2
    n_shard, n_piece = 2 * shard.shape[1], model // 8 + EXTRA

    held = shard[None]
    got = swap(held, GATHER[0])
    made = features_call(0, 0, 2, inputs, gains, w_qkv, omega, None)
    held = jnp.concatenate([held, gate(got, made[0])])
    got = swap(held, GATHER[1])
    made = features_call(1, 1, 2, inputs, gains, w_qkv, omega, made, (held,))
    got = gate(got, made[0])
    local = gate(made[4], got)
    near = swap(local, CORE)
    mine = chip_half(local, near)
    held = jnp.concatenate([held, got])
    got = swap(held, GATHER[2])
    far = along_x(mine, False)
    made = features_call(2, 0, 1, inputs, gains, w_qkv, omega, made, (held, mine))
    far, got = gate(far, made[0]), gate(got, made[0])
    first = (near, far, swap(far, CORE))
    local = gate(made[4], far, got)
    near = swap(local, CORE)
    mine = chip_half(local, near)
    held = jnp.concatenate([held, got])
    got = swap(held, GATHER[3])
    far = along_x(mine, False)
    beside = swap(held, CORE)
    qkv, phi_q, phi_k, h1 = made[:4]
    made = mix_call(
        0, 2, inputs, gains, w_out, phi_q, phi_k, qkv, (first, 0, 2 * pairs), None, hd, (held, mine)
    )
    far = gate(far, made[0])
    got, beside = gate(got, far), gate(beside, far)
    second = (near, far, swap(far, CORE))
    made = mix_call(
        2, 1, inputs, gains, w_out, phi_q, phi_k, qkv, (second, 0, pairs), made, hd, (got,)
    )
    weights = [beside, gate(swap(got, CORE), made[0]), held, got]
    mixed, rden, x1, h2 = made
    carried = [(first, 0, 2 * pairs), (first, 1, 2 * pairs), (second, 0, pairs)]

    act, pre, g1, ga, gain, side, local = ffn_call(
        h2, cotangent, x1, mixed, rden, phi_q, w_out, gains, weights, hd
    )
    near = swap(local, CORE)
    mine = chip_half(local, near)
    far = along_x(mine, True)
    send, low = ffn_weight_call(act, pre, cotangent, h2, gain, mixed, ga, weights, True, (mine,))
    far = gate(far, low)
    send = gate(send, far)
    later = (near, far, swap(far, CORE))

    def back(b, before, *after):
        return attention_back_call(
            b, side, phi_q, phi_k, qkv, omega, carried[b], (later, b, batch * pairs), before, after
        )

    got = swap(send, CORE)
    made = back(0, None)
    got = gate(got, made[0])
    (low, high), (got_low, got_high) = halves(low), halves(got)
    low, high = summed_low(low, got_low), summed_low(high, got_high)
    got = swap(high, GATHER[3])
    made = back(1, made, high)
    low, high = next_halves(low, gate(got, made[0]), n_shard, 8, False)
    got = swap(high, GATHER[2])
    made = back(2, made, high)
    low, high = next_halves(low, gate(got, made[0]), n_shard, 4, True)
    got = swap(high, GATHER[1])
    (grads,) = made
    late = qkv_weight_call(h1, grads, True, (high,))
    got = gate(got, late[1])
    low, high = next_halves(low, got, n_shard, 2, True)
    shard_got = swap(high, GATHER[0])

    def into(b, before, *after):
        return inputs_back_call(b, grads, w_qkv, inputs, g1, gains, before, after)

    def onto(b, before, *after):
        return outputs_call(b, act, x1, weights, before, after)

    send, keep, high = [a.reshape(a.shape[0], -1, model) for a in late]
    send = gate(send, got)
    got_low, got_high = halves(swap(send, CORE))
    high = summed_low(high, got_high)
    keep = summed_low(keep, got_low)
    got = swap(high, PLANE[0])
    into_made = into(0, None, high, keep)
    got = gate(got, into_made[0])
    high = summed_low(keep[1], got[1])
    keep = summed_low(keep[0], got[0])
    got = swap(high, PLANE[1])
    into_made = into(1, into_made, high, keep)
    keep = summed_low(keep, gate(got, into_made[0]))
    got = swap(keep, LINE[0])
    into_made = into(2, into_made, keep)
    shard_got = gate(shard_got, into_made[0])
    grad_ffn = summed(low[:n_shard], shard_got[:n_shard])
    piece = summed_low(low[n_shard:], shard_got[n_shard:])
    keep = summed_low(keep, gate(got, into_made[0]))
    got = swap(keep, LINE[1])
    onto_made = onto(0, None, keep)
    keep = jnp.concatenate([summed_low(keep, gate(got, onto_made[0])), piece])
    got = swap(keep, PLANE[1])
    onto_made = onto(1, onto_made, keep)
    near = jnp.stack([keep, gate(got, onto_made[0])])
    got = swap(near, PLANE[0])
    beside = swap(near, CORE)
    onto_made = onto(2, onto_made, near)
    ahead = gate(got, onto_made[0])
    far = jnp.concatenate([beside, swap(ahead, CORE)])
    grad_wqkv, grad_wout, grad_gains = assemble_call(near, ahead, far, w_qkv, gains)
    return onto_made[0], into_made[0], grad_gains, grad_wqkv, grad_wout, grad_ffn


def plain(inputs, gains, w_qkv, w_out, shard, omega, cotangent):
    batch, rows, model = inputs.shape
    heads, hd, _ = omega.shape
    pairs = heads // 2
    pair = lax.all_gather(shard, AXES, axis=1, tiled=True)
    hidden = pair.shape[1]
    block = min(512, hidden)
    weights = [jnp.swapaxes(pair.reshape(2, hidden // block, block, model), 0, 1)]
    made = None
    for b in range(batch):
        made = features_call(b, b, batch, inputs, gains, w_qkv, omega, made)
    qkv, phi_q, phi_k, h1, local = made
    sums = all_states(local, False)
    mixed, rden, x1, h2 = mix_call(
        0, batch, inputs, gains, w_out, phi_q, phi_k, qkv, (sums, 0, batch * pairs), None, hd
    )
    act, pre, g1, ga, gain, side, local = ffn_call(
        h2, cotangent, x1, mixed, rden, phi_q, w_out, gains, weights, hd
    )
    later = all_states(local, True)
    both, grad_wout = ffn_weight_call(act, pre, cotangent, h2, gain, mixed, ga, weights, False)
    both = jnp.swapaxes(both, 0, 1).reshape(2, -1, model)
    grad_ffn = lax.psum_scatter(both, AXES, scatter_dimension=1, tiled=True).astype(f32)
    made = None
    for b in range(batch):
        spot = (b, batch * pairs)
        made = attention_back_call(b, side, phi_q, phi_k, qkv, omega, (sums,) + spot, (later,) + spot, made)
    (grads,) = made
    (grad_wqkv,) = qkv_weight_call(h1, grads, False)
    into_made = onto_made = None
    for b in range(batch):
        into_made = inputs_back_call(b, grads, w_qkv, inputs, g1, gains, into_made)
        onto_made = outputs_call(b, act, x1, weights, onto_made)
    grad_wqkv, grad_wout, gain = lax.psum((grad_wqkv, grad_wout, gain), AXES)
    grad_gains = pl.pallas_call(
        gains_kernel,
        out_shape=jax.ShapeDtypeStruct(gains.shape, f32),
        compiler_params=params(),
    )(grad_wqkv, gain, w_qkv, gains)
    return onto_made[0], into_made[0], grad_gains, grad_wqkv, grad_wout, grad_ffn


def on_device(inputs, gains, w_qkv, w_out, ffn_weight, omega, cotangent):
    fast = lax.axis_size("dp") == 8 and lax.axis_size("seq") == 4 and inputs.shape[0] == 3
    outputs, grad_inputs, *grads = (planned if fast else plain)(
        inputs, gains[0], w_qkv[0], w_out[0], ffn_weight[0], jnp.swapaxes(omega[0], 1, 2), cotangent
    )
    grad_gains, grad_wqkv, grad_wout, grad_ffn = grads
    grad_ffn = grad_ffn.reshape(ffn_weight.shape)
    return (outputs, grad_inputs, grad_gains[None], grad_wqkv[None], grad_wout[None], grad_ffn)


def solution(mesh):
    in_specs = (
        P("dp", "seq", None),
        P(),
        P(),
        P(),
        P(None, None, ("dp", "seq"), None),
        P(),
        P("dp", "seq", None),
    )
    out_specs = (
        P("dp", "seq", None),
        P("dp", "seq", None),
        P(),
        P(),
        P(),
        P(None, None, ("dp", "seq"), None),
    )
    return jax.shard_map(
        on_device, mesh=mesh, in_specs=in_specs, out_specs=out_specs, check_vma=False
    )
```

```python
import functools
import math

import jax
import jax.numpy as jnp
from jax import lax
from jax.experimental import pallas as pl
from jax.experimental.pallas import tpu as pltpu
from jax.sharding import PartitionSpec as P

epsilon = 1e-05
bf16 = jnp.bfloat16
f32 = jnp.float32
AXES = ("dp", "seq")
MIB = 2**20


def nn(a, b):
    return lax.dot_general(a, b, (((1,), (0,)), ((), ())), preferred_element_type=f32)


def nt(a, b):
    return lax.dot_general(a, b, (((1,), (1,)), ((), ())), preferred_element_type=f32)


def tn(a, b):
    return lax.dot_general(a, b, (((0,), (0,)), ((), ())), preferred_element_type=f32)


def lanes_of(shape):
    return lax.broadcasted_iota(jnp.int32, shape, len(shape) - 1)


def params(mib=63):
    return pltpu.CompilerParams(vmem_limit_bytes=mib * MIB)


def cost(flops, nbytes, trans=0):
    return pl.CostEstimate(flops=int(flops), bytes_accessed=int(nbytes), transcendentals=int(trans))


def in_hbm(arrays):
    return [pltpu.with_memory_space_constraint(a, pltpu.HBM) for a in arrays]


def const_block(shape):
    return pl.BlockSpec(shape, lambda *_: (0,) * len(shape))


def stacked_call(kernel, grid, in_specs, out_specs, out_shapes, stacked, before, args, scratch, estimate, after=()):
    n_in = len(args)
    aliases = {}
    extra = list(after)
    if before is not None:
        for at, (flag, buffer) in enumerate(zip(stacked, before)):
            if flag:
                aliases[n_in + len(extra)] = at
                extra.append(buffer)
    n_extra = len(extra)

    def body(*refs):
        kernel(*refs[:n_in], *refs[n_in + n_extra :])

    return pl.pallas_call(
        body,
        grid=grid,
        in_specs=list(in_specs) + [pl.BlockSpec(memory_space=pltpu.HBM)] * n_extra,
        out_specs=out_specs,
        out_shape=out_shapes,
        scratch_shapes=scratch,
        input_output_aliases=aliases,
        compiler_params=params(),
        cost_estimate=estimate,
    )(*args, *in_hbm(extra))


def normed(values):
    center = values - jnp.mean(values, axis=-1, keepdims=True)
    spread = jnp.mean(center * center, axis=-1, keepdims=True)
    scale = lax.rsqrt(spread + epsilon)
    return center * scale, scale


def norm_back(grad, xhat, scale, gain):
    gy = grad * gain
    return scale * (
        gy - jnp.mean(gy, axis=-1, keepdims=True) - xhat * jnp.mean(gy * xhat, axis=-1, keepdims=True)
    )


def causal_tile(rows):
    return lax.broadcasted_iota(jnp.int32, (rows, rows), 0) >= lax.broadcasted_iota(
        jnp.int32, (rows, rows), 1
    )


def feature_weights(omega, odd):
    ones = jnp.full(omega.shape, -1.0, omega.dtype)
    zeros = jnp.zeros_like(ones)
    parts = [ones, omega, zeros, ones] if odd else [omega, ones, ones, zeros]
    return jnp.concatenate(parts, axis=0)


PER = 2
BACK_PER = 1


def features_kernel(hd, x_ref, gains_ref, w_ref, omega_ref, qkv_ref, phiq_ref, phik_ref, h1_ref, state_ref, qkv_scr):
    step = pl.program_id(0)
    width = 2 * hd
    rows, model = x_ref.shape[1:]
    s = hd ** (-0.25)
    feats = omega_ref.shape[2]
    per = omega_ref.shape[0] // 2

    @pl.when(step == 0)
    def _():
        xhat, _ = normed(x_ref[0].astype(f32))
        hidden = (xhat * gains_ref[0:1, :]).astype(bf16)
        h1_ref[0] = hidden
        for part in range(3):
            cols = slice(part * model, (part + 1) * model)
            made = nn(hidden, w_ref[:, cols]).astype(bf16)
            qkv_ref[0, :, cols] = made
            qkv_scr[part] = made

    low = lanes_of((rows, width)) < hd
    lefts = []
    for at in range(per):
        column = pl.ds(pl.multiple_of((step * per + at) * width, width), width)
        for part in range(2):
            points = qkv_scr[part, :, column].astype(f32)
            energy = points * points * (0.5 * s)
            high = energy.astype(bf16).astype(f32)
            rest = (energy - high).astype(bf16)
            turned = pltpu.roll(high, hd, 1)
            for odd in range(2):
                first = jnp.where(low, turned, points) if odd else jnp.where(low, points, turned)
                lefts.append((at, part, odd, jnp.concatenate([first.astype(bf16), rest], axis=1)))
    made = {}
    for at, part, odd, left in lefts:
        proj = nn(left, feature_weights(omega_ref[2 * at + odd], odd))
        phi = jnp.exp2(proj * (s * math.log2(math.e)) - 0.5 * math.log2(feats)).astype(bf16)
        head = 2 * at + odd
        (phik_ref if part else phiq_ref)[0, :, head * feats : (head + 1) * feats] = phi
        if part:
            made[at, odd] = phi
    for at in range(per):
        column = pl.ds(pl.multiple_of((step * per + at) * width, width), width)
        values = qkv_scr[2, :, column]
        state_ref[at, 0:hd, :] = tn(values, made[at, 0])[0:hd].astype(bf16)
        state_ref[at, hd:width, :] = tn(values, made[at, 1])[hd:width].astype(bf16)
        sums = jnp.concatenate(
            [
                jnp.sum(made[at, 0].astype(f32), axis=0, keepdims=True),
                jnp.sum(made[at, 1].astype(f32), axis=0, keepdims=True),
                jnp.zeros((14, feats), f32),
            ],
            axis=0,
        )
        state_ref[at, width : width + 16, :] = sums.astype(bf16)


def features_call(index, at, count, inputs, gains, w_qkv, omega, before, after=()):
    batch, rows, model = inputs.shape
    heads, hd, feats = omega.shape
    pairs = heads // 2
    per = pairs
    steps = pairs // per
    n_rows = 2 * hd + 16
    phi_spec = pl.BlockSpec((1, rows, 2 * per * feats), lambda g: (index, 0, g))
    return stacked_call(
        functools.partial(features_kernel, hd),
        (steps,),
        [
            pl.BlockSpec((1, rows, model), lambda g: (index, 0, 0)),
            const_block(gains.shape),
            const_block(w_qkv.shape),
            pl.BlockSpec((2 * per, hd, feats), lambda g: (g, 0, 0)),
        ],
        [
            pl.BlockSpec((1, rows, 3 * model), lambda g: (index, 0, 0)),
            phi_spec,
            phi_spec,
            pl.BlockSpec((1, rows, model), lambda g: (index, 0, 0)),
            pl.BlockSpec((per, n_rows, feats), lambda g: (at * steps + g, 0, 0)),
        ],
        [
            jax.ShapeDtypeStruct((batch, rows, 3 * model), bf16),
            jax.ShapeDtypeStruct((batch, rows, heads * feats), bf16),
            jax.ShapeDtypeStruct((batch, rows, heads * feats), bf16),
            jax.ShapeDtypeStruct((batch, rows, model), bf16),
            jax.ShapeDtypeStruct((count * pairs, n_rows, feats), bf16),
        ],
        (True, True, True, True, at > 0),
        before,
        (inputs, gains, w_qkv, omega),
        [pltpu.VMEM((3, rows, model), bf16)],
        cost(2 * rows * model * 3 * model + 4 * heads * rows * 256 * feats, 9 * MIB, 2 * rows * heads * feats),
        after,
    )


def state_block(state_refs, backward, at, step, per, hd, first, count):
    if len(state_refs) == 1:
        total = state_refs[0][at].astype(f32)
    else:
        near, got, other = state_refs
        seq = lax.axis_index("seq")
        core = lax.rem(seq, 2)
        own_half = (first + step * per + at) // (count // 2) == core
        beyond = (seq // 2) == (0 if backward else 1)
        beside = core == (0 if backward else 1)
        total = jnp.where(own_half, got[at].astype(f32), other[at].astype(f32))
        total = jnp.where(beyond, total, 0.0) + jnp.where(beside, near[at].astype(f32), 0.0)
    feats = total.shape[-1]
    width = 2 * hd
    zeros = jnp.zeros((hd, feats), bf16)
    low = total.astype(bf16)
    even_norm = jnp.broadcast_to(total[width : width + 1], (hd, feats)).astype(bf16)
    odd_norm = jnp.broadcast_to(total[width + 1 : width + 2], (hd, feats)).astype(bf16)
    even = jnp.concatenate([low[0:hd], zeros, even_norm, zeros], axis=0)
    odd = jnp.concatenate([zeros, low[hd:width], zeros, odd_norm], axis=0)
    return even, odd


def state_specs(carried, pairs, per):
    states, at, count = carried
    shape = (per,) + states[0].shape[1:]
    first = at * pairs // per
    specs = [pl.BlockSpec(shape, lambda g: (first + g, 0, 0))]
    if len(states) > 1:
        specs += [pl.BlockSpec(shape, lambda g: (lax.rem(first + g, count // 2 // per), 0, 0))] * 2
    return specs


def mix_kernel(hd, n_states, first, count, tile, *refs):
    x_ref, gains_ref, wout_ref, phiq_ref, phik_ref, v_ref = refs[:6]
    state_refs = refs[6 : 6 + n_states]
    mixed_ref, rden_ref, x1_ref, h2_ref, mixed_scr = refs[6 + n_states :]
    step = pl.program_id(0)
    width = 2 * hd
    rows, model = x_ref.shape[1:]
    steps = model // width // PER
    feats = phiq_ref.shape[-1] // (2 * PER)
    causal = causal_tile(tile)
    low = lanes_of((rows, width)) < hd
    ones = jnp.where(low, 1.0, 0.0)
    spans = [(slice(at * tile, (at + 1) * tile), (at + 1) * tile) for at in range(rows // tile)]
    scores = {}
    for at in range(PER):
        for odd in range(2):
            cols = slice((2 * at + odd) * feats, (2 * at + odd + 1) * feats)
            for t, (here, end) in enumerate(spans):
                scores[at, odd, t] = masked(nt(phiq_ref[0, here, cols], phik_ref[0, 0:end, cols]), causal, t, tile)
    for at in range(PER):
        even, odd = state_block(state_refs, False, at, step, PER, hd, first, count)
        both_state = jnp.concatenate([even, odd], axis=1)
        values = v_ref[0, :, at * width : (at + 1) * width].astype(f32)
        sides = [
            jnp.concatenate([jnp.where(low, values, 0.0), ones], axis=1).astype(bf16),
            jnp.concatenate([jnp.where(low, 0.0, values), 1.0 - ones], axis=1).astype(bf16),
        ]
        cols = slice(2 * at * feats, 2 * (at + 1) * feats)
        lanes = slice(at * width, (at + 1) * width)
        column = pl.ds(pl.multiple_of((lax.rem(step, steps) * PER + at) * width, width), width)
        for t, (here, end) in enumerate(spans):
            total = nt(phiq_ref[0, here, cols], both_state)
            for odd in range(2):
                total = total + nn(scores[at, odd, t], sides[odd][0:end])
            rden = 1.0 / total[:, width:]
            mixed = (total[:, :width] * rden).astype(bf16)
            rden_ref[0, here, lanes] = rden
            mixed_ref[0, here, lanes] = mixed
            mixed_scr[here, column] = mixed

    @pl.when(lax.rem(step, steps) == steps - 1)
    def _():
        x1 = x_ref[0].astype(f32) + nn(mixed_scr[...], wout_ref[...])
        x1_ref[0] = x1
        xhat, _ = normed(x1)
        h2_ref[0] = (xhat * gains_ref[1:2, :]).astype(bf16)


def masked(made, causal, at, tile):
    last = jnp.where(causal, made[:, at * tile :], 0.0)
    if at > 0:
        last = jnp.concatenate([made[:, : at * tile], last], axis=1)
    return last.astype(bf16)


def mix_call(index, members, inputs, gains, w_out, phi_q, phi_k, qkv, carried, before, hd, after=()):
    batch, rows, model = inputs.shape
    width = 2 * hd
    pairs = model // width
    steps = pairs // PER
    states, at, count = carried
    heads = 2 * pairs
    feats = phi_q.shape[-1] // heads
    tile = min(256, rows)
    whole = pl.BlockSpec((1, rows, model), lambda g: (index + g // steps, 0, 0))
    narrow = pl.BlockSpec((1, rows, PER * width), lambda g: (index + g // steps, 0, lax.rem(g, steps)))
    phi_spec = pl.BlockSpec((1, rows, 2 * PER * feats), lambda g: (index + g // steps, 0, lax.rem(g, steps)))
    return stacked_call(
        functools.partial(mix_kernel, hd, len(states), at * pairs, count, tile),
        (members * steps,),
        [
            whole,
            const_block(gains.shape),
            const_block(w_out.shape),
            phi_spec,
            phi_spec,
            pl.BlockSpec((1, rows, PER * width), lambda g: (index + g // steps, 0, 2 * steps + lax.rem(g, steps))),
        ]
        + state_specs(carried, pairs, PER),
        [narrow, narrow, whole, whole],
        [
            jax.ShapeDtypeStruct((batch, rows, model), bf16),
            jax.ShapeDtypeStruct((batch, rows, model), f32),
            jax.ShapeDtypeStruct((batch, rows, model), f32),
            jax.ShapeDtypeStruct((batch, rows, model), bf16),
        ],
        (True,) * 4,
        before,
        (inputs, gains, w_out, phi_q, phi_k, qkv) + tuple(states),
        [pltpu.VMEM((rows, model), bf16)],
        cost(members * (heads * 2 * rows * rows * 512 + 2 * rows * model * model), members * 9 * MIB),
        after,
    )


def ffn_kernel(groups, batch, hd, *refs):
    h2_ref, gf_ref, wout_ref, gains_ref = refs[:4]
    late_any = refs[4:8]
    weights = refs[8 : 8 + groups]
    act_ref, pre_ref, g1_ref, ga_ref, gain_ref, side_ref, gstate_ref = refs[8 + groups : 15 + groups]
    up_scr, down_scr, pre_scr, x1_scr, mixed_scr, rden_scr, phiq_scr, sems, late_sems = refs[15 + groups :]
    step = pl.program_id(0)
    n_blocks = pl.num_programs(0) - batch
    each = n_blocks // groups
    block = act_ref.shape[-1]
    rows = h2_ref.shape[1]
    model = h2_ref.shape[2]
    shards, unit = up_scr.shape[1:3]
    taken = block // unit
    started = []
    for group in range(groups):
        started.append(pltpu.make_async_copy(weights[group].at[:, 0], up_scr.at[group], sems.at[2 * group]))
        started.append(pltpu.make_async_copy(weights[group].at[:, 1], down_scr.at[group], sems.at[2 * group + 1]))

    def late_copies(b):
        slot = lax.rem(b, 2)
        return [
            pltpu.make_async_copy(src.at[b], dst.at[slot], late_sems.at[slot, at])
            for at, (src, dst) in enumerate(zip(late_any, (x1_scr, mixed_scr, rden_scr, phiq_scr)))
        ]

    @pl.when(step == 0)
    def _():
        for copy in started:
            copy.start()

    @pl.when((step >= n_blocks - 1) & (step < n_blocks + batch - 1))
    def _():
        for copy in late_copies(step - n_blocks + 1):
            copy.start()

    for group in range(groups):

        @pl.when(step == group * each)
        def _():
            started[2 * group].wait()
            started[2 * group + 1].wait()

    @pl.when(step < n_blocks)
    def _():
        here = pl.ds(pl.multiple_of(lax.rem(step, each) * taken, taken), taken)
        up = up_scr[step // each, here].reshape(block, model)
        down = down_scr[step // each, here].reshape(block, model)
        cols = pl.ds(pl.multiple_of(step * block, block), block)
        for b in range(batch):
            pre = nt(h2_ref[b], up)
            part = 0.5 * lax.erf(pre * math.sqrt(0.5)) + 0.5
            act_ref[b] = (pre * part).astype(bf16)
            slope = part + pre * (
                jnp.exp2(pre * pre * (-0.5 * math.log2(math.e))) * (1.0 / math.sqrt(2.0 * math.pi))
            )
            grad_pre = (nt(gf_ref[b], down) * slope).astype(bf16)
            pre_ref[b] = grad_pre
            pre_scr[b, :, cols] = grad_pre

    @pl.when(step >= n_blocks)
    def _():
        b = step - n_blocks
        slot = lax.rem(b, 2)
        grad = nn(pre_scr[b], up_scr[...].reshape(n_blocks * block, model))
        for copy in late_copies(b):
            copy.wait()
        phiq = phiq_scr.at[slot]
        xhat, scale = normed(x1_scr[slot])
        g1 = gf_ref[b].astype(f32) + norm_back(grad, xhat, scale, gains_ref[1:2, :])
        g1_ref[0] = g1
        gain = jnp.sum(grad * xhat, axis=0, keepdims=True)

        @pl.when(b == 0)
        def _():
            gain_ref[...] = jnp.zeros_like(gain_ref)

        gain_ref[0:1] += gain
        ga = g1.astype(bf16)
        ga_ref[0] = ga
        gn_full = nt(ga, wout_ref[...]) * rden_scr[slot]
        gn_low = gn_full.astype(bf16)
        product = gn_full * mixed_scr[slot].astype(f32)
        high = product.astype(bf16)
        rest = (product - high.astype(f32)).astype(bf16)
        width = 2 * hd
        same = lax.div(lax.rem(lax.broadcasted_iota(jnp.int32, (2 * width, width), 0), width), hd) == lax.div(
            lax.broadcasted_iota(jnp.int32, (2 * width, width), 1), hd
        )
        minus = jnp.where(same, -1.0, 0.0).astype(bf16)
        inner = lax.rem(lanes_of((rows, width)), hd)
        feats = phiq.shape[-1] // (model // hd)
        sides = []
        for at in range(model // width):
            cols = slice(at * width, (at + 1) * width)
            gd = nn(jnp.concatenate([high[:, cols], rest[:, cols]], axis=1), minus)
            gd_high = gd.astype(bf16).astype(f32)
            gdx = jnp.where(inner == 0, gd_high, jnp.where(inner == 1, gd - gd_high, 0.0))
            sides.append(jnp.concatenate([gn_low[:, cols], gdx.astype(bf16)], axis=1))
        for at, side in enumerate(sides):
            side_ref[0, at] = side
        sums = [
            [tn(side, phiq[:, (2 * at + odd) * feats : (2 * at + odd + 1) * feats]) for odd in range(2)]
            for at, side in enumerate(sides)
        ]
        for at, (even, odd) in enumerate(sums):
            gstate_ref[at, 0:hd] = even[0:hd].astype(bf16)
            gstate_ref[at, hd:width] = odd[hd:width].astype(bf16)
            norms = jnp.concatenate(
                [
                    even[width : width + 1] + even[width + 1 : width + 2],
                    odd[width + hd : width + hd + 1] + odd[width + hd + 1 : width + hd + 2],
                    jnp.zeros((14, feats), f32),
                ],
                axis=0,
            )
            gstate_ref[at, width : width + 16] = norms.astype(bf16)


def ffn_call(h2, gf, x1, mixed, rden, phi_q, w_out, gains, weights, hd):
    batch, rows, model = h2.shape
    groups = len(weights)
    shards, _, unit, _ = weights[0].shape
    hidden = groups * shards * unit
    block = min(512, shards * unit)
    n_blocks = hidden // block
    pairs = model // (2 * hd)
    feats = phi_q.shape[-1] // (2 * pairs)
    n_rows = 2 * hd + 16
    here = lambda j: jnp.clip(j - n_blocks, 0, batch - 1)
    late = pl.BlockSpec((1, rows, model), lambda j: (here(j), 0, 0))
    wide = pl.BlockSpec((batch, rows, block), lambda j: (0, 0, jnp.minimum(j, n_blocks - 1)))
    scratch = (groups, shards, unit, model)
    return pl.pallas_call(
        functools.partial(ffn_kernel, groups, batch, hd),
        grid=(n_blocks + batch,),
        in_specs=[
            const_block(h2.shape),
            const_block(gf.shape),
            const_block(w_out.shape),
            const_block(gains.shape),
        ]
        + [pl.BlockSpec(memory_space=pl.ANY)] * (4 + groups),
        out_specs=[
            wide,
            wide,
            late,
            late,
            const_block((16, model)),
            pl.BlockSpec((1, pairs, rows, 4 * hd), lambda j: (here(j), 0, 0, 0)),
            pl.BlockSpec((pairs, n_rows, feats), lambda j: (here(j), 0, 0)),
        ],
        out_shape=[
            jax.ShapeDtypeStruct((batch, rows, hidden), bf16),
            jax.ShapeDtypeStruct((batch, rows, hidden), bf16),
            jax.ShapeDtypeStruct((batch, rows, model), f32),
            jax.ShapeDtypeStruct((batch, rows, model), bf16),
            jax.ShapeDtypeStruct((16, model), f32),
            jax.ShapeDtypeStruct((batch, pairs, rows, 4 * hd), bf16),
            jax.ShapeDtypeStruct((batch * pairs, n_rows, feats), bf16),
        ],
        scratch_shapes=[
            pltpu.VMEM(scratch, bf16),
            pltpu.VMEM(scratch, bf16),
            pltpu.VMEM((batch, rows, hidden), bf16),
            pltpu.VMEM((2, rows, model), f32),
            pltpu.VMEM((2, rows, model), bf16),
            pltpu.VMEM((2, rows, model), f32),
            pltpu.VMEM((2, rows, phi_q.shape[-1]), bf16),
            pltpu.SemaphoreType.DMA((2 * groups,)),
            pltpu.SemaphoreType.DMA((2, 4)),
        ],
        compiler_params=params(),
        cost_estimate=cost(6 * batch * rows * hidden * model, 30 * MIB, 2 * batch * rows * hidden),
    )(h2, gf, w_out, gains, x1, mixed, rden, phi_q, *weights)


def row_owner(far, y_bit, x_bit):
    seq = lax.axis_index("seq")
    y, x, core = lax.rem(lax.axis_index("dp"), 2), seq // 2, lax.rem(seq, 2)
    return (core ^ far) * 4 + (y ^ y_bit) * 2 + (x ^ x_bit)


def plane_of(far, first, second):
    turned = (lax.rem(lax.axis_index("seq"), 2) ^ far) == 1
    return jnp.where(turned, second, first), jnp.where(turned, first, second)


EXTRA = 16


def ffn_weight_kernel(n_pieces, n_after, *refs):
    act_ref, pre_ref, gf_ref, h2_ref, gain_ref, mixed_any, ga_any = refs[:7]
    outs = refs[7 + n_after : 9 + n_after]
    mixed_scr, ga_scr, sum_scr, row_scr, piece_scr, in_sems, row_sems, piece_sems = refs[9 + n_after :]
    step = pl.program_id(0)
    n_blocks = pl.num_programs(0)
    batch, rows, block = act_ref.shape
    model = gf_ref.shape[2]
    n_rows = row_scr.shape[1]
    unit = n_rows // 2 if not n_pieces else n_rows // 8
    slot = lax.rem(step, 2)
    copies = [
        pltpu.make_async_copy(mixed_any, mixed_scr, in_sems.at[0]),
        pltpu.make_async_copy(ga_any, ga_scr, in_sems.at[1]),
    ]

    def row_copy(out, row, slot):
        row = pl.multiple_of(row, 16)
        return pltpu.make_async_copy(row_scr.at[slot], out.at[pl.ds(row, n_rows)], row_sems.at[slot])

    @pl.when(step == 0)
    def _():
        for copy in copies:
            copy.start()

    down = tn(act_ref[...].reshape(batch * rows, block), gf_ref[...].reshape(batch * rows, model)).astype(bf16)
    up = tn(pre_ref[...].reshape(batch * rows, block), h2_ref[...].reshape(batch * rows, model)).astype(bf16)

    @pl.when(step >= 2)
    def _():
        row_copy(outs[0], 0, slot).wait()

    for at in range(block // unit):
        here = slice(at * unit, (at + 1) * unit)
        row_scr[slot, 2 * at * unit : (2 * at + 1) * unit] = up[here]
        row_scr[slot, (2 * at + 1) * unit : (2 * at + 2) * unit] = down[here]
    if n_pieces:
        half = n_blocks // 2
        quarter = n_blocks // 4
        held = outs[0].shape[0] // 2
        inside = lax.rem(step, half)
        row = (inside // quarter) * held + lax.rem(inside, quarter) * n_rows
        for at in range(2):

            @pl.when(step // half == at)
            def _():
                row_copy(outs[at], row, slot).start()
    else:
        row_copy(outs[0], step * n_rows, slot).start()

    def piece_copies():
        if not n_pieces:
            return [pltpu.make_async_copy(sum_scr, outs[1], piece_sems.at[0])]
        held = outs[0].shape[0] // 2
        n_piece = piece_scr.shape[1]
        return [
            pltpu.make_async_copy(
                piece_scr.at[2 * at + first],
                outs[at].at[(first + 1) * held - n_piece : (first + 1) * held],
                piece_sems.at[2 * at + first],
            )
            for at in range(2)
            for first in range(2)
        ]

    @pl.when(step == n_blocks // 2)
    def _():
        for copy in copies:
            copy.wait()
        sum_scr[...] = tn(
            mixed_scr[...].reshape(batch * rows, model), ga_scr[...].reshape(batch * rows, model)
        )
        if n_pieces:
            piece = model // 8
            gain = gain_ref[...].astype(bf16)
            for at in range(2):
                for first in range(2):
                    for second in range(2):
                        owner = row_owner(1 - at, *plane_of(1 - at, first, second))
                        taken = sum_scr[pl.ds(pl.multiple_of(owner * piece, piece), piece), :].astype(bf16)
                        row = second * (piece + EXTRA)
                        piece_scr[2 * at + first, row : row + piece] = taken
                        piece_scr[2 * at + first, row + piece : row + piece + EXTRA] = gain
        for copy in piece_copies():
            copy.start()

    @pl.when(step == n_blocks - 1)
    def _():
        row_copy(outs[0], 0, 1 - slot).wait()
        row_copy(outs[0], 0, slot).wait()
        for copy in piece_copies():
            copy.wait()


def ffn_weight_call(act, pre, gf, h2, gain, mixed, ga, unit, fast, after=()):
    batch, rows, model = h2.shape
    hidden = act.shape[-1]
    block = min(256, hidden)
    n_blocks = hidden // block
    wide = pl.BlockSpec((batch, rows, block), lambda j: (0, 0, j))
    n_piece = 2 * (model // 8 + EXTRA)
    if fast:
        out_shapes = [jax.ShapeDtypeStruct((hidden + 2 * n_piece, model), bf16)] * 2
    else:
        out_shapes = [jax.ShapeDtypeStruct((2 * hidden, model), bf16), jax.ShapeDtypeStruct((model, model), f32)]
    anywhere = pl.BlockSpec(memory_space=pl.ANY)
    return pl.pallas_call(
        functools.partial(ffn_weight_kernel, 8 if fast else 0, len(after)),
        grid=(n_blocks,),
        in_specs=[wide, wide, const_block(gf.shape), const_block(h2.shape), const_block(gain.shape), anywhere, anywhere]
        + [anywhere] * len(after),
        out_specs=[anywhere] * 2,
        out_shape=out_shapes,
        scratch_shapes=[
            pltpu.VMEM(mixed.shape, bf16),
            pltpu.VMEM(ga.shape, bf16),
            pltpu.VMEM((model, model), f32),
            pltpu.VMEM((2, 2 * block, model), bf16),
            pltpu.VMEM((4, n_piece, model), bf16),
            pltpu.SemaphoreType.DMA((2,)),
            pltpu.SemaphoreType.DMA((2,)),
            pltpu.SemaphoreType.DMA((4,)),
        ],
        compiler_params=params(),
        cost_estimate=cost(4 * batch * rows * hidden * model, 22 * MIB),
    )(act, pre, gf, h2, gain, mixed, ga, *in_hbm(after))


def attention_back_kernel(hd, n_prev, n_later, spots, tile, *refs):
    side_ref, phiq_ref, phik_ref, q_ref, k_ref, v_ref, omega_ref = refs[:7]
    prev_refs = refs[7 : 7 + n_prev]
    later_refs = refs[7 + n_prev : 7 + n_prev + n_later]
    (out_ref,) = refs[7 + n_prev + n_later :]
    step = pl.program_id(0)
    width = 2 * hd
    rows = q_ref.shape[1]
    feats = phiq_ref.shape[-1] // (2 * BACK_PER)
    tiles = rows // tile
    s = hd ** (-0.25)
    low = lanes_of((rows, width)) < hd
    low_tile = low[0:tile]
    inner = lax.rem(lanes_of((rows, width)), hd)
    ones = jnp.where(inner < 2, 1.0, 0.0)
    one = jnp.where(inner == 0, 1.0, 0.0).astype(bf16)
    causal = causal_tile(tile)
    spans = [(slice(t * tile, (t + 1) * tile), (t + 1) * tile) for t in range(tiles)]
    heads = [(at, odd) for at in range(BACK_PER) for odd in range(2)]
    each = [(at, odd, t) for at, odd in heads for t in range(tiles)]
    cols = {(at, odd): slice((2 * at + odd) * feats, (2 * at + odd + 1) * feats) for at, odd in heads}
    lanes = [slice(at * width, (at + 1) * width) for at in range(BACK_PER)]

    def column(made, at, odd, t):
        return jnp.concatenate([made[at, odd, i][:, t * tile : (t + 1) * tile] for i in range(t, tiles)], axis=0)

    made, scores, weights, value_sides = {}, {}, {}, {}
    for at in range(BACK_PER):
        values = v_ref[0, :, lanes[at]].astype(f32)
        value_sides[at, 0] = jnp.concatenate(
            [jnp.where(low, values, 0.0), jnp.where(low, ones, 0.0)], axis=1
        ).astype(bf16)
        value_sides[at, 1] = jnp.concatenate(
            [jnp.where(low, 0.0, values), jnp.where(low, 0.0, ones)], axis=1
        ).astype(bf16)
    for at, odd, t in each:
        here, end = spans[t]
        made[at, odd, t] = masked(nt(side_ref[0, at, here], value_sides[at, odd][0:end]), causal, t, tile)
    for at, odd, t in each:
        here, end = spans[t]
        scores[at, odd, t] = masked(
            nt(phiq_ref[0, here, cols[at, odd]], phik_ref[0, 0:end, cols[at, odd]]), causal, t, tile
        )
    prev = [state_block(prev_refs, False, at, step, BACK_PER, hd, *spots[0]) for at in range(BACK_PER)]
    later = [state_block(later_refs, True, at, step, BACK_PER, hd, *spots[1]) for at in range(BACK_PER)]
    for at, odd in heads:
        weights[at, odd] = feature_weights(omega_ref[2 * at + odd], odd)
    proj_q, proj_k = {}, {}
    for at, odd, t in each:
        here, end = spans[t]
        grad_phi = nn(side_ref[0, at, here], prev[at][odd]) + nn(made[at, odd, t], phik_ref[0, 0:end, cols[at, odd]])
        proj_q[at, odd, t] = (grad_phi * phiq_ref[0, here, cols[at, odd]].astype(f32)).astype(bf16)
    for at, odd, t in each:
        here = spans[t][0]
        beside = jnp.concatenate([v_ref[0, here, lanes[at]], one[here]], axis=1)
        grad_phi = nn(beside, later[at][odd]) + tn(column(made, at, odd, t), phiq_ref[0, t * tile :, cols[at, odd]])
        proj_k[at, odd, t] = (grad_phi * phik_ref[0, here, cols[at, odd]].astype(f32)).astype(bf16)
    back_q = {key: nt(proj_q[key], weights[key[:2]]) for key in each}
    back_k = {key: nt(proj_k[key], weights[key[:2]]) for key in each}
    for at in range(BACK_PER):
        both = jnp.concatenate([later[at][0][0:width], later[at][1][0:width]], axis=1)
        gn_pair = side_ref[0, at, :, 0:width].astype(f32)
        gn_sides = [jnp.where(low, gn_pair, 0.0).astype(bf16), jnp.where(low, 0.0, gn_pair).astype(bf16)]
        for t in range(tiles):
            here = spans[t][0]
            grad_v = nt(phik_ref[0, here, 2 * at * feats : 2 * (at + 1) * feats], both)
            for odd in range(2):
                grad_v = grad_v + tn(column(scores, at, odd, t), gn_sides[odd][t * tile :])
            out_ref[0, 2, here, lanes[at]] = grad_v.astype(bf16)
    for part, back, points_ref in ((0, back_q, q_ref), (1, back_k, k_ref)):
        for at in range(BACK_PER):
            for t in range(tiles):
                here = spans[t][0]
                even, odd = back[at, 0, t], back[at, 1, t]
                along = jnp.where(low_tile, even[:, :width], odd[:, :width])
                total = jnp.where(low_tile, even[:, width:], odd[:, width:])
                points = points_ref[0, here, lanes[at]].astype(f32)
                out_ref[0, part, here, lanes[at]] = (s * along + (s * s) * points * total).astype(bf16)


def attention_back_call(index, side, phi_q, phi_k, qkv, omega, carried, later, before, after=()):
    batch, pairs, rows, wide = side.shape
    heads, hd, feats = omega.shape
    steps = pairs // BACK_PER
    model = pairs * 2 * hd
    tile = min(256, rows)
    phi_spec = pl.BlockSpec((1, rows, 2 * BACK_PER * feats), lambda g: (index, 0, g))
    spots = tuple((at * pairs, count) for _, at, count in (carried, later))

    def part(n):
        return pl.BlockSpec((1, rows, 2 * BACK_PER * hd), lambda g: (index, 0, n * steps + g))

    return stacked_call(
        functools.partial(attention_back_kernel, hd, len(carried[0]), len(later[0]), spots, tile),
        (steps,),
        [
            pl.BlockSpec((1, BACK_PER, rows, wide), lambda g: (index, g, 0, 0)),
            phi_spec,
            phi_spec,
            part(0),
            part(1),
            part(2),
            pl.BlockSpec((2 * BACK_PER, hd, feats), lambda g: (g, 0, 0)),
        ]
        + state_specs(carried, pairs, BACK_PER)
        + state_specs(later, pairs, BACK_PER),
        [pl.BlockSpec((1, 3, rows, 2 * BACK_PER * hd), lambda g: (index, 0, 0, g))],
        [jax.ShapeDtypeStruct((batch, 3, rows, model), bf16)],
        (True,),
        before,
        (side, phi_q, phi_k, qkv, qkv, qkv, omega) + tuple(carried[0]) + tuple(later[0]),
        [],
        cost(heads * 2 * rows * (rows * 1024 + 6 * 65536), 12 * MIB),
        after,
    )


def qkv_weight_kernel(fast, n_after, *refs):
    h1_ref, grad_ref = refs[:2]
    outs = refs[2 + n_after :]
    batch, rows, model = h1_ref.shape
    total = tn(h1_ref[...].reshape(batch * rows, model), grad_ref[...].reshape(batch * rows, model))
    if not fast:
        outs[0][...] = total
        return
    far_ref, *near_refs, sum_scr = outs
    sum_scr[...] = total
    piece = model // 8
    for far in range(2):
        for plane in range(4):
            owner = row_owner(far, plane // 2, plane % 2)
            taken = sum_scr[pl.ds(pl.multiple_of(owner * piece, piece), piece), :].astype(bf16)
            if far:
                far_ref[plane, 0] = taken
            else:
                near_refs[plane][0] = taken


def qkv_weight_call(h1, grads, fast, after=()):
    batch, rows, model = h1.shape
    if fast:
        out_specs = [pl.BlockSpec((4, 1, model // 8, model), lambda p: (0, p, 0, 0))]
        out_shapes = [jax.ShapeDtypeStruct((4, 3, model // 8, model), bf16)]
        out_specs += [pl.BlockSpec((1, model // 8, model), lambda p: (p, 0, 0))] * 4
        out_shapes += [jax.ShapeDtypeStruct((3, model // 8, model), bf16)] * 4
    else:
        out_specs = [pl.BlockSpec((model, model), lambda p: (0, p))]
        out_shapes = [jax.ShapeDtypeStruct((model, 3 * model), f32)]
    return pl.pallas_call(
        functools.partial(qkv_weight_kernel, fast, len(after)),
        grid=(3,),
        in_specs=[const_block(h1.shape), pl.BlockSpec((batch, 1, rows, model), lambda p: (0, p, 0, 0))]
        + [pl.BlockSpec(memory_space=pl.ANY)] * len(after),
        out_specs=out_specs,
        out_shape=out_shapes,
        scratch_shapes=[pltpu.VMEM((model, model), f32)] if fast else [],
        compiler_params=params(),
        cost_estimate=cost(6 * batch * rows * model * model, 8 * MIB),
    )(h1, grads, *in_hbm(after))


def inputs_back_kernel(grads_ref, w_ref, x_ref, g1_ref, gains_ref, grad_ref):
    model = x_ref.shape[2]
    grad = nt(grads_ref[0, 0], w_ref[:, :model])
    for part in (1, 2):
        grad = grad + nt(grads_ref[0, part], w_ref[:, part * model : (part + 1) * model])
    xhat, scale = normed(x_ref[0].astype(f32))
    grad_ref[0] = g1_ref[0] + norm_back(grad, xhat, scale, gains_ref[0:1, :])


def inputs_back_call(index, grads, w_qkv, inputs, g1, gains, before, after=()):
    batch, rows, model = inputs.shape
    whole = pl.BlockSpec((1, rows, model), lambda j: (index, 0, 0))
    return stacked_call(
        inputs_back_kernel,
        (1,),
        [
            pl.BlockSpec((1, 3, rows, model), lambda j: (index, 0, 0, 0)),
            const_block(w_qkv.shape),
            whole,
            whole,
            const_block(gains.shape),
        ],
        [whole],
        [jax.ShapeDtypeStruct((batch, rows, model), f32)],
        (True,),
        before,
        (grads, w_qkv, inputs, g1, gains),
        [],
        cost(6 * rows * model * model, 6 * MIB),
        after,
    )


def outputs_kernel(groups, *refs):
    act_ref, x1_ref = refs[:2]
    weights = refs[2 : 2 + groups]
    out_ref, down_scr, sems = refs[2 + groups :]
    copies = [
        pltpu.make_async_copy(weights[group].at[:, 1], down_scr.at[group], sems.at[group]) for group in range(groups)
    ]
    for copy in copies:
        copy.start()
    for copy in copies:
        copy.wait()
    down = down_scr[...].reshape(act_ref.shape[2], x1_ref.shape[2])
    out_ref[0] = (x1_ref[0] + nn(act_ref[0], down)).astype(bf16)


def outputs_call(index, act, x1, weights, before, after=()):
    batch, rows, model = x1.shape
    hidden = act.shape[2]
    groups = len(weights)
    shards, _, unit, _ = weights[0].shape
    one = lambda j: (index, 0, 0)
    return stacked_call(
        functools.partial(outputs_kernel, groups),
        (1,),
        [pl.BlockSpec((1, rows, hidden), one), pl.BlockSpec((1, rows, model), one)]
        + [pl.BlockSpec(memory_space=pl.ANY)] * groups,
        [pl.BlockSpec((1, rows, model), one)],
        [jax.ShapeDtypeStruct((batch, rows, model), bf16)],
        (True,),
        before,
        (act, x1) + tuple(weights),
        [pltpu.VMEM((groups, shards, unit, model), bf16), pltpu.SemaphoreType.DMA((groups,))],
        cost(2 * rows * model * hidden, 6 * MIB),
        after,
    )


CORE = (1, 1)
GATHER = ((16, 8), (8, 16), (2, 4), (4, 2))
PLANE = ((2, 2), (4, 4), (6, 6))
LINE = ((16, 8), (8, 16))


def swap(array, masks):
    return lax.ppermute(array, AXES, [(i, i ^ masks[i & 1]) for i in range(32)])


def gate(array, *deps):
    anywhere = pl.BlockSpec(memory_space=pltpu.HBM)
    return pl.pallas_call(
        lambda *refs: None,
        in_specs=[anywhere] * (1 + len(deps)),
        out_specs=anywhere,
        out_shape=jax.ShapeDtypeStruct(array.shape, array.dtype),
        input_output_aliases={0: 0},
    )(*in_hbm((array,) + deps))


def all_states(local, backward):
    everything = lax.all_gather(local, "seq").astype(f32)
    count, place = lax.axis_size("seq"), lax.axis_index("seq")
    at = jnp.arange(count)
    wanted = (at > place) if backward else (at < place)
    total = jnp.sum(jnp.where(wanted[:, None, None, None], everything, 0.0), axis=0)
    return (total.astype(bf16),)


def chip_half(local, near):
    core = lax.rem(lax.axis_index("seq"), 2)
    half = local.shape[0] // 2
    low, high = [
        (local[rows].astype(f32) + near[rows].astype(f32)).astype(bf16) for rows in (slice(0, half), slice(half, None))
    ]
    return jnp.where(core == 0, low, high)


def sums_kernel(n_terms, plan, *refs):
    terms, outs = refs[:n_terms], refs[n_terms:]
    for out, pieces in zip(outs, plan):
        to = 0
        for names, first, size in pieces:
            total = terms[names[0]][first : first + size].astype(f32)
            for name in names[1:]:
                total = total + terms[name][first : first + size].astype(f32)
            out[to : to + size] = total.astype(out.dtype)
            to += size


def sums(terms, plan, kinds=None):
    model = terms[0].shape[-1]
    kinds = kinds or [bf16] * len(plan)
    shapes = [
        jax.ShapeDtypeStruct((sum(size for _, _, size in pieces), model), kind)
        for pieces, kind in zip(plan, kinds)
    ]
    return pl.pallas_call(
        functools.partial(sums_kernel, len(terms), plan),
        out_shape=shapes,
        compiler_params=params(),
        cost_estimate=cost(sum(t.size for t in terms), 3 * sum(t.size for t in terms)),
    )(*terms)


def split_kernel(near_ref, got_ref, low_ref, high_ref):
    for at, out_ref in enumerate((low_ref, high_ref)):
        out_ref[...] = (near_ref[at].astype(f32) + got_ref[at].astype(f32)).astype(bf16)


def split_sum(near, got):
    rows, model = near.shape
    half = rows // 2
    block = half // 2
    both = pl.BlockSpec((2, block, model), lambda i: (0, i, 0))
    one = pl.BlockSpec((block, model), lambda i: (i, 0))
    return pl.pallas_call(
        split_kernel,
        grid=(2,),
        in_specs=[both, both],
        out_specs=[one, one],
        out_shape=[jax.ShapeDtypeStruct((half, model), bf16)] * 2,
        compiler_params=params(),
        cost_estimate=cost(near.size, 6 * near.size),
    )(near.reshape(2, half, model), got.reshape(2, half, model))


def along_x(mine):
    return swap(mine, (2, 2))


def assemble_kernel(*refs):
    pieces = refs[:8]
    wqkv_ref, gains_ref, gw_ref, gwout_ref, ggain_ref = refs[8:]
    model = gwout_ref.shape[0]
    rows = model // 8
    for far in range(2):
        for plane in range(4):
            owner = row_owner(far, plane // 2, plane % 2)
            at = pl.ds(pl.multiple_of(owner * rows, rows), rows)
            piece = pieces[4 * far + plane]
            for part in range(3):
                gw_ref[at, part * model : (part + 1) * model] = piece[part * rows : (part + 1) * rows].astype(f32)
            gwout_ref[at, :] = piece[3 * rows : 4 * rows].astype(f32)

            @pl.when(owner == 0)
            def _():
                ggain_ref[1:2, :] = piece[4 * rows : 4 * rows + EXTRA].astype(f32)[0:1]

    ggain_ref[0:1, :] = first_gain(gw_ref, wqkv_ref, gains_ref)


def first_gain(gw_ref, wqkv_ref, gains_ref):
    along = jnp.sum(gw_ref[...] * wqkv_ref[...].astype(f32), axis=1, keepdims=True)
    return jnp.broadcast_to(along, (along.shape[0], 128)).T[0:1, :] / gains_ref[0:1, :]


def assemble_call(pieces, w_qkv, gains):
    model = w_qkv.shape[0]
    return pl.pallas_call(
        assemble_kernel,
        out_shape=[
            jax.ShapeDtypeStruct(w_qkv.shape, f32),
            jax.ShapeDtypeStruct((model, model), f32),
            jax.ShapeDtypeStruct(gains.shape, f32),
        ],
        compiler_params=params(),
    )(*pieces, w_qkv, gains)


def gains_kernel(gw_ref, gain_ref, wqkv_ref, gains_ref, ggain_ref):
    ggain_ref[0:1, :] = first_gain(gw_ref, wqkv_ref, gains_ref)
    ggain_ref[1:2, :] = gain_ref[0:1, :]


def plane_kernel(far_ref, *refs):
    for at in range(4):
        refs[4 + at][...] = (far_ref[at].astype(f32) + refs[at][...].astype(f32)).astype(bf16)


def plane_sums(far, near):
    return pl.pallas_call(
        plane_kernel,
        out_shape=[jax.ShapeDtypeStruct(a.shape, bf16) for a in near],
        compiler_params=params(),
        cost_estimate=cost(far.size, 6 * far.size),
    )(far, *near)


def next_halves(low, got, n_shard, shards, whole_pieces):
    cut = shards * n_shard
    n_pieces = low.shape[0] - cut
    pieces = [(cut, n_pieces)] * 2 if whole_pieces else [(cut, n_pieces // 2), (cut + n_pieces // 2, n_pieces // 2)]
    return sums(
        [low, got],
        [[((0, 1), at * cut // 2, cut // 2), ((0, 1),) + pieces[at]] for at in range(2)],
    )


def planned(inputs, gains, w_qkv, w_out, shard, omega, cotangent):
    batch, rows, model = inputs.shape
    heads, hd, _ = omega.shape
    pairs = heads // 2
    n_shard, n_piece = 2 * shard.shape[1], model // 8 + EXTRA

    held = shard[None]
    got = swap(held, GATHER[0])
    made = features_call(0, 0, 2, inputs, gains, w_qkv, omega, None)
    held = jnp.concatenate([held, gate(got, made[0])])
    got = swap(held, GATHER[1])
    made = features_call(1, 1, 2, inputs, gains, w_qkv, omega, made, (held,))
    got = gate(got, made[0])
    local = gate(made[4], got)
    near = swap(local, CORE)
    mine = chip_half(local, near)
    held = jnp.concatenate([held, got])
    got = swap(held, GATHER[2])
    far = along_x(mine)
    made = features_call(2, 0, 1, inputs, gains, w_qkv, omega, made, (held, mine))
    far, got = gate(far, made[0]), gate(got, made[0])
    first = (near, far, swap(far, CORE))
    local = gate(made[4], far, got)
    near = swap(local, CORE)
    mine = chip_half(local, near)
    held = jnp.concatenate([held, got])
    got = swap(held, GATHER[3])
    far = along_x(mine)
    beside = swap(held, CORE)
    qkv, phi_q, phi_k, h1 = made[:4]
    made = mix_call(
        0, 2, inputs, gains, w_out, phi_q, phi_k, qkv, (first, 0, 2 * pairs), None, hd, (held, mine)
    )
    far = gate(far, made[0])
    got, beside = gate(got, far), gate(beside, far)
    second = (near, far, swap(far, CORE))
    made = mix_call(
        2, 1, inputs, gains, w_out, phi_q, phi_k, qkv, (second, 0, pairs), made, hd, (got,)
    )
    weights = [beside, gate(swap(got, CORE), made[0]), held, got]
    mixed, rden, x1, h2 = made
    carried = [(first, 0, 2 * pairs), (first, 1, 2 * pairs), (second, 0, pairs)]

    act, pre, g1, ga, gain, side, local = ffn_call(
        h2, cotangent, x1, mixed, rden, phi_q, w_out, gains, weights, hd
    )
    near = swap(local, CORE)
    mine = chip_half(local, near)
    far = along_x(mine)
    send, low = ffn_weight_call(act, pre, cotangent, h2, gain, mixed, ga, n_shard // 2, True, (mine,))
    far = gate(far, low)
    other = swap(far, CORE)
    send = gate(send, other)
    later = (near, far, other)

    def back(b, before, *after):
        return attention_back_call(
            b, side, phi_q, phi_k, qkv, omega, carried[b], (later, b, batch * pairs), before, after
        )

    def into(b, before, *after):
        return inputs_back_call(b, grads, w_qkv, inputs, g1, gains, before, after)

    def onto(b, before, *after):
        return outputs_call(b, act, x1, weights, before, after)

    got = swap(send, CORE)
    made = back(0, None)
    got = gate(got, made[0])
    low, high = split_sum(low, got)
    got = swap(high, GATHER[3])
    made = back(1, made, high)
    onto_made = onto(0, None, made[0])
    low, high = next_halves(low, gate(got, onto_made[0]), n_shard, 8, False)
    got = swap(high, GATHER[2])
    made = back(2, made, high)
    low, high = next_halves(low, gate(got, made[0]), n_shard, 4, True)
    got = swap(high, GATHER[1])
    (grads,) = made
    late = qkv_weight_call(h1, grads, True, (high,))

    send, *keep = [a.reshape(a.shape[:-3] + (-1, model)) for a in late]
    far = swap(send, CORE)
    into_made = into(0, None, *keep)
    got, far = gate(got, into_made[0]), gate(far, into_made[0])
    keep = plane_sums(far, keep)
    far = [swap(keep[plane], PLANE[plane - 1]) for plane in (1, 2, 3)]
    low, high = next_halves(low, got, n_shard, 2, True)
    got = swap(high, GATHER[0])
    into_made = into(1, into_made, high, *keep)
    got = gate(got, into_made[0])
    n_late = keep[0].shape[0]
    far = [gate(a, into_made[0]) for a in far]
    keep, grad_ffn, piece = sums(
        [keep[0]] + far + [low, got],
        [[((0, 1, 2, 3), 0, n_late)], [((4, 5), 0, n_shard)], [((4, 5), n_shard, n_piece)]],
        [bf16, f32, bf16],
    )
    got = swap(keep, LINE[0])
    into_made = into(2, into_made, keep)
    (keep,) = sums([keep, gate(got, into_made[0])], [[((0, 1), 0, n_late)]])
    got = swap(keep, LINE[1])
    onto_made = onto(1, onto_made, keep)
    (keep,) = sums(
        [keep, gate(got, onto_made[0]), piece], [[((0, 1), 0, n_late), ((2,), 0, n_piece)]]
    )
    got = [swap(keep, masks) for masks in PLANE]
    beside = swap(keep, CORE)
    onto_made = onto(2, onto_made, keep)
    near = [keep] + [gate(a, onto_made[0]) for a in got]
    far = [gate(beside, onto_made[0])] + [swap(a, CORE) for a in near[1:]]
    grad_wqkv, grad_wout, grad_gains = assemble_call(near + far, w_qkv, gains)
    return onto_made[0], into_made[0], grad_gains, grad_wqkv, grad_wout, grad_ffn


def plain(inputs, gains, w_qkv, w_out, shard, omega, cotangent):
    batch, rows, model = inputs.shape
    heads, hd, _ = omega.shape
    pairs = heads // 2
    pair = lax.all_gather(shard, AXES, axis=1, tiled=True)
    hidden = pair.shape[1]
    unit = min(256, hidden)
    weights = [jnp.swapaxes(pair.reshape(2, hidden // unit, unit, model), 0, 1)]
    made = None
    for b in range(batch):
        made = features_call(b, b, batch, inputs, gains, w_qkv, omega, made)
    qkv, phi_q, phi_k, h1, local = made
    sums = all_states(local, False)
    mixed, rden, x1, h2 = mix_call(
        0, batch, inputs, gains, w_out, phi_q, phi_k, qkv, (sums, 0, batch * pairs), None, hd
    )
    act, pre, g1, ga, gain, side, local = ffn_call(
        h2, cotangent, x1, mixed, rden, phi_q, w_out, gains, weights, hd
    )
    later = all_states(local, True)
    both, grad_wout = ffn_weight_call(act, pre, cotangent, h2, gain, mixed, ga, unit, False)
    both = jnp.swapaxes(both.reshape(-1, 2, unit, model), 0, 1).reshape(2, -1, model)
    grad_ffn = lax.psum_scatter(both, AXES, scatter_dimension=1, tiled=True).astype(f32)
    made = None
    for b in range(batch):
        spot = (b, batch * pairs)
        made = attention_back_call(b, side, phi_q, phi_k, qkv, omega, (sums,) + spot, (later,) + spot, made)
    (grads,) = made
    (grad_wqkv,) = qkv_weight_call(h1, grads, False)
    into_made = onto_made = None
    for b in range(batch):
        into_made = inputs_back_call(b, grads, w_qkv, inputs, g1, gains, into_made)
        onto_made = outputs_call(b, act, x1, weights, onto_made)
    grad_wqkv, grad_wout, gain = lax.psum((grad_wqkv, grad_wout, gain), AXES)
    grad_gains = pl.pallas_call(
        gains_kernel,
        out_shape=jax.ShapeDtypeStruct(gains.shape, f32),
        compiler_params=params(),
    )(grad_wqkv, gain, w_qkv, gains)
    return onto_made[0], into_made[0], grad_gains, grad_wqkv, grad_wout, grad_ffn


def on_device(inputs, gains, w_qkv, w_out, ffn_weight, omega, cotangent):
    fast = lax.axis_size("dp") == 8 and lax.axis_size("seq") == 4 and inputs.shape[0] == 3
    outputs, grad_inputs, *grads = (planned if fast else plain)(
        inputs, gains[0], w_qkv[0], w_out[0], ffn_weight[0], jnp.swapaxes(omega[0], 1, 2), cotangent
    )
    grad_gains, grad_wqkv, grad_wout, grad_ffn = grads
    grad_ffn = grad_ffn.reshape(ffn_weight.shape)
    return (outputs, grad_inputs, grad_gains[None], grad_wqkv[None], grad_wout[None], grad_ffn)


def solution(mesh):
    in_specs = (
        P("dp", "seq", None),
        P(),
        P(),
        P(),
        P(None, None, ("dp", "seq"), None),
        P(),
        P("dp", "seq", None),
    )
    out_specs = (
        P("dp", "seq", None),
        P("dp", "seq", None),
        P(),
        P(),
        P(),
        P(None, None, ("dp", "seq"), None),
    )
    return jax.shard_map(
        on_device, mesh=mesh, in_specs=in_specs, out_specs=out_specs, check_vma=False
    )
```

```python
import functools
import math

import jax
import jax.numpy as jnp
from jax import lax
from jax.experimental import pallas as pl
from jax.experimental.pallas import tpu as pltpu
from jax.sharding import PartitionSpec as P

epsilon = 1e-05
bf16 = jnp.bfloat16
f32 = jnp.float32
AXES = ("dp", "seq")
MIB = 2**20


def nn(a, b):
    return lax.dot_general(a, b, (((1,), (0,)), ((), ())), preferred_element_type=f32)


def nt(a, b):
    return lax.dot_general(a, b, (((1,), (1,)), ((), ())), preferred_element_type=f32)


def tn(a, b):
    return lax.dot_general(a, b, (((0,), (0,)), ((), ())), preferred_element_type=f32)


def lanes_of(shape):
    return lax.broadcasted_iota(jnp.int32, shape, len(shape) - 1)


def params(mib=62):
    return pltpu.CompilerParams(vmem_limit_bytes=mib * MIB)


def cost(flops, nbytes, trans=0):
    return pl.CostEstimate(flops=int(flops), bytes_accessed=int(nbytes), transcendentals=int(trans))


def in_hbm(arrays):
    return [pltpu.with_memory_space_constraint(a, pltpu.HBM) for a in arrays]


def in_vmem(arrays):
    return [pltpu.with_memory_space_constraint(a, pltpu.VMEM) for a in arrays]


def const_block(shape):
    return pl.BlockSpec(shape, lambda *_: (0,) * len(shape))


def stacked_call(kernel, grid, in_specs, out_specs, out_shapes, stacked, before, args, scratch, estimate, after=(), mib=62):
    n_in = len(args)
    aliases = {}
    extra = list(after)
    if before is not None:
        for at, (flag, buffer) in enumerate(zip(stacked, before)):
            if flag:
                aliases[n_in + len(extra)] = at
                extra += in_hbm((buffer,))
    n_extra = len(extra)

    def body(*refs):
        kernel(*refs[:n_in], *refs[n_in + n_extra :])

    return pl.pallas_call(
        body,
        grid=grid,
        in_specs=list(in_specs) + [pl.BlockSpec(memory_space=pl.ANY)] * n_extra,
        out_specs=out_specs,
        out_shape=out_shapes,
        scratch_shapes=scratch,
        input_output_aliases=aliases,
        compiler_params=params(mib),
        cost_estimate=estimate,
    )(*args, *extra)


def normed(values):
    center = values - jnp.mean(values, axis=-1, keepdims=True)
    spread = jnp.mean(center * center, axis=-1, keepdims=True)
    scale = lax.rsqrt(spread + epsilon)
    return center * scale, scale


def norm_back(grad, xhat, scale, gain):
    gy = grad * gain
    return scale * (
        gy - jnp.mean(gy, axis=-1, keepdims=True) - xhat * jnp.mean(gy * xhat, axis=-1, keepdims=True)
    )


def causal_tile(rows):
    return lax.broadcasted_iota(jnp.int32, (rows, rows), 0) >= lax.broadcasted_iota(
        jnp.int32, (rows, rows), 1
    )


def feature_weights(omega, odd):
    ones = jnp.full(omega.shape, -1.0, omega.dtype)
    zeros = jnp.zeros_like(ones)
    parts = [ones, omega, zeros, ones] if odd else [omega, ones, ones, zeros]
    return jnp.concatenate(parts, axis=0)


PER = 2
BACK_PER = 1


def features_kernel(hd, x_ref, gains_ref, w_ref, omega_ref, qkv_ref, phiq_ref, phik_ref, h1_ref, state_ref, qkv_scr):
    step = pl.program_id(0)
    width = 2 * hd
    rows, model = x_ref.shape[1:]
    s = hd ** (-0.25)
    feats = omega_ref.shape[2]
    per = omega_ref.shape[0] // 2

    @pl.when(step == 0)
    def _():
        xhat, _ = normed(x_ref[0].astype(f32))
        hidden = (xhat * gains_ref[0:1, :]).astype(bf16)
        h1_ref[0] = hidden
        for part in range(3):
            cols = slice(part * model, (part + 1) * model)
            made = nn(hidden, w_ref[:, cols]).astype(bf16)
            qkv_ref[0, :, cols] = made
            qkv_scr[part] = made

    low = lanes_of((rows, width)) < hd
    lefts = []
    for at in range(per):
        column = pl.ds(pl.multiple_of((step * per + at) * width, width), width)
        for part in range(2):
            points = qkv_scr[part, :, column].astype(f32)
            energy = points * points * (0.5 * s)
            high = energy.astype(bf16).astype(f32)
            rest = (energy - high).astype(bf16)
            turned = pltpu.roll(high, hd, 1)
            for odd in range(2):
                first = jnp.where(low, turned, points) if odd else jnp.where(low, points, turned)
                lefts.append((at, part, odd, jnp.concatenate([first.astype(bf16), rest], axis=1)))
    made = {}
    for at, part, odd, left in lefts:
        proj = nn(left, feature_weights(omega_ref[2 * at + odd], odd))
        phi = jnp.exp2(proj * (s * math.log2(math.e)) - 0.5 * math.log2(feats)).astype(bf16)
        head = 2 * at + odd
        (phik_ref if part else phiq_ref)[0, :, head * feats : (head + 1) * feats] = phi
        if part:
            made[at, odd] = phi
    for at in range(per):
        column = pl.ds(pl.multiple_of((step * per + at) * width, width), width)
        values = qkv_scr[2, :, column]
        state_ref[at, 0:hd, :] = tn(values, made[at, 0])[0:hd].astype(bf16)
        state_ref[at, hd:width, :] = tn(values, made[at, 1])[hd:width].astype(bf16)
        sums = jnp.concatenate(
            [
                jnp.sum(made[at, 0].astype(f32), axis=0, keepdims=True),
                jnp.sum(made[at, 1].astype(f32), axis=0, keepdims=True),
                jnp.zeros((14, feats), f32),
            ],
            axis=0,
        )
        state_ref[at, width : width + 16, :] = sums.astype(bf16)


def features_call(index, at, count, inputs, gains, w_qkv, omega, before, after=()):
    batch, rows, model = inputs.shape
    heads, hd, feats = omega.shape
    pairs = heads // 2
    per = pairs
    steps = pairs // per
    n_rows = 2 * hd + 16
    phi_spec = pl.BlockSpec((1, rows, 2 * per * feats), lambda g: (index, 0, g))
    return stacked_call(
        functools.partial(features_kernel, hd),
        (steps,),
        [
            pl.BlockSpec((1, rows, model), lambda g: (index, 0, 0)),
            const_block(gains.shape),
            const_block(w_qkv.shape),
            pl.BlockSpec((2 * per, hd, feats), lambda g: (g, 0, 0)),
        ],
        [
            pl.BlockSpec((1, rows, 3 * model), lambda g: (index, 0, 0)),
            phi_spec,
            phi_spec,
            pl.BlockSpec((1, rows, model), lambda g: (index, 0, 0)),
            pl.BlockSpec((per, n_rows, feats), lambda g: (at * steps + g, 0, 0)),
        ],
        [
            jax.ShapeDtypeStruct((batch, rows, 3 * model), bf16),
            jax.ShapeDtypeStruct((batch, rows, heads * feats), bf16),
            jax.ShapeDtypeStruct((batch, rows, heads * feats), bf16),
            jax.ShapeDtypeStruct((batch, rows, model), bf16),
            jax.ShapeDtypeStruct((count * pairs, n_rows, feats), bf16),
        ],
        (True, True, True, True, at > 0),
        before,
        (inputs, gains, w_qkv, omega),
        [pltpu.VMEM((3, rows, model), bf16)],
        cost(2 * rows * model * 3 * model + 4 * heads * rows * 256 * feats, 9 * MIB, 2 * rows * heads * feats),
        after,
    )


def state_block(state_refs, backward, at, step, per, hd, first, count):
    if len(state_refs) == 1:
        total = state_refs[0][at].astype(f32)
    else:
        near, got, other = state_refs
        seq = lax.axis_index("seq")
        core = lax.rem(seq, 2)
        own_half = (first + step * per + at) // (count // 2) == core
        beyond = (seq // 2) == (0 if backward else 1)
        beside = core == (0 if backward else 1)
        total = jnp.where(own_half, got[at].astype(f32), other[at].astype(f32))
        total = jnp.where(beyond, total, 0.0) + jnp.where(beside, near[at].astype(f32), 0.0)
    feats = total.shape[-1]
    width = 2 * hd
    zeros = jnp.zeros((hd, feats), bf16)
    low = total.astype(bf16)
    even_norm = jnp.broadcast_to(total[width : width + 1], (hd, feats)).astype(bf16)
    odd_norm = jnp.broadcast_to(total[width + 1 : width + 2], (hd, feats)).astype(bf16)
    even = jnp.concatenate([low[0:hd], zeros, even_norm, zeros], axis=0)
    odd = jnp.concatenate([zeros, low[hd:width], zeros, odd_norm], axis=0)
    return even, odd


def state_specs(carried, pairs, per):
    states, at, count = carried
    shape = (per,) + states[0].shape[1:]
    first = at * pairs // per
    specs = [pl.BlockSpec(shape, lambda g: (first + g, 0, 0))]
    if len(states) > 1:
        specs += [pl.BlockSpec(shape, lambda g: (lax.rem(first + g, count // 2 // per), 0, 0))] * 2
    return specs


def mix_kernel(hd, n_states, first, count, tile, *refs):
    x_ref, gains_ref, wout_ref, phiq_ref, phik_ref, v_ref = refs[:6]
    state_refs = refs[6 : 6 + n_states]
    mixed_ref, rden_ref, x1_ref, h2_ref, mixed_scr = refs[6 + n_states :]
    step = pl.program_id(0)
    width = 2 * hd
    rows, model = x_ref.shape[1:]
    steps = model // width // PER
    feats = phiq_ref.shape[-1] // (2 * PER)
    causal = causal_tile(tile)
    low = lanes_of((rows, width)) < hd
    ones = jnp.where(low, 1.0, 0.0)
    spans = [(slice(at * tile, (at + 1) * tile), (at + 1) * tile) for at in range(rows // tile)]
    scores = {}
    for at in range(PER):
        for odd in range(2):
            cols = slice((2 * at + odd) * feats, (2 * at + odd + 1) * feats)
            for t, (here, end) in enumerate(spans):
                scores[at, odd, t] = masked(nt(phiq_ref[0, here, cols], phik_ref[0, 0:end, cols]), causal, t, tile)
    for at in range(PER):
        even, odd = state_block(state_refs, False, at, step, PER, hd, first, count)
        both_state = jnp.concatenate([even, odd], axis=1)
        values = v_ref[0, :, at * width : (at + 1) * width].astype(f32)
        sides = [
            jnp.concatenate([jnp.where(low, values, 0.0), ones], axis=1).astype(bf16),
            jnp.concatenate([jnp.where(low, 0.0, values), 1.0 - ones], axis=1).astype(bf16),
        ]
        cols = slice(2 * at * feats, 2 * (at + 1) * feats)
        lanes = slice(at * width, (at + 1) * width)
        column = pl.ds(pl.multiple_of((lax.rem(step, steps) * PER + at) * width, width), width)
        for t, (here, end) in enumerate(spans):
            total = nt(phiq_ref[0, here, cols], both_state)
            for odd in range(2):
                total = total + nn(scores[at, odd, t], sides[odd][0:end])
            rden = 1.0 / total[:, width:]
            mixed = (total[:, :width] * rden).astype(bf16)
            rden_ref[0, here, lanes] = rden
            mixed_ref[0, here, lanes] = mixed
            mixed_scr[here, column] = mixed

    @pl.when(lax.rem(step, steps) == steps - 1)
    def _():
        x1 = x_ref[0].astype(f32) + nn(mixed_scr[...], wout_ref[...])
        x1_ref[0] = x1
        xhat, _ = normed(x1)
        h2_ref[0] = (xhat * gains_ref[1:2, :]).astype(bf16)


def masked(made, causal, at, tile):
    last = jnp.where(causal, made[:, at * tile :], 0.0)
    if at > 0:
        last = jnp.concatenate([made[:, : at * tile], last], axis=1)
    return last.astype(bf16)


def mix_call(index, members, inputs, gains, w_out, phi_q, phi_k, qkv, carried, before, hd, after=()):
    batch, rows, model = inputs.shape
    width = 2 * hd
    pairs = model // width
    steps = pairs // PER
    states, at, count = carried
    heads = 2 * pairs
    feats = phi_q.shape[-1] // heads
    tile = min(256, rows)
    whole = pl.BlockSpec((1, rows, model), lambda g: (index + g // steps, 0, 0))
    narrow = pl.BlockSpec((1, rows, PER * width), lambda g: (index + g // steps, 0, lax.rem(g, steps)))
    phi_spec = pl.BlockSpec((1, rows, 2 * PER * feats), lambda g: (index + g // steps, 0, lax.rem(g, steps)))
    return stacked_call(
        functools.partial(mix_kernel, hd, len(states), at * pairs, count, tile),
        (members * steps,),
        [
            whole,
            const_block(gains.shape),
            const_block(w_out.shape),
            phi_spec,
            phi_spec,
            pl.BlockSpec((1, rows, PER * width), lambda g: (index + g // steps, 0, 2 * steps + lax.rem(g, steps))),
        ]
        + state_specs(carried, pairs, PER),
        [narrow, narrow, whole, whole],
        [
            jax.ShapeDtypeStruct((batch, rows, model), bf16),
            jax.ShapeDtypeStruct((batch, rows, model), f32),
            jax.ShapeDtypeStruct((batch, rows, model), f32),
            jax.ShapeDtypeStruct((batch, rows, model), bf16),
        ],
        (True,) * 4,
        before,
        (inputs, gains, w_out, phi_q, phi_k, qkv) + tuple(states),
        [pltpu.VMEM((rows, model), bf16)],
        cost(members * (heads * 2 * rows * rows * 512 + 2 * rows * model * model), members * 9 * MIB),
        after,
    )


def ffn_kernel(groups, batch, hd, *refs):
    h2_ref, gf_ref, wout_ref, gains_ref = refs[:4]
    late_any = refs[4:8]
    weights = refs[8 : 8 + groups]
    act_ref, pre_ref, g1_ref, ga_ref, gain_ref, side_ref, gstate_ref = refs[8 + groups : 15 + groups]
    up_scr, down_scr, pre_scr, x1_scr, mixed_scr, rden_scr, phiq_scr, sems, late_sems = refs[15 + groups :]
    step = pl.program_id(0)
    n_blocks = pl.num_programs(0) - batch
    each = n_blocks // groups
    block = act_ref.shape[-1]
    rows = h2_ref.shape[1]
    model = h2_ref.shape[2]
    shards, unit = up_scr.shape[1:3]
    taken = block // unit
    started = []
    for group in range(groups):
        started.append(pltpu.make_async_copy(weights[group].at[:, 0], up_scr.at[group], sems.at[2 * group]))
        started.append(pltpu.make_async_copy(weights[group].at[:, 1], down_scr.at[group], sems.at[2 * group + 1]))

    def late_copies(b):
        slot = lax.rem(b, 2)
        return [
            pltpu.make_async_copy(src.at[b], dst.at[slot], late_sems.at[slot, at])
            for at, (src, dst) in enumerate(zip(late_any, (x1_scr, mixed_scr, rden_scr, phiq_scr)))
        ]

    @pl.when(step == 0)
    def _():
        for copy in started:
            copy.start()

    @pl.when((step >= n_blocks - 1) & (step < n_blocks + batch - 1))
    def _():
        for copy in late_copies(step - n_blocks + 1):
            copy.start()

    for group in range(groups):

        @pl.when(step == group * each)
        def _():
            started[2 * group].wait()
            started[2 * group + 1].wait()

    @pl.when(step < n_blocks)
    def _():
        here = pl.ds(pl.multiple_of(lax.rem(step, each) * taken, taken), taken)
        up = up_scr[step // each, here].reshape(block, model)
        down = down_scr[step // each, here].reshape(block, model)
        cols = pl.ds(pl.multiple_of(step * block, block), block)
        for b in range(batch):
            pre = nt(h2_ref[b], up)
            part = 0.5 * lax.erf(pre * math.sqrt(0.5)) + 0.5
            act_ref[b] = (pre * part).astype(bf16)
            slope = part + pre * (
                jnp.exp2(pre * pre * (-0.5 * math.log2(math.e))) * (1.0 / math.sqrt(2.0 * math.pi))
            )
            grad_pre = (nt(gf_ref[b], down) * slope).astype(bf16)
            pre_ref[b] = grad_pre
            pre_scr[b, :, cols] = grad_pre

    @pl.when(step >= n_blocks)
    def _():
        b = step - n_blocks
        slot = lax.rem(b, 2)
        grad = nn(pre_scr[b], up_scr[...].reshape(n_blocks * block, model))
        for copy in late_copies(b):
            copy.wait()
        phiq = phiq_scr.at[slot]
        xhat, scale = normed(x1_scr[slot])
        g1 = gf_ref[b].astype(f32) + norm_back(grad, xhat, scale, gains_ref[1:2, :])
        g1_ref[0] = g1
        gain = jnp.sum(grad * xhat, axis=0, keepdims=True)

        @pl.when(b == 0)
        def _():
            gain_ref[...] = jnp.zeros_like(gain_ref)

        gain_ref[0:1] += gain
        ga = g1.astype(bf16)
        ga_ref[0] = ga
        gn_full = nt(ga, wout_ref[...]) * rden_scr[slot]
        gn_low = gn_full.astype(bf16)
        product = gn_full * mixed_scr[slot].astype(f32)
        high = product.astype(bf16)
        rest = (product - high.astype(f32)).astype(bf16)
        width = 2 * hd
        same = lax.div(lax.rem(lax.broadcasted_iota(jnp.int32, (2 * width, width), 0), width), hd) == lax.div(
            lax.broadcasted_iota(jnp.int32, (2 * width, width), 1), hd
        )
        minus = jnp.where(same, -1.0, 0.0).astype(bf16)
        inner = lax.rem(lanes_of((rows, width)), hd)
        feats = phiq.shape[-1] // (model // hd)
        sides = []
        for at in range(model // width):
            cols = slice(at * width, (at + 1) * width)
            gd = nn(jnp.concatenate([high[:, cols], rest[:, cols]], axis=1), minus)
            gd_high = gd.astype(bf16).astype(f32)
            gdx = jnp.where(inner == 0, gd_high, jnp.where(inner == 1, gd - gd_high, 0.0))
            sides.append(jnp.concatenate([gn_low[:, cols], gdx.astype(bf16)], axis=1))
        for at, side in enumerate(sides):
            side_ref[0, at] = side
        sums = [
            [tn(side, phiq[:, (2 * at + odd) * feats : (2 * at + odd + 1) * feats]) for odd in range(2)]
            for at, side in enumerate(sides)
        ]
        for at, (even, odd) in enumerate(sums):
            gstate_ref[at, 0:hd] = even[0:hd].astype(bf16)
            gstate_ref[at, hd:width] = odd[hd:width].astype(bf16)
            norms = jnp.concatenate(
                [
                    even[width : width + 1] + even[width + 1 : width + 2],
                    odd[width + hd : width + hd + 1] + odd[width + hd + 1 : width + hd + 2],
                    jnp.zeros((14, feats), f32),
                ],
                axis=0,
            )
            gstate_ref[at, width : width + 16] = norms.astype(bf16)


def ffn_call(h2, gf, x1, mixed, rden, phi_q, w_out, gains, weights, hd):
    batch, rows, model = h2.shape
    groups = len(weights)
    shards, _, unit, _ = weights[0].shape
    hidden = groups * shards * unit
    block = min(512, shards * unit)
    n_blocks = hidden // block
    pairs = model // (2 * hd)
    feats = phi_q.shape[-1] // (2 * pairs)
    n_rows = 2 * hd + 16
    here = lambda j: jnp.clip(j - n_blocks, 0, batch - 1)
    late = pl.BlockSpec((1, rows, model), lambda j: (here(j), 0, 0))
    wide = pl.BlockSpec((batch, rows, block), lambda j: (0, 0, jnp.minimum(j, n_blocks - 1)))
    scratch = (groups, shards, unit, model)
    return pl.pallas_call(
        functools.partial(ffn_kernel, groups, batch, hd),
        grid=(n_blocks + batch,),
        in_specs=[
            const_block(h2.shape),
            const_block(gf.shape),
            const_block(w_out.shape),
            const_block(gains.shape),
        ]
        + [pl.BlockSpec(memory_space=pl.ANY)] * (4 + groups),
        out_specs=[
            wide,
            wide,
            late,
            late,
            const_block((16, model)),
            pl.BlockSpec((1, pairs, rows, 4 * hd), lambda j: (here(j), 0, 0, 0)),
            pl.BlockSpec((pairs, n_rows, feats), lambda j: (here(j), 0, 0)),
        ],
        out_shape=[
            jax.ShapeDtypeStruct((batch, rows, hidden), bf16),
            jax.ShapeDtypeStruct((batch, rows, hidden), bf16),
            jax.ShapeDtypeStruct((batch, rows, model), f32),
            jax.ShapeDtypeStruct((batch, rows, model), bf16),
            jax.ShapeDtypeStruct((16, model), f32),
            jax.ShapeDtypeStruct((batch, pairs, rows, 4 * hd), bf16),
            jax.ShapeDtypeStruct((batch * pairs, n_rows, feats), bf16),
        ],
        scratch_shapes=[
            pltpu.VMEM(scratch, bf16),
            pltpu.VMEM(scratch, bf16),
            pltpu.VMEM((batch, rows, hidden), bf16),
            pltpu.VMEM((2, rows, model), f32),
            pltpu.VMEM((2, rows, model), bf16),
            pltpu.VMEM((2, rows, model), f32),
            pltpu.VMEM((2, rows, phi_q.shape[-1]), bf16),
            pltpu.SemaphoreType.DMA((2 * groups,)),
            pltpu.SemaphoreType.DMA((2, 4)),
        ],
        compiler_params=params(),
        cost_estimate=cost(6 * batch * rows * hidden * model, 30 * MIB, 2 * batch * rows * hidden),
    )(h2, gf, w_out, gains, x1, mixed, rden, phi_q, *weights)


def row_owner(far, y_bit, x_bit):
    seq = lax.axis_index("seq")
    y, x, core = lax.rem(lax.axis_index("dp"), 2), seq // 2, lax.rem(seq, 2)
    return (core ^ far) * 4 + (y ^ y_bit) * 2 + (x ^ x_bit)


def plane_of(far, first, second):
    turned = (lax.rem(lax.axis_index("seq"), 2) ^ far) == 1
    return jnp.where(turned, second, first), jnp.where(turned, first, second)


EXTRA = 16


def ffn_weight_kernel(unit, n_pieces, n_after, *refs):
    act_ref, pre_ref, gf_ref, h2_ref, gain_ref, mixed_any, ga_any = refs[:7]
    outs = refs[7 + n_after : 9 + n_after]
    mixed_scr, ga_scr, sum_scr, row_scr, piece_scr, in_sems, row_sems, piece_sems = refs[9 + n_after :]
    step = pl.program_id(0)
    n_blocks = pl.num_programs(0)
    batch, rows, block = act_ref.shape
    model = gf_ref.shape[2]
    n_rows = row_scr.shape[1]
    slot = lax.rem(step, 2)
    copies = [
        pltpu.make_async_copy(mixed_any, mixed_scr, in_sems.at[0]),
        pltpu.make_async_copy(ga_any, ga_scr, in_sems.at[1]),
    ]

    def row_copy(out, row, slot):
        row = pl.multiple_of(row, 16)
        return pltpu.make_async_copy(row_scr.at[slot], out.at[pl.ds(row, n_rows)], row_sems.at[slot])

    @pl.when(step == 0)
    def _():
        for copy in copies:
            copy.start()

    down = tn(act_ref[...].reshape(batch * rows, block), gf_ref[...].reshape(batch * rows, model)).astype(bf16)
    up = tn(pre_ref[...].reshape(batch * rows, block), h2_ref[...].reshape(batch * rows, model)).astype(bf16)

    @pl.when(step >= 2)
    def _():
        row_copy(outs[0], 0, slot).wait()

    for at in range(block // unit):
        here = slice(at * unit, (at + 1) * unit)
        row_scr[slot, 2 * at * unit : (2 * at + 1) * unit] = up[here]
        row_scr[slot, (2 * at + 1) * unit : (2 * at + 2) * unit] = down[here]
    if n_pieces:
        half = n_blocks // 2
        quarter = n_blocks // 4
        held = outs[0].shape[0] // 2
        inside = lax.rem(step, half)
        row = (inside // quarter) * held + lax.rem(inside, quarter) * n_rows
        for at in range(2):

            @pl.when(step // half == at)
            def _():
                row_copy(outs[at], row, slot).start()
    else:
        row_copy(outs[0], step * n_rows, slot).start()

    def piece_copies():
        if not n_pieces:
            return [pltpu.make_async_copy(sum_scr, outs[1], piece_sems.at[0])]
        held = outs[0].shape[0] // 2
        n_piece = piece_scr.shape[1]
        return [
            pltpu.make_async_copy(
                piece_scr.at[2 * at + first],
                outs[at].at[(first + 1) * held - n_piece : (first + 1) * held],
                piece_sems.at[2 * at + first],
            )
            for at in range(2)
            for first in range(2)
        ]

    @pl.when(step == n_blocks // 2)
    def _():
        for copy in copies:
            copy.wait()
        sum_scr[...] = tn(
            mixed_scr[...].reshape(batch * rows, model), ga_scr[...].reshape(batch * rows, model)
        )
        if n_pieces:
            piece = model // 8
            gain = gain_ref[...].astype(bf16)
            for at in range(2):
                for first in range(2):
                    for second in range(2):
                        owner = row_owner(1 - at, *plane_of(1 - at, first, second))
                        taken = sum_scr[pl.ds(pl.multiple_of(owner * piece, piece), piece), :].astype(bf16)
                        row = second * (piece + EXTRA)
                        piece_scr[2 * at + first, row : row + piece] = taken
                        piece_scr[2 * at + first, row + piece : row + piece + EXTRA] = gain
        for copy in piece_copies():
            copy.start()

    @pl.when(step == n_blocks - 1)
    def _():
        row_copy(outs[0], 0, 1 - slot).wait()
        row_copy(outs[0], 0, slot).wait()
        for copy in piece_copies():
            copy.wait()


def ffn_weight_call(act, pre, gf, h2, gain, mixed, ga, unit, fast, after=()):
    batch, rows, model = h2.shape
    hidden = act.shape[-1]
    block = min(512, hidden)
    n_blocks = hidden // block
    wide = pl.BlockSpec((batch, rows, block), lambda j: (0, 0, j))
    n_piece = 2 * (model // 8 + EXTRA)
    if fast:
        out_shapes = [jax.ShapeDtypeStruct((hidden + 2 * n_piece, model), bf16)] * 2
    else:
        out_shapes = [jax.ShapeDtypeStruct((2 * hidden, model), bf16), jax.ShapeDtypeStruct((model, model), f32)]
    anywhere = pl.BlockSpec(memory_space=pl.ANY)
    return pl.pallas_call(
        functools.partial(ffn_weight_kernel, unit, 8 if fast else 0, len(after)),
        grid=(n_blocks,),
        in_specs=[wide, wide, const_block(gf.shape), const_block(h2.shape), const_block(gain.shape), anywhere, anywhere]
        + [anywhere] * len(after),
        out_specs=[anywhere] * 2,
        out_shape=out_shapes,
        scratch_shapes=[
            pltpu.VMEM(mixed.shape, bf16),
            pltpu.VMEM(ga.shape, bf16),
            pltpu.VMEM((model, model), f32),
            pltpu.VMEM((2, 2 * block, model), bf16),
            pltpu.VMEM((4, n_piece, model), bf16),
            pltpu.SemaphoreType.DMA((2,)),
            pltpu.SemaphoreType.DMA((2,)),
            pltpu.SemaphoreType.DMA((4,)),
        ],
        compiler_params=params(),
        cost_estimate=cost(4 * batch * rows * hidden * model, 22 * MIB),
    )(act, pre, gf, h2, gain, mixed, ga, *in_hbm(after))


def attention_back_kernel(hd, n_prev, n_later, spots, tile, *refs):
    side_ref, phiq_ref, phik_ref, q_ref, k_ref, v_ref, omega_ref = refs[:7]
    prev_refs = refs[7 : 7 + n_prev]
    later_refs = refs[7 + n_prev : 7 + n_prev + n_later]
    (out_ref,) = refs[7 + n_prev + n_later :]
    step = pl.program_id(0)
    width = 2 * hd
    rows = q_ref.shape[1]
    feats = phiq_ref.shape[-1] // (2 * BACK_PER)
    tiles = rows // tile
    s = hd ** (-0.25)
    low = lanes_of((rows, width)) < hd
    low_tile = low[0:tile]
    inner = lax.rem(lanes_of((rows, width)), hd)
    ones = jnp.where(inner < 2, 1.0, 0.0)
    one = jnp.where(inner == 0, 1.0, 0.0).astype(bf16)
    causal = causal_tile(tile)
    spans = [(slice(t * tile, (t + 1) * tile), (t + 1) * tile) for t in range(tiles)]
    heads = [(at, odd) for at in range(BACK_PER) for odd in range(2)]
    each = [(at, odd, t) for at, odd in heads for t in range(tiles)]
    cols = {(at, odd): slice((2 * at + odd) * feats, (2 * at + odd + 1) * feats) for at, odd in heads}
    lanes = [slice(at * width, (at + 1) * width) for at in range(BACK_PER)]

    def column(made, at, odd, t):
        return jnp.concatenate([made[at, odd, i][:, t * tile : (t + 1) * tile] for i in range(t, tiles)], axis=0)

    made, scores, weights, value_sides = {}, {}, {}, {}
    for at in range(BACK_PER):
        values = v_ref[0, :, lanes[at]].astype(f32)
        value_sides[at, 0] = jnp.concatenate(
            [jnp.where(low, values, 0.0), jnp.where(low, ones, 0.0)], axis=1
        ).astype(bf16)
        value_sides[at, 1] = jnp.concatenate(
            [jnp.where(low, 0.0, values), jnp.where(low, 0.0, ones)], axis=1
        ).astype(bf16)
    for at, odd, t in each:
        here, end = spans[t]
        made[at, odd, t] = masked(nt(side_ref[0, at, here], value_sides[at, odd][0:end]), causal, t, tile)
    for at, odd, t in each:
        here, end = spans[t]
        scores[at, odd, t] = masked(
            nt(phiq_ref[0, here, cols[at, odd]], phik_ref[0, 0:end, cols[at, odd]]), causal, t, tile
        )
    prev = [state_block(prev_refs, False, at, step, BACK_PER, hd, *spots[0]) for at in range(BACK_PER)]
    later = [state_block(later_refs, True, at, step, BACK_PER, hd, *spots[1]) for at in range(BACK_PER)]
    for at, odd in heads:
        weights[at, odd] = feature_weights(omega_ref[2 * at + odd], odd)
    proj_q, proj_k = {}, {}
    for at, odd, t in each:
        here, end = spans[t]
        grad_phi = nn(side_ref[0, at, here], prev[at][odd]) + nn(made[at, odd, t], phik_ref[0, 0:end, cols[at, odd]])
        proj_q[at, odd, t] = (grad_phi * phiq_ref[0, here, cols[at, odd]].astype(f32)).astype(bf16)
    for at, odd, t in each:
        here = spans[t][0]
        beside = jnp.concatenate([v_ref[0, here, lanes[at]], one[here]], axis=1)
        grad_phi = nn(beside, later[at][odd]) + tn(column(made, at, odd, t), phiq_ref[0, t * tile :, cols[at, odd]])
        proj_k[at, odd, t] = (grad_phi * phik_ref[0, here, cols[at, odd]].astype(f32)).astype(bf16)
    back_q = {key: nt(proj_q[key], weights[key[:2]]) for key in each}
    back_k = {key: nt(proj_k[key], weights[key[:2]]) for key in each}
    for at in range(BACK_PER):
        both = jnp.concatenate([later[at][0][0:width], later[at][1][0:width]], axis=1)
        gn_pair = side_ref[0, at, :, 0:width].astype(f32)
        gn_sides = [jnp.where(low, gn_pair, 0.0).astype(bf16), jnp.where(low, 0.0, gn_pair).astype(bf16)]
        for t in range(tiles):
            here = spans[t][0]
            grad_v = nt(phik_ref[0, here, 2 * at * feats : 2 * (at + 1) * feats], both)
            for odd in range(2):
                grad_v = grad_v + tn(column(scores, at, odd, t), gn_sides[odd][t * tile :])
            out_ref[0, 2, here, lanes[at]] = grad_v.astype(bf16)
    for part, back, points_ref in ((0, back_q, q_ref), (1, back_k, k_ref)):
        for at in range(BACK_PER):
            for t in range(tiles):
                here = spans[t][0]
                even, odd = back[at, 0, t], back[at, 1, t]
                along = jnp.where(low_tile, even[:, :width], odd[:, :width])
                total = jnp.where(low_tile, even[:, width:], odd[:, width:])
                points = points_ref[0, here, lanes[at]].astype(f32)
                out_ref[0, part, here, lanes[at]] = (s * along + (s * s) * points * total).astype(bf16)


def attention_back_call(index, side, phi_q, phi_k, qkv, omega, carried, later, before, after=()):
    batch, pairs, rows, wide = side.shape
    heads, hd, feats = omega.shape
    steps = pairs // BACK_PER
    model = pairs * 2 * hd
    tile = min(256, rows)
    phi_spec = pl.BlockSpec((1, rows, 2 * BACK_PER * feats), lambda g: (index, 0, g))
    spots = tuple((at * pairs, count) for _, at, count in (carried, later))

    def part(n):
        return pl.BlockSpec((1, rows, 2 * BACK_PER * hd), lambda g: (index, 0, n * steps + g))

    return stacked_call(
        functools.partial(attention_back_kernel, hd, len(carried[0]), len(later[0]), spots, tile),
        (steps,),
        [
            pl.BlockSpec((1, BACK_PER, rows, wide), lambda g: (index, g, 0, 0)),
            phi_spec,
            phi_spec,
            part(0),
            part(1),
            part(2),
            pl.BlockSpec((2 * BACK_PER, hd, feats), lambda g: (g, 0, 0)),
        ]
        + state_specs(carried, pairs, BACK_PER)
        + state_specs(later, pairs, BACK_PER),
        [pl.BlockSpec((1, 3, rows, 2 * BACK_PER * hd), lambda g: (index, 0, 0, g))],
        [jax.ShapeDtypeStruct((batch, 3, rows, model), bf16)],
        (True,),
        before,
        (side, phi_q, phi_k, qkv, qkv, qkv, omega) + tuple(carried[0]) + tuple(later[0]),
        [],
        cost(heads * 2 * rows * (rows * 1024 + 6 * 65536), 12 * MIB),
        after,
    )


def qkv_weight_kernel(fast, n_after, *refs):
    h1_ref, grad_ref = refs[:2]
    outs = refs[2 + n_after :]
    batch, rows, model = h1_ref.shape
    total = tn(h1_ref[...].reshape(batch * rows, model), grad_ref[...].reshape(batch * rows, model))
    if not fast:
        outs[0][...] = total
        return
    far_ref, *near_refs, sum_scr = outs
    sum_scr[...] = total
    piece = model // 8
    for far in range(2):
        for plane in range(4):
            owner = row_owner(far, plane // 2, plane % 2)
            taken = sum_scr[pl.ds(pl.multiple_of(owner * piece, piece), piece), :].astype(bf16)
            if far:
                far_ref[plane, 0] = taken
            else:
                near_refs[plane][0] = taken


def qkv_weight_call(h1, grads, fast, after=()):
    batch, rows, model = h1.shape
    if fast:
        out_specs = [pl.BlockSpec((4, 1, model // 8, model), lambda p: (0, p, 0, 0))]
        out_shapes = [jax.ShapeDtypeStruct((4, 3, model // 8, model), bf16)]
        out_specs += [pl.BlockSpec((1, model // 8, model), lambda p: (p, 0, 0))] * 4
        out_shapes += [jax.ShapeDtypeStruct((3, model // 8, model), bf16)] * 4
    else:
        out_specs = [pl.BlockSpec((model, model), lambda p: (0, p))]
        out_shapes = [jax.ShapeDtypeStruct((model, 3 * model), f32)]
    return pl.pallas_call(
        functools.partial(qkv_weight_kernel, fast, len(after)),
        grid=(3,),
        in_specs=[const_block(h1.shape), pl.BlockSpec((batch, 1, rows, model), lambda p: (0, p, 0, 0))]
        + [pl.BlockSpec(memory_space=pl.ANY)] * len(after),
        out_specs=out_specs,
        out_shape=out_shapes,
        scratch_shapes=[pltpu.VMEM((model, model), f32)] if fast else [],
        compiler_params=params(),
        cost_estimate=cost(6 * batch * rows * model * model, 8 * MIB),
    )(h1, grads, *in_hbm(after))


def inputs_back_kernel(grads_ref, w_ref, x_ref, g1_ref, gains_ref, grad_ref):
    model = x_ref.shape[2]
    grad = nt(grads_ref[0, 0], w_ref[:, :model])
    for part in (1, 2):
        grad = grad + nt(grads_ref[0, part], w_ref[:, part * model : (part + 1) * model])
    xhat, scale = normed(x_ref[0].astype(f32))
    grad_ref[0] = g1_ref[0] + norm_back(grad, xhat, scale, gains_ref[0:1, :])


def inputs_back_call(index, grads, w_qkv, inputs, g1, gains, before, after=()):
    batch, rows, model = inputs.shape
    whole = pl.BlockSpec((1, rows, model), lambda j: (index, 0, 0))
    return stacked_call(
        inputs_back_kernel,
        (1,),
        [
            pl.BlockSpec((1, 3, rows, model), lambda j: (index, 0, 0, 0)),
            const_block(w_qkv.shape),
            whole,
            whole,
            const_block(gains.shape),
        ],
        [whole],
        [jax.ShapeDtypeStruct((batch, rows, model), f32)],
        (True,),
        before,
        (grads, w_qkv, inputs, g1, gains),
        [],
        cost(6 * rows * model * model, 6 * MIB),
        after,
        62,
    )


def outputs_kernel(groups, *refs):
    act_ref, x1_ref = refs[:2]
    weights = refs[2 : 2 + groups]
    out_ref, down_scr, sems = refs[2 + groups :]
    copies = [
        pltpu.make_async_copy(weights[group].at[:, 1], down_scr.at[group], sems.at[group]) for group in range(groups)
    ]
    for copy in copies:
        copy.start()
    for copy in copies:
        copy.wait()
    down = down_scr[...].reshape(act_ref.shape[2], x1_ref.shape[2])
    out_ref[0] = (x1_ref[0] + nn(act_ref[0], down)).astype(bf16)


def outputs_call(index, act, x1, weights, before, after=()):
    batch, rows, model = x1.shape
    hidden = act.shape[2]
    groups = len(weights)
    shards, _, unit, _ = weights[0].shape
    one = lambda j: (index, 0, 0)
    return stacked_call(
        functools.partial(outputs_kernel, groups),
        (1,),
        [pl.BlockSpec((1, rows, hidden), one), pl.BlockSpec((1, rows, model), one)]
        + [pl.BlockSpec(memory_space=pl.ANY)] * groups,
        [pl.BlockSpec((1, rows, model), one)],
        [jax.ShapeDtypeStruct((batch, rows, model), bf16)],
        (True,),
        before,
        (act, x1) + tuple(weights),
        [pltpu.VMEM((groups, shards, unit, model), bf16), pltpu.SemaphoreType.DMA((groups,))],
        cost(2 * rows * model * hidden, 6 * MIB),
        after,
        62,
    )


CORE = (1, 1)
GATHER = ((16, 8), (8, 16), (2, 4), (4, 2))
PLANE = ((2, 2), (4, 4), (6, 6))
LINE = ((16, 8), (8, 16))


def swap(array, masks):
    return lax.ppermute(array, AXES, [(i, i ^ masks[i & 1]) for i in range(32)])


def small(array, kib):
    return array.size * array.dtype.itemsize <= kib * 1024


def gate(array, *deps, close=False):
    anywhere = pl.BlockSpec(memory_space=pl.ANY)
    return pl.pallas_call(
        lambda *refs: None,
        in_specs=[anywhere] * (1 + len(deps)),
        out_specs=anywhere,
        out_shape=jax.ShapeDtypeStruct(array.shape, array.dtype),
        input_output_aliases={0: 0},
    )(*(in_vmem if close or small(array, 400) else in_hbm)((array,)), *in_hbm(deps))


def all_states(local, backward):
    everything = lax.all_gather(local, "seq").astype(f32)
    count, place = lax.axis_size("seq"), lax.axis_index("seq")
    at = jnp.arange(count)
    wanted = (at > place) if backward else (at < place)
    total = jnp.sum(jnp.where(wanted[:, None, None, None], everything, 0.0), axis=0)
    return (total.astype(bf16),)


def chip_half(local, near):
    core = lax.rem(lax.axis_index("seq"), 2)
    half = local.shape[0] // 2
    low, high = [
        (local[rows].astype(f32) + near[rows].astype(f32)).astype(bf16) for rows in (slice(0, half), slice(half, None))
    ]
    return jnp.where(core == 0, low, high)


def sums_kernel(n_terms, plan, *refs):
    terms, outs = refs[:n_terms], refs[n_terms:]
    for out, pieces in zip(outs, plan):
        to = 0
        for names, first, size in pieces:
            total = terms[names[0]][first : first + size].astype(f32)
            for name in names[1:]:
                total = total + terms[name][first : first + size].astype(f32)
            out[to : to + size] = total.astype(out.dtype)
            to += size


def sums(terms, plan, kinds=None, close=()):
    model = terms[0].shape[-1]
    kinds = kinds or [bf16] * len(plan)
    shapes = [
        jax.ShapeDtypeStruct((sum(size for _, _, size in pieces), model), kind)
        for pieces, kind in zip(plan, kinds)
    ]
    return pl.pallas_call(
        functools.partial(sums_kernel, len(terms), plan),
        out_shape=shapes,
        compiler_params=params(),
        cost_estimate=cost(sum(t.size for t in terms), 3 * sum(t.size for t in terms)),
    )(*[in_vmem((t,))[0] if at in close else t for at, t in enumerate(terms)])


def split_kernel(near_ref, got_ref, low_ref, high_ref):
    for at, out_ref in enumerate((low_ref, high_ref)):
        out_ref[...] = (near_ref[at].astype(f32) + got_ref[at].astype(f32)).astype(bf16)


def split_sum(near, got):
    rows, model = near.shape
    half = rows // 2
    block = half // 2
    both = pl.BlockSpec((2, block, model), lambda i: (0, i, 0))
    one = pl.BlockSpec((block, model), lambda i: (i, 0))
    return pl.pallas_call(
        split_kernel,
        grid=(2,),
        in_specs=[both, both],
        out_specs=[one, one],
        out_shape=[jax.ShapeDtypeStruct((half, model), bf16)] * 2,
        compiler_params=params(),
        cost_estimate=cost(near.size, 6 * near.size),
    )(near.reshape(2, half, model), got.reshape(2, half, model))


def along_x(mine):
    return swap(mine, (2, 2))


def assemble_kernel(*refs):
    pieces = refs[:8]
    wqkv_ref, gains_ref, gw_ref, gwout_ref, ggain_ref = refs[8:]
    model = gwout_ref.shape[0]
    rows = model // 8
    for far in range(2):
        for plane in range(4):
            owner = row_owner(far, plane // 2, plane % 2)
            at = pl.ds(pl.multiple_of(owner * rows, rows), rows)
            piece = pieces[4 * far + plane]
            for part in range(3):
                gw_ref[at, part * model : (part + 1) * model] = piece[part * rows : (part + 1) * rows].astype(f32)
            gwout_ref[at, :] = piece[3 * rows : 4 * rows].astype(f32)

            @pl.when(owner == 0)
            def _():
                ggain_ref[1:2, :] = piece[4 * rows : 4 * rows + EXTRA].astype(f32)[0:1]

    ggain_ref[0:1, :] = first_gain(gw_ref, wqkv_ref, gains_ref)


def first_gain(gw_ref, wqkv_ref, gains_ref):
    along = jnp.sum(gw_ref[...] * wqkv_ref[...].astype(f32), axis=1, keepdims=True)
    return jnp.broadcast_to(along, (along.shape[0], 128)).T[0:1, :] / gains_ref[0:1, :]


def assemble_call(pieces, w_qkv, gains):
    model = w_qkv.shape[0]
    return pl.pallas_call(
        assemble_kernel,
        out_shape=[
            jax.ShapeDtypeStruct(w_qkv.shape, f32),
            jax.ShapeDtypeStruct((model, model), f32),
            jax.ShapeDtypeStruct(gains.shape, f32),
        ],
        compiler_params=params(40),
    )(*in_vmem(pieces), w_qkv, gains)


def gains_kernel(gw_ref, gain_ref, wqkv_ref, gains_ref, ggain_ref):
    ggain_ref[0:1, :] = first_gain(gw_ref, wqkv_ref, gains_ref)
    ggain_ref[1:2, :] = gain_ref[0:1, :]


def plane_kernel(far_ref, *refs):
    for at in range(4):
        refs[4 + at][...] = (far_ref[at].astype(f32) + refs[at][...].astype(f32)).astype(bf16)


def plane_sums(far, near):
    return pl.pallas_call(
        plane_kernel,
        out_shape=[jax.ShapeDtypeStruct(a.shape, bf16) for a in near],
        compiler_params=params(),
        cost_estimate=cost(far.size, 6 * far.size),
    )(*in_vmem((far,)), *near)


def next_halves(low, got, n_shard, shards, whole_pieces):
    cut = shards * n_shard
    n_pieces = low.shape[0] - cut
    pieces = [(cut, n_pieces)] * 2 if whole_pieces else [(cut, n_pieces // 2), (cut + n_pieces // 2, n_pieces // 2)]
    return sums(
        [low, got],
        [[((0, 1), at * cut // 2, cut // 2), ((0, 1),) + pieces[at]] for at in range(2)],
        None,
        (1,) if small(got, 400) else (),
    )


def planned(inputs, gains, w_qkv, w_out, shard, omega, cotangent):
    batch, rows, model = inputs.shape
    heads, hd, _ = omega.shape
    pairs = heads // 2
    n_shard, n_piece = 2 * shard.shape[1], model // 8 + EXTRA

    held = shard[None]
    got = swap(held, GATHER[0])
    made = features_call(0, 0, 2, inputs, gains, w_qkv, omega, None)
    held = jnp.concatenate([held, gate(got, made[0])])
    got = swap(held, GATHER[1])
    made = features_call(1, 1, 2, inputs, gains, w_qkv, omega, made, in_vmem((held,)))
    got = gate(got, made[0])
    local = gate(made[4], got)
    near = swap(local, CORE)
    mine = chip_half(local, near)
    held = jnp.concatenate([held, got])
    got = swap(held, GATHER[2])
    far = along_x(mine)
    made = features_call(2, 0, 1, inputs, gains, w_qkv, omega, made, in_hbm((held,)) + in_vmem((mine,)))
    far, got = gate(far, made[0]), gate(got, made[0])
    first = (near, far, swap(far, CORE))
    local = gate(made[4], far, got)
    near = swap(local, CORE)
    mine = chip_half(local, near)
    held = jnp.concatenate([held, got])
    got = swap(held, GATHER[3])
    far = along_x(mine)
    beside = swap(held, CORE)
    qkv, phi_q, phi_k, h1 = made[:4]
    made = mix_call(
        0, 2, inputs, gains, w_out, phi_q, phi_k, qkv, (first, 0, 2 * pairs), None, hd, in_hbm((held,)) + in_vmem((mine,))
    )
    far = gate(far, made[0])
    got, beside = gate(got, far), gate(beside, far)
    second = (near, far, swap(far, CORE))
    made = mix_call(
        2, 1, inputs, gains, w_out, phi_q, phi_k, qkv, (second, 0, pairs), made, hd, in_hbm((got,))
    )
    weights = [beside, gate(swap(got, CORE), made[0]), held, got]
    mixed, rden, x1, h2 = made
    carried = [(first, 0, 2 * pairs), (first, 1, 2 * pairs), (second, 0, pairs)]

    act, pre, g1, ga, gain, side, local = ffn_call(
        h2, cotangent, x1, mixed, rden, phi_q, w_out, gains, weights, hd
    )
    near = swap(local, CORE)
    mine = chip_half(local, near)
    far = along_x(mine)
    send, low = ffn_weight_call(act, pre, cotangent, h2, gain, mixed, ga, n_shard // 2, True, (mine,))
    far = gate(far, low)
    other = swap(far, CORE)
    send = gate(send, other)
    later = (near, far, other)

    def back(b, before, *after):
        return attention_back_call(
            b, side, phi_q, phi_k, qkv, omega, carried[b], (later, b, batch * pairs), before, in_hbm(after)
        )

    def into(b, before, *after):
        return inputs_back_call(b, grads, w_qkv, inputs, g1, gains, before, in_hbm(after))

    def onto(b, before, *after):
        return outputs_call(b, act, x1, weights, before, in_hbm(after))

    got = swap(send, CORE)
    made = back(0, None)
    got = gate(got, made[0])
    low, high = split_sum(low, got)
    got = swap(high, GATHER[3])
    made = back(1, made, high)
    onto_made = onto(0, None, made[0])
    low, high = next_halves(low, gate(got, onto_made[0]), n_shard, 8, False)
    got = swap(high, GATHER[2])
    made = back(2, made, high)
    low, high = next_halves(low, gate(got, made[0]), n_shard, 4, True)
    got = swap(high, GATHER[1])
    (grads,) = made
    late = qkv_weight_call(h1, grads, True, (high,))

    send, *keep = [a.reshape(a.shape[:-3] + (-1, model)) for a in late]
    got = gate(got, send)
    far = swap(gate(send, got), CORE)
    low, high = next_halves(low, got, n_shard, 2, True)
    keep = plane_sums(far, keep)
    got = swap(high, GATHER[0])
    far = [swap(keep[plane], PLANE[plane - 1]) for plane in (1, 2, 3)]
    into_made = into(1, into(0, None, high, *keep))
    got = gate(got, into_made[0])
    far = [gate(a, into_made[0], close=True) for a in far]
    n_late = keep[0].shape[0]
    keep, grad_ffn, piece = sums(
        [keep[0]] + far + [low, got],
        [[((0, 1, 2, 3), 0, n_late)], [((4, 5), 0, n_shard)], [((4, 5), n_shard, n_piece)]],
        [bf16, f32, bf16],
        (1, 2, 3),
    )
    got = swap(keep, LINE[0])
    into_made = into(2, into_made, keep)
    (keep,) = sums([keep, gate(got, into_made[0], close=True)], [[((0, 1), 0, n_late)]], None, (1,))
    got = swap(keep, LINE[1])
    onto_made = onto(1, onto_made, keep)
    (keep,) = sums(
        [keep, gate(got, onto_made[0], close=True), piece], [[((0, 1), 0, n_late), ((2,), 0, n_piece)]], None, (1,)
    )
    got = [swap(keep, masks) for masks in PLANE]
    beside = swap(keep, CORE)
    onto_made = onto(2, onto_made, keep)
    near = [keep] + [gate(a, onto_made[0], close=True) for a in got]
    far = [gate(beside, onto_made[0], close=True)] + [swap(a, CORE) for a in near[1:]]
    grad_wqkv, grad_wout, grad_gains = assemble_call(near + far, w_qkv, gains)
    return onto_made[0], into_made[0], grad_gains, grad_wqkv, grad_wout, grad_ffn


def plain(inputs, gains, w_qkv, w_out, shard, omega, cotangent):
    batch, rows, model = inputs.shape
    heads, hd, _ = omega.shape
    pairs = heads // 2
    pair = lax.all_gather(shard, AXES, axis=1, tiled=True)
    hidden = pair.shape[1]
    unit = min(256, hidden)
    weights = [jnp.swapaxes(pair.reshape(2, hidden // unit, unit, model), 0, 1)]
    made = None
    for b in range(batch):
        made = features_call(b, b, batch, inputs, gains, w_qkv, omega, made)
    qkv, phi_q, phi_k, h1, local = made
    sums = all_states(local, False)
    mixed, rden, x1, h2 = mix_call(
        0, batch, inputs, gains, w_out, phi_q, phi_k, qkv, (sums, 0, batch * pairs), None, hd
    )
    act, pre, g1, ga, gain, side, local = ffn_call(
        h2, cotangent, x1, mixed, rden, phi_q, w_out, gains, weights, hd
    )
    later = all_states(local, True)
    both, grad_wout = ffn_weight_call(act, pre, cotangent, h2, gain, mixed, ga, unit, False)
    both = jnp.swapaxes(both.reshape(-1, 2, unit, model), 0, 1).reshape(2, -1, model)
    grad_ffn = lax.psum_scatter(both, AXES, scatter_dimension=1, tiled=True).astype(f32)
    made = None
    for b in range(batch):
        spot = (b, batch * pairs)
        made = attention_back_call(b, side, phi_q, phi_k, qkv, omega, (sums,) + spot, (later,) + spot, made)
    (grads,) = made
    (grad_wqkv,) = qkv_weight_call(h1, grads, False)
    into_made = onto_made = None
    for b in range(batch):
        into_made = inputs_back_call(b, grads, w_qkv, inputs, g1, gains, into_made)
        onto_made = outputs_call(b, act, x1, weights, onto_made)
    grad_wqkv, grad_wout, gain = lax.psum((grad_wqkv, grad_wout, gain), AXES)
    grad_gains = pl.pallas_call(
        gains_kernel,
        out_shape=jax.ShapeDtypeStruct(gains.shape, f32),
        compiler_params=params(),
    )(grad_wqkv, gain, w_qkv, gains)
    return onto_made[0], into_made[0], grad_gains, grad_wqkv, grad_wout, grad_ffn


def on_device(inputs, gains, w_qkv, w_out, ffn_weight, omega, cotangent):
    fast = lax.axis_size("dp") == 8 and lax.axis_size("seq") == 4 and inputs.shape[0] == 3
    outputs, grad_inputs, *grads = (planned if fast else plain)(
        inputs, gains[0], w_qkv[0], w_out[0], ffn_weight[0], jnp.swapaxes(omega[0], 1, 2), cotangent
    )
    grad_gains, grad_wqkv, grad_wout, grad_ffn = grads
    grad_ffn = grad_ffn.reshape(ffn_weight.shape)
    return (outputs, grad_inputs, grad_gains[None], grad_wqkv[None], grad_wout[None], grad_ffn)


def solution(mesh):
    in_specs = (
        P("dp", "seq", None),
        P(),
        P(),
        P(),
        P(None, None, ("dp", "seq"), None),
        P(),
        P("dp", "seq", None),
    )
    out_specs = (
        P("dp", "seq", None),
        P("dp", "seq", None),
        P(),
        P(),
        P(),
        P(None, None, ("dp", "seq"), None),
    )
    return jax.shard_map(
        on_device, mesh=mesh, in_specs=in_specs, out_specs=out_specs, check_vma=False
    )
```

```python
import functools
import math

import jax
import jax.numpy as jnp
from jax import lax
from jax.experimental import pallas as pl
from jax.experimental.pallas import tpu as pltpu
from jax.sharding import PartitionSpec as P

epsilon = 1e-05
bf16 = jnp.bfloat16
f32 = jnp.float32
AXES = ("dp", "seq")
MIB = 2**20


def nn(a, b):
    return lax.dot_general(a, b, (((1,), (0,)), ((), ())), preferred_element_type=f32)


def nt(a, b):
    return lax.dot_general(a, b, (((1,), (1,)), ((), ())), preferred_element_type=f32)


def tn(a, b):
    return lax.dot_general(a, b, (((0,), (0,)), ((), ())), preferred_element_type=f32)


def lanes_of(shape):
    return lax.broadcasted_iota(jnp.int32, shape, len(shape) - 1)


def params(mib=62):
    return pltpu.CompilerParams(vmem_limit_bytes=mib * MIB)


def cost(flops, nbytes, trans=0):
    return pl.CostEstimate(flops=int(flops), bytes_accessed=int(nbytes), transcendentals=int(trans))


def in_hbm(arrays):
    return [pltpu.with_memory_space_constraint(a, pltpu.HBM) for a in arrays]


def in_vmem(arrays):
    return [pltpu.with_memory_space_constraint(a, pltpu.VMEM) for a in arrays]


def const_block(shape):
    return pl.BlockSpec(shape, lambda *_: (0,) * len(shape))


def stacked_call(kernel, grid, in_specs, out_specs, out_shapes, stacked, before, args, scratch, estimate, after=(), mib=62):
    n_in = len(args)
    aliases = {}
    extra = list(after)
    if before is not None:
        for at, (flag, buffer) in enumerate(zip(stacked, before)):
            if flag:
                aliases[n_in + len(extra)] = at
                extra += in_hbm((buffer,))
    n_extra = len(extra)

    def body(*refs):
        kernel(*refs[:n_in], *refs[n_in + n_extra :])

    return pl.pallas_call(
        body,
        grid=grid,
        in_specs=list(in_specs) + [pl.BlockSpec(memory_space=pl.ANY)] * n_extra,
        out_specs=out_specs,
        out_shape=out_shapes,
        scratch_shapes=scratch,
        input_output_aliases=aliases,
        compiler_params=params(mib),
        cost_estimate=estimate,
    )(*args, *extra)


def normed(values):
    center = values - jnp.mean(values, axis=-1, keepdims=True)
    spread = jnp.mean(center * center, axis=-1, keepdims=True)
    scale = lax.rsqrt(spread + epsilon)
    return center * scale, scale


def norm_back(grad, xhat, scale, gain):
    gy = grad * gain
    return scale * (
        gy - jnp.mean(gy, axis=-1, keepdims=True) - xhat * jnp.mean(gy * xhat, axis=-1, keepdims=True)
    )


def causal_tile(rows):
    return lax.broadcasted_iota(jnp.int32, (rows, rows), 0) >= lax.broadcasted_iota(
        jnp.int32, (rows, rows), 1
    )


def feature_weights(omega, odd):
    ones = jnp.full(omega.shape, -1.0, omega.dtype)
    zeros = jnp.zeros_like(ones)
    parts = [ones, omega, zeros, ones] if odd else [omega, ones, ones, zeros]
    return jnp.concatenate(parts, axis=0)


PER = 2
BACK_PER = 1


def features_kernel(hd, x_ref, gains_ref, w_ref, omega_ref, qkv_ref, phiq_ref, phik_ref, h1_ref, state_ref, qkv_scr):
    step = pl.program_id(0)
    width = 2 * hd
    rows, model = x_ref.shape[1:]
    s = hd ** (-0.25)
    feats = omega_ref.shape[2]
    per = omega_ref.shape[0] // 2

    @pl.when(step == 0)
    def _():
        xhat, _ = normed(x_ref[0].astype(f32))
        hidden = (xhat * gains_ref[0:1, :]).astype(bf16)
        h1_ref[0] = hidden
        for part in range(3):
            cols = slice(part * model, (part + 1) * model)
            made = nn(hidden, w_ref[:, cols]).astype(bf16)
            qkv_ref[0, :, cols] = made
            qkv_scr[part] = made

    low = lanes_of((rows, width)) < hd
    lefts = []
    for at in range(per):
        column = pl.ds(pl.multiple_of((step * per + at) * width, width), width)
        for part in range(2):
            points = qkv_scr[part, :, column].astype(f32)
            energy = points * points * (0.5 * s)
            high = energy.astype(bf16).astype(f32)
            rest = (energy - high).astype(bf16)
            turned = pltpu.roll(high, hd, 1)
            for odd in range(2):
                first = jnp.where(low, turned, points) if odd else jnp.where(low, points, turned)
                lefts.append((at, part, odd, jnp.concatenate([first.astype(bf16), rest], axis=1)))
    made = {}
    for at, part, odd, left in lefts:
        proj = nn(left, feature_weights(omega_ref[2 * at + odd], odd))
        phi = jnp.exp2(proj * (s * math.log2(math.e)) - 0.5 * math.log2(feats)).astype(bf16)
        head = 2 * at + odd
        (phik_ref if part else phiq_ref)[0, :, head * feats : (head + 1) * feats] = phi
        if part:
            made[at, odd] = phi
    for at in range(per):
        column = pl.ds(pl.multiple_of((step * per + at) * width, width), width)
        values = qkv_scr[2, :, column]
        state_ref[at, 0:hd, :] = tn(values, made[at, 0])[0:hd].astype(bf16)
        state_ref[at, hd:width, :] = tn(values, made[at, 1])[hd:width].astype(bf16)
        sums = jnp.concatenate(
            [
                jnp.sum(made[at, 0].astype(f32), axis=0, keepdims=True),
                jnp.sum(made[at, 1].astype(f32), axis=0, keepdims=True),
                jnp.zeros((14, feats), f32),
            ],
            axis=0,
        )
        state_ref[at, width : width + 16, :] = sums.astype(bf16)


def features_call(index, at, count, inputs, gains, w_qkv, omega, before, after=()):
    batch, rows, model = inputs.shape
    heads, hd, feats = omega.shape
    pairs = heads // 2
    per = pairs
    steps = pairs // per
    n_rows = 2 * hd + 16
    phi_spec = pl.BlockSpec((1, rows, 2 * per * feats), lambda g: (index, 0, g))
    return stacked_call(
        functools.partial(features_kernel, hd),
        (steps,),
        [
            pl.BlockSpec((1, rows, model), lambda g: (index, 0, 0)),
            const_block(gains.shape),
            const_block(w_qkv.shape),
            pl.BlockSpec((2 * per, hd, feats), lambda g: (g, 0, 0)),
        ],
        [
            pl.BlockSpec((1, rows, 3 * model), lambda g: (index, 0, 0)),
            phi_spec,
            phi_spec,
            pl.BlockSpec((1, rows, model), lambda g: (index, 0, 0)),
            pl.BlockSpec((per, n_rows, feats), lambda g: (at * steps + g, 0, 0)),
        ],
        [
            jax.ShapeDtypeStruct((batch, rows, 3 * model), bf16),
            jax.ShapeDtypeStruct((batch, rows, heads * feats), bf16),
            jax.ShapeDtypeStruct((batch, rows, heads * feats), bf16),
            jax.ShapeDtypeStruct((batch, rows, model), bf16),
            jax.ShapeDtypeStruct((count * pairs, n_rows, feats), bf16),
        ],
        (True, True, True, True, at > 0),
        before,
        (inputs, gains, w_qkv, omega),
        [pltpu.VMEM((3, rows, model), bf16)],
        cost(2 * rows * model * 3 * model + 4 * heads * rows * 256 * feats, 9 * MIB, 2 * rows * heads * feats),
        after,
    )


def state_block(state_refs, backward, at, step, per, hd, first, count):
    if len(state_refs) == 1:
        total = state_refs[0][at].astype(f32)
    else:
        near, got, other = state_refs
        seq = lax.axis_index("seq")
        core = lax.rem(seq, 2)
        own_half = (first + step * per + at) // (count // 2) == core
        beyond = (seq // 2) == (0 if backward else 1)
        beside = core == (0 if backward else 1)
        total = jnp.where(own_half, got[at].astype(f32), other[at].astype(f32))
        total = jnp.where(beyond, total, 0.0) + jnp.where(beside, near[at].astype(f32), 0.0)
    feats = total.shape[-1]
    width = 2 * hd
    zeros = jnp.zeros((hd, feats), bf16)
    low = total.astype(bf16)
    even_norm = jnp.broadcast_to(total[width : width + 1], (hd, feats)).astype(bf16)
    odd_norm = jnp.broadcast_to(total[width + 1 : width + 2], (hd, feats)).astype(bf16)
    even = jnp.concatenate([low[0:hd], zeros, even_norm, zeros], axis=0)
    odd = jnp.concatenate([zeros, low[hd:width], zeros, odd_norm], axis=0)
    return even, odd


def state_specs(carried, pairs, per):
    states, at, count = carried
    shape = (per,) + states[0].shape[1:]
    first = at * pairs // per
    specs = [pl.BlockSpec(shape, lambda g: (first + g, 0, 0))]
    if len(states) > 1:
        specs += [pl.BlockSpec(shape, lambda g: (lax.rem(first + g, count // 2 // per), 0, 0))] * 2
    return specs


def mix_kernel(hd, n_states, first, count, tile, *refs):
    x_ref, gains_ref, wout_ref, phiq_ref, phik_ref, v_ref = refs[:6]
    state_refs = refs[6 : 6 + n_states]
    mixed_ref, rden_ref, x1_ref, h2_ref, mixed_scr = refs[6 + n_states :]
    step = pl.program_id(0)
    width = 2 * hd
    rows, model = x_ref.shape[1:]
    steps = model // width // PER
    feats = phiq_ref.shape[-1] // (2 * PER)
    causal = causal_tile(tile)
    low = lanes_of((rows, width)) < hd
    ones = jnp.where(low, 1.0, 0.0)
    spans = [(slice(at * tile, (at + 1) * tile), (at + 1) * tile) for at in range(rows // tile)]
    scores = {}
    for at in range(PER):
        for odd in range(2):
            cols = slice((2 * at + odd) * feats, (2 * at + odd + 1) * feats)
            for t, (here, end) in enumerate(spans):
                scores[at, odd, t] = masked(nt(phiq_ref[0, here, cols], phik_ref[0, 0:end, cols]), causal, t, tile)
    for at in range(PER):
        even, odd = state_block(state_refs, False, at, step, PER, hd, first, count)
        both_state = jnp.concatenate([even, odd], axis=1)
        values = v_ref[0, :, at * width : (at + 1) * width].astype(f32)
        sides = [
            jnp.concatenate([jnp.where(low, values, 0.0), ones], axis=1).astype(bf16),
            jnp.concatenate([jnp.where(low, 0.0, values), 1.0 - ones], axis=1).astype(bf16),
        ]
        cols = slice(2 * at * feats, 2 * (at + 1) * feats)
        lanes = slice(at * width, (at + 1) * width)
        column = pl.ds(pl.multiple_of((lax.rem(step, steps) * PER + at) * width, width), width)
        for t, (here, end) in enumerate(spans):
            total = nt(phiq_ref[0, here, cols], both_state)
            for odd in range(2):
                total = total + nn(scores[at, odd, t], sides[odd][0:end])
            rden = 1.0 / total[:, width:]
            mixed = (total[:, :width] * rden).astype(bf16)
            rden_ref[0, here, lanes] = rden
            mixed_ref[0, here, lanes] = mixed
            mixed_scr[here, column] = mixed

    @pl.when(lax.rem(step, steps) == steps - 1)
    def _():
        x1 = x_ref[0].astype(f32) + nn(mixed_scr[...], wout_ref[...])
        x1_ref[0] = x1
        xhat, _ = normed(x1)
        h2_ref[0] = (xhat * gains_ref[1:2, :]).astype(bf16)


def masked(made, causal, at, tile):
    last = jnp.where(causal, made[:, at * tile :], 0.0)
    if at > 0:
        last = jnp.concatenate([made[:, : at * tile], last], axis=1)
    return last.astype(bf16)


def mix_call(index, members, inputs, gains, w_out, phi_q, phi_k, qkv, carried, before, hd, after=()):
    batch, rows, model = inputs.shape
    width = 2 * hd
    pairs = model // width
    steps = pairs // PER
    states, at, count = carried
    heads = 2 * pairs
    feats = phi_q.shape[-1] // heads
    tile = min(256, rows)
    whole = pl.BlockSpec((1, rows, model), lambda g: (index + g // steps, 0, 0))
    narrow = pl.BlockSpec((1, rows, PER * width), lambda g: (index + g // steps, 0, lax.rem(g, steps)))
    phi_spec = pl.BlockSpec((1, rows, 2 * PER * feats), lambda g: (index + g // steps, 0, lax.rem(g, steps)))
    return stacked_call(
        functools.partial(mix_kernel, hd, len(states), at * pairs, count, tile),
        (members * steps,),
        [
            whole,
            const_block(gains.shape),
            const_block(w_out.shape),
            phi_spec,
            phi_spec,
            pl.BlockSpec((1, rows, PER * width), lambda g: (index + g // steps, 0, 2 * steps + lax.rem(g, steps))),
        ]
        + state_specs(carried, pairs, PER),
        [narrow, narrow, whole, whole],
        [
            jax.ShapeDtypeStruct((batch, rows, model), bf16),
            jax.ShapeDtypeStruct((batch, rows, model), f32),
            jax.ShapeDtypeStruct((batch, rows, model), f32),
            jax.ShapeDtypeStruct((batch, rows, model), bf16),
        ],
        (True,) * 4,
        before,
        (inputs, gains, w_out, phi_q, phi_k, qkv) + tuple(states),
        [pltpu.VMEM((rows, model), bf16)],
        cost(members * (heads * 2 * rows * rows * 512 + 2 * rows * model * model), members * 9 * MIB),
        after,
    )


def ffn_kernel(groups, batch, hd, *refs):
    h2_ref, gf_ref, wout_ref, gains_ref = refs[:4]
    late_any = refs[4:8]
    weights = refs[8 : 8 + groups]
    act_ref, pre_ref, g1_ref, ga_ref, gain_ref, side_ref, gstate_ref = refs[8 + groups : 15 + groups]
    up_scr, down_scr, pre_scr, x1_scr, mixed_scr, rden_scr, phiq_scr, sems, late_sems = refs[15 + groups :]
    step = pl.program_id(0)
    n_blocks = pl.num_programs(0) - batch
    each = n_blocks // groups
    block = act_ref.shape[-1]
    rows = h2_ref.shape[1]
    model = h2_ref.shape[2]
    shards, unit = up_scr.shape[1:3]
    taken = block // unit
    started = []
    for group in range(groups):
        started.append(pltpu.make_async_copy(weights[group].at[:, 0], up_scr.at[group], sems.at[2 * group]))
        started.append(pltpu.make_async_copy(weights[group].at[:, 1], down_scr.at[group], sems.at[2 * group + 1]))

    def late_copies(b):
        slot = lax.rem(b, 2)
        return [
            pltpu.make_async_copy(src.at[b], dst.at[slot], late_sems.at[slot, at])
            for at, (src, dst) in enumerate(zip(late_any, (x1_scr, mixed_scr, rden_scr, phiq_scr)))
        ]

    @pl.when(step == 0)
    def _():
        for copy in started:
            copy.start()

    @pl.when((step >= n_blocks - 1) & (step < n_blocks + batch - 1))
    def _():
        for copy in late_copies(step - n_blocks + 1):
            copy.start()

    for group in range(groups):

        @pl.when(step == group * each)
        def _():
            started[2 * group].wait()
            started[2 * group + 1].wait()

    @pl.when(step < n_blocks)
    def _():
        here = pl.ds(pl.multiple_of(lax.rem(step, each) * taken, taken), taken)
        up = up_scr[step // each, here].reshape(block, model)
        down = down_scr[step // each, here].reshape(block, model)
        cols = pl.ds(pl.multiple_of(step * block, block), block)
        for b in range(batch):
            pre = nt(h2_ref[b], up)
            part = 0.5 * lax.erf(pre * math.sqrt(0.5)) + 0.5
            act_ref[b] = (pre * part).astype(bf16)
            slope = part + pre * (
                jnp.exp2(pre * pre * (-0.5 * math.log2(math.e))) * (1.0 / math.sqrt(2.0 * math.pi))
            )
            grad_pre = (nt(gf_ref[b], down) * slope).astype(bf16)
            pre_ref[b] = grad_pre
            pre_scr[b, :, cols] = grad_pre

    @pl.when(step >= n_blocks)
    def _():
        b = step - n_blocks
        slot = lax.rem(b, 2)
        grad = nn(pre_scr[b], up_scr[...].reshape(n_blocks * block, model))
        for copy in late_copies(b):
            copy.wait()
        phiq = phiq_scr.at[slot]
        xhat, scale = normed(x1_scr[slot])
        g1 = gf_ref[b].astype(f32) + norm_back(grad, xhat, scale, gains_ref[1:2, :])
        g1_ref[0] = g1
        gain = jnp.sum(grad * xhat, axis=0, keepdims=True)

        @pl.when(b == 0)
        def _():
            gain_ref[...] = jnp.zeros_like(gain_ref)

        gain_ref[0:1] += gain
        ga = g1.astype(bf16)
        ga_ref[0] = ga
        gn_full = nt(ga, wout_ref[...]) * rden_scr[slot]
        gn_low = gn_full.astype(bf16)
        product = gn_full * mixed_scr[slot].astype(f32)
        high = product.astype(bf16)
        rest = (product - high.astype(f32)).astype(bf16)
        width = 2 * hd
        same = lax.div(lax.rem(lax.broadcasted_iota(jnp.int32, (2 * width, width), 0), width), hd) == lax.div(
            lax.broadcasted_iota(jnp.int32, (2 * width, width), 1), hd
        )
        minus = jnp.where(same, -1.0, 0.0).astype(bf16)
        inner = lax.rem(lanes_of((rows, width)), hd)
        feats = phiq.shape[-1] // (model // hd)
        sides = []
        for at in range(model // width):
            cols = slice(at * width, (at + 1) * width)
            gd = nn(jnp.concatenate([high[:, cols], rest[:, cols]], axis=1), minus)
            gd_high = gd.astype(bf16).astype(f32)
            gdx = jnp.where(inner == 0, gd_high, jnp.where(inner == 1, gd - gd_high, 0.0))
            sides.append(jnp.concatenate([gn_low[:, cols], gdx.astype(bf16)], axis=1))
        for at, side in enumerate(sides):
            side_ref[0, at] = side
        sums = [
            [tn(side, phiq[:, (2 * at + odd) * feats : (2 * at + odd + 1) * feats]) for odd in range(2)]
            for at, side in enumerate(sides)
        ]
        for at, (even, odd) in enumerate(sums):
            gstate_ref[at, 0:hd] = even[0:hd].astype(bf16)
            gstate_ref[at, hd:width] = odd[hd:width].astype(bf16)
            norms = jnp.concatenate(
                [
                    even[width : width + 1] + even[width + 1 : width + 2],
                    odd[width + hd : width + hd + 1] + odd[width + hd + 1 : width + hd + 2],
                    jnp.zeros((14, feats), f32),
                ],
                axis=0,
            )
            gstate_ref[at, width : width + 16] = norms.astype(bf16)


def ffn_call(h2, gf, x1, mixed, rden, phi_q, w_out, gains, weights, hd):
    batch, rows, model = h2.shape
    groups = len(weights)
    shards, _, unit, _ = weights[0].shape
    hidden = groups * shards * unit
    block = min(512, shards * unit)
    n_blocks = hidden // block
    pairs = model // (2 * hd)
    feats = phi_q.shape[-1] // (2 * pairs)
    n_rows = 2 * hd + 16
    here = lambda j: jnp.clip(j - n_blocks, 0, batch - 1)
    late = pl.BlockSpec((1, rows, model), lambda j: (here(j), 0, 0))
    wide = pl.BlockSpec((batch, rows, block), lambda j: (0, 0, jnp.minimum(j, n_blocks - 1)))
    scratch = (groups, shards, unit, model)
    return pl.pallas_call(
        functools.partial(ffn_kernel, groups, batch, hd),
        grid=(n_blocks + batch,),
        in_specs=[
            const_block(h2.shape),
            const_block(gf.shape),
            const_block(w_out.shape),
            const_block(gains.shape),
        ]
        + [pl.BlockSpec(memory_space=pl.ANY)] * (4 + groups),
        out_specs=[
            wide,
            wide,
            late,
            late,
            const_block((16, model)),
            pl.BlockSpec((1, pairs, rows, 4 * hd), lambda j: (here(j), 0, 0, 0)),
            pl.BlockSpec((pairs, n_rows, feats), lambda j: (here(j), 0, 0)),
        ],
        out_shape=[
            jax.ShapeDtypeStruct((batch, rows, hidden), bf16),
            jax.ShapeDtypeStruct((batch, rows, hidden), bf16),
            jax.ShapeDtypeStruct((batch, rows, model), f32),
            jax.ShapeDtypeStruct((batch, rows, model), bf16),
            jax.ShapeDtypeStruct((16, model), f32),
            jax.ShapeDtypeStruct((batch, pairs, rows, 4 * hd), bf16),
            jax.ShapeDtypeStruct((batch * pairs, n_rows, feats), bf16),
        ],
        scratch_shapes=[
            pltpu.VMEM(scratch, bf16),
            pltpu.VMEM(scratch, bf16),
            pltpu.VMEM((batch, rows, hidden), bf16),
            pltpu.VMEM((2, rows, model), f32),
            pltpu.VMEM((2, rows, model), bf16),
            pltpu.VMEM((2, rows, model), f32),
            pltpu.VMEM((2, rows, phi_q.shape[-1]), bf16),
            pltpu.SemaphoreType.DMA((2 * groups,)),
            pltpu.SemaphoreType.DMA((2, 4)),
        ],
        compiler_params=params(),
        cost_estimate=cost(6 * batch * rows * hidden * model, 30 * MIB, 2 * batch * rows * hidden),
    )(h2, gf, w_out, gains, x1, mixed, rden, phi_q, *weights)


def row_owner(far, y_bit, x_bit):
    seq = lax.axis_index("seq")
    y, x, core = lax.rem(lax.axis_index("dp"), 2), seq // 2, lax.rem(seq, 2)
    return (core ^ far) * 4 + (y ^ y_bit) * 2 + (x ^ x_bit)


def plane_of(far, first, second):
    turned = (lax.rem(lax.axis_index("seq"), 2) ^ far) == 1
    return jnp.where(turned, second, first), jnp.where(turned, first, second)


EXTRA = 16


def ffn_weight_kernel(unit, n_pieces, n_after, *refs):
    act_ref, pre_ref, gf_ref, h2_ref, gain_ref, mixed_any, ga_any = refs[:7]
    outs = refs[7 + n_after : 9 + n_after]
    mixed_scr, ga_scr, sum_scr, row_scr, piece_scr, in_sems, row_sems, piece_sems = refs[9 + n_after :]
    step = pl.program_id(0)
    n_blocks = pl.num_programs(0)
    batch, rows, block = act_ref.shape
    model = gf_ref.shape[2]
    n_rows = row_scr.shape[1]
    slot = lax.rem(step, 2)
    copies = [
        pltpu.make_async_copy(mixed_any, mixed_scr, in_sems.at[0]),
        pltpu.make_async_copy(ga_any, ga_scr, in_sems.at[1]),
    ]

    def row_copy(out, row, slot):
        row = pl.multiple_of(row, 16)
        return pltpu.make_async_copy(row_scr.at[slot], out.at[pl.ds(row, n_rows)], row_sems.at[slot])

    @pl.when(step == 0)
    def _():
        for copy in copies:
            copy.start()

    down = tn(act_ref[...].reshape(batch * rows, block), gf_ref[...].reshape(batch * rows, model)).astype(bf16)
    up = tn(pre_ref[...].reshape(batch * rows, block), h2_ref[...].reshape(batch * rows, model)).astype(bf16)

    @pl.when(step >= 2)
    def _():
        row_copy(outs[0], 0, slot).wait()

    for at in range(block // unit):
        here = slice(at * unit, (at + 1) * unit)
        row_scr[slot, 2 * at * unit : (2 * at + 1) * unit] = up[here]
        row_scr[slot, (2 * at + 1) * unit : (2 * at + 2) * unit] = down[here]
    if n_pieces:
        half = n_blocks // 2
        quarter = n_blocks // 4
        held = outs[0].shape[0] // 2
        inside = lax.rem(step, half)
        row = (inside // quarter) * held + lax.rem(inside, quarter) * n_rows
        for at in range(2):

            @pl.when(step // half == at)
            def _():
                row_copy(outs[at], row, slot).start()
    else:
        row_copy(outs[0], step * n_rows, slot).start()

    def piece_copies():
        if not n_pieces:
            return [pltpu.make_async_copy(sum_scr, outs[1], piece_sems.at[0])]
        held = outs[0].shape[0] // 2
        n_piece = piece_scr.shape[1]
        return [
            pltpu.make_async_copy(
                piece_scr.at[2 * at + first],
                outs[at].at[(first + 1) * held - n_piece : (first + 1) * held],
                piece_sems.at[2 * at + first],
            )
            for at in range(2)
            for first in range(2)
        ]

    @pl.when(step == n_blocks // 2)
    def _():
        for copy in copies:
            copy.wait()
        sum_scr[...] = tn(
            mixed_scr[...].reshape(batch * rows, model), ga_scr[...].reshape(batch * rows, model)
        )
        if n_pieces:
            piece = model // 8
            gain = gain_ref[...].astype(bf16)
            for at in range(2):
                for first in range(2):
                    for second in range(2):
                        owner = row_owner(1 - at, *plane_of(1 - at, first, second))
                        taken = sum_scr[pl.ds(pl.multiple_of(owner * piece, piece), piece), :].astype(bf16)
                        row = second * (piece + EXTRA)
                        piece_scr[2 * at + first, row : row + piece] = taken
                        piece_scr[2 * at + first, row + piece : row + piece + EXTRA] = gain
        for copy in piece_copies():
            copy.start()

    @pl.when(step == n_blocks - 1)
    def _():
        row_copy(outs[0], 0, 1 - slot).wait()
        row_copy(outs[0], 0, slot).wait()
        for copy in piece_copies():
            copy.wait()


def ffn_weight_call(act, pre, gf, h2, gain, mixed, ga, unit, fast, after=()):
    batch, rows, model = h2.shape
    hidden = act.shape[-1]
    block = min(512, hidden)
    n_blocks = hidden // block
    wide = pl.BlockSpec((batch, rows, block), lambda j: (0, 0, j))
    n_piece = 2 * (model // 8 + EXTRA)
    if fast:
        out_shapes = [jax.ShapeDtypeStruct((hidden + 2 * n_piece, model), bf16)] * 2
    else:
        out_shapes = [jax.ShapeDtypeStruct((2 * hidden, model), bf16), jax.ShapeDtypeStruct((model, model), f32)]
    anywhere = pl.BlockSpec(memory_space=pl.ANY)
    return pl.pallas_call(
        functools.partial(ffn_weight_kernel, unit, 8 if fast else 0, len(after)),
        grid=(n_blocks,),
        in_specs=[wide, wide, const_block(gf.shape), const_block(h2.shape), const_block(gain.shape), anywhere, anywhere]
        + [anywhere] * len(after),
        out_specs=[anywhere] * 2,
        out_shape=out_shapes,
        scratch_shapes=[
            pltpu.VMEM(mixed.shape, bf16),
            pltpu.VMEM(ga.shape, bf16),
            pltpu.VMEM((model, model), f32),
            pltpu.VMEM((2, 2 * block, model), bf16),
            pltpu.VMEM((4, n_piece, model), bf16),
            pltpu.SemaphoreType.DMA((2,)),
            pltpu.SemaphoreType.DMA((2,)),
            pltpu.SemaphoreType.DMA((4,)),
        ],
        compiler_params=params(),
        cost_estimate=cost(4 * batch * rows * hidden * model, 22 * MIB),
    )(act, pre, gf, h2, gain, mixed, ga, *in_hbm(after))


def attention_back_kernel(hd, n_prev, n_later, spots, tile, *refs):
    side_ref, phiq_ref, phik_ref, q_ref, k_ref, v_ref, omega_ref = refs[:7]
    prev_refs = refs[7 : 7 + n_prev]
    later_refs = refs[7 + n_prev : 7 + n_prev + n_later]
    (out_ref,) = refs[7 + n_prev + n_later :]
    step = pl.program_id(0)
    width = 2 * hd
    rows = q_ref.shape[1]
    feats = phiq_ref.shape[-1] // (2 * BACK_PER)
    tiles = rows // tile
    s = hd ** (-0.25)
    low = lanes_of((rows, width)) < hd
    low_tile = low[0:tile]
    inner = lax.rem(lanes_of((rows, width)), hd)
    ones = jnp.where(inner < 2, 1.0, 0.0)
    one = jnp.where(inner == 0, 1.0, 0.0).astype(bf16)
    causal = causal_tile(tile)
    spans = [(slice(t * tile, (t + 1) * tile), (t + 1) * tile) for t in range(tiles)]
    heads = [(at, odd) for at in range(BACK_PER) for odd in range(2)]
    each = [(at, odd, t) for at, odd in heads for t in range(tiles)]
    cols = {(at, odd): slice((2 * at + odd) * feats, (2 * at + odd + 1) * feats) for at, odd in heads}
    lanes = [slice(at * width, (at + 1) * width) for at in range(BACK_PER)]

    def column(made, at, odd, t):
        return jnp.concatenate([made[at, odd, i][:, t * tile : (t + 1) * tile] for i in range(t, tiles)], axis=0)

    made, scores, weights, value_sides = {}, {}, {}, {}
    for at in range(BACK_PER):
        values = v_ref[0, :, lanes[at]].astype(f32)
        value_sides[at, 0] = jnp.concatenate(
            [jnp.where(low, values, 0.0), jnp.where(low, ones, 0.0)], axis=1
        ).astype(bf16)
        value_sides[at, 1] = jnp.concatenate(
            [jnp.where(low, 0.0, values), jnp.where(low, 0.0, ones)], axis=1
        ).astype(bf16)
    for at, odd, t in each:
        here, end = spans[t]
        made[at, odd, t] = masked(nt(side_ref[0, at, here], value_sides[at, odd][0:end]), causal, t, tile)
    for at, odd, t in each:
        here, end = spans[t]
        scores[at, odd, t] = masked(
            nt(phiq_ref[0, here, cols[at, odd]], phik_ref[0, 0:end, cols[at, odd]]), causal, t, tile
        )
    prev = [state_block(prev_refs, False, at, step, BACK_PER, hd, *spots[0]) for at in range(BACK_PER)]
    later = [state_block(later_refs, True, at, step, BACK_PER, hd, *spots[1]) for at in range(BACK_PER)]
    for at, odd in heads:
        weights[at, odd] = feature_weights(omega_ref[2 * at + odd], odd)
    proj_q, proj_k = {}, {}
    for at, odd, t in each:
        here, end = spans[t]
        grad_phi = nn(side_ref[0, at, here], prev[at][odd]) + nn(made[at, odd, t], phik_ref[0, 0:end, cols[at, odd]])
        proj_q[at, odd, t] = (grad_phi * phiq_ref[0, here, cols[at, odd]].astype(f32)).astype(bf16)
    for at, odd, t in each:
        here = spans[t][0]
        beside = jnp.concatenate([v_ref[0, here, lanes[at]], one[here]], axis=1)
        grad_phi = nn(beside, later[at][odd]) + tn(column(made, at, odd, t), phiq_ref[0, t * tile :, cols[at, odd]])
        proj_k[at, odd, t] = (grad_phi * phik_ref[0, here, cols[at, odd]].astype(f32)).astype(bf16)
    back_q = {key: nt(proj_q[key], weights[key[:2]]) for key in each}
    back_k = {key: nt(proj_k[key], weights[key[:2]]) for key in each}
    for at in range(BACK_PER):
        both = jnp.concatenate([later[at][0][0:width], later[at][1][0:width]], axis=1)
        gn_pair = side_ref[0, at, :, 0:width].astype(f32)
        gn_sides = [jnp.where(low, gn_pair, 0.0).astype(bf16), jnp.where(low, 0.0, gn_pair).astype(bf16)]
        for t in range(tiles):
            here = spans[t][0]
            grad_v = nt(phik_ref[0, here, 2 * at * feats : 2 * (at + 1) * feats], both)
            for odd in range(2):
                grad_v = grad_v + tn(column(scores, at, odd, t), gn_sides[odd][t * tile :])
            out_ref[0, 2, here, lanes[at]] = grad_v.astype(bf16)
    for part, back, points_ref in ((0, back_q, q_ref), (1, back_k, k_ref)):
        for at in range(BACK_PER):
            for t in range(tiles):
                here = spans[t][0]
                even, odd = back[at, 0, t], back[at, 1, t]
                along = jnp.where(low_tile, even[:, :width], odd[:, :width])
                total = jnp.where(low_tile, even[:, width:], odd[:, width:])
                points = points_ref[0, here, lanes[at]].astype(f32)
                out_ref[0, part, here, lanes[at]] = (s * along + (s * s) * points * total).astype(bf16)


def attention_back_call(index, side, phi_q, phi_k, qkv, omega, carried, later, before, after=()):
    batch, pairs, rows, wide = side.shape
    heads, hd, feats = omega.shape
    steps = pairs // BACK_PER
    model = pairs * 2 * hd
    tile = min(256, rows)
    phi_spec = pl.BlockSpec((1, rows, 2 * BACK_PER * feats), lambda g: (index, 0, g))
    spots = tuple((at * pairs, count) for _, at, count in (carried, later))

    def part(n):
        return pl.BlockSpec((1, rows, 2 * BACK_PER * hd), lambda g: (index, 0, n * steps + g))

    return stacked_call(
        functools.partial(attention_back_kernel, hd, len(carried[0]), len(later[0]), spots, tile),
        (steps,),
        [
            pl.BlockSpec((1, BACK_PER, rows, wide), lambda g: (index, g, 0, 0)),
            phi_spec,
            phi_spec,
            part(0),
            part(1),
            part(2),
            pl.BlockSpec((2 * BACK_PER, hd, feats), lambda g: (g, 0, 0)),
        ]
        + state_specs(carried, pairs, BACK_PER)
        + state_specs(later, pairs, BACK_PER),
        [pl.BlockSpec((1, 3, rows, 2 * BACK_PER * hd), lambda g: (index, 0, 0, g))],
        [jax.ShapeDtypeStruct((batch, 3, rows, model), bf16)],
        (True,),
        before,
        (side, phi_q, phi_k, qkv, qkv, qkv, omega) + tuple(carried[0]) + tuple(later[0]),
        [],
        cost(heads * 2 * rows * (rows * 1024 + 6 * 65536), 12 * MIB),
        after,
    )


def qkv_weight_kernel(fast, n_after, *refs):
    h1_ref, grad_ref = refs[:2]
    outs = refs[2 + n_after :]
    batch, rows, model = h1_ref.shape
    total = tn(h1_ref[...].reshape(batch * rows, model), grad_ref[...].reshape(batch * rows, model))
    if not fast:
        outs[0][...] = total
        return
    far_ref, *near_refs, sum_scr = outs
    sum_scr[...] = total
    piece = model // 8
    for far in range(2):
        for plane in range(4):
            owner = row_owner(far, plane // 2, plane % 2)
            taken = sum_scr[pl.ds(pl.multiple_of(owner * piece, piece), piece), :].astype(bf16)
            if far:
                far_ref[plane, 0] = taken
            else:
                near_refs[plane][0] = taken


def qkv_weight_call(h1, grads, fast, after=()):
    batch, rows, model = h1.shape
    if fast:
        out_specs = [pl.BlockSpec((4, 1, model // 8, model), lambda p: (0, p, 0, 0))]
        out_shapes = [jax.ShapeDtypeStruct((4, 3, model // 8, model), bf16)]
        out_specs += [pl.BlockSpec((1, model // 8, model), lambda p: (p, 0, 0))] * 4
        out_shapes += [jax.ShapeDtypeStruct((3, model // 8, model), bf16)] * 4
    else:
        out_specs = [pl.BlockSpec((model, model), lambda p: (0, p))]
        out_shapes = [jax.ShapeDtypeStruct((model, 3 * model), f32)]
    return pl.pallas_call(
        functools.partial(qkv_weight_kernel, fast, len(after)),
        grid=(3,),
        in_specs=[const_block(h1.shape), pl.BlockSpec((batch, 1, rows, model), lambda p: (0, p, 0, 0))]
        + [pl.BlockSpec(memory_space=pl.ANY)] * len(after),
        out_specs=out_specs,
        out_shape=out_shapes,
        scratch_shapes=[pltpu.VMEM((model, model), f32)] if fast else [],
        compiler_params=params(),
        cost_estimate=cost(6 * batch * rows * model * model, 8 * MIB),
    )(h1, grads, *in_hbm(after))


def inputs_back_kernel(grads_ref, w_ref, x_ref, g1_ref, gains_ref, grad_ref):
    model = x_ref.shape[2]
    grad = nt(grads_ref[0, 0], w_ref[:, :model])
    for part in (1, 2):
        grad = grad + nt(grads_ref[0, part], w_ref[:, part * model : (part + 1) * model])
    xhat, scale = normed(x_ref[0].astype(f32))
    grad_ref[0] = g1_ref[0] + norm_back(grad, xhat, scale, gains_ref[0:1, :])


def inputs_back_call(index, members, grads, w_qkv, inputs, g1, gains, before, after=()):
    batch, rows, model = inputs.shape
    whole = pl.BlockSpec((1, rows, model), lambda j: (index + j, 0, 0))
    return stacked_call(
        inputs_back_kernel,
        (members,),
        [
            pl.BlockSpec((1, 3, rows, model), lambda j: (index + j, 0, 0, 0)),
            const_block(w_qkv.shape),
            whole,
            whole,
            const_block(gains.shape),
        ],
        [whole],
        [jax.ShapeDtypeStruct((batch, rows, model), f32)],
        (True,),
        before,
        (grads, w_qkv, inputs, g1, gains),
        [],
        cost(6 * members * rows * model * model, 6 * members * MIB),
        after,
        62,
    )


def outputs_kernel(groups, *refs):
    act_ref, x1_ref = refs[:2]
    weights = refs[2 : 2 + groups]
    out_ref, down_scr, sems = refs[2 + groups :]
    copies = [
        pltpu.make_async_copy(weights[group].at[:, 1], down_scr.at[group], sems.at[group]) for group in range(groups)
    ]
    for copy in copies:
        copy.start()
    for copy in copies:
        copy.wait()
    down = down_scr[...].reshape(act_ref.shape[2], x1_ref.shape[2])
    out_ref[0] = (x1_ref[0] + nn(act_ref[0], down)).astype(bf16)


def outputs_call(index, act, x1, weights, before, after=()):
    batch, rows, model = x1.shape
    hidden = act.shape[2]
    groups = len(weights)
    shards, _, unit, _ = weights[0].shape
    one = lambda j: (index, 0, 0)
    return stacked_call(
        functools.partial(outputs_kernel, groups),
        (1,),
        [pl.BlockSpec((1, rows, hidden), one), pl.BlockSpec((1, rows, model), one)]
        + [pl.BlockSpec(memory_space=pl.ANY)] * groups,
        [pl.BlockSpec((1, rows, model), one)],
        [jax.ShapeDtypeStruct((batch, rows, model), bf16)],
        (True,),
        before,
        (act, x1) + tuple(weights),
        [pltpu.VMEM((groups, shards, unit, model), bf16), pltpu.SemaphoreType.DMA((groups,))],
        cost(2 * rows * model * hidden, 6 * MIB),
        after,
        62,
    )


CORE = (1, 1)
GATHER = ((16, 8), (8, 16), (2, 4), (4, 2))
PLANE = ((2, 2), (4, 4), (6, 6))
LINE = ((16, 8), (8, 16))


def swap(array, masks):
    return lax.ppermute(array, AXES, [(i, i ^ masks[i & 1]) for i in range(32)])


def small(array, kib):
    return array.size * array.dtype.itemsize <= kib * 1024


def gate(array, *deps, close=False):
    anywhere = pl.BlockSpec(memory_space=pl.ANY)
    return pl.pallas_call(
        lambda *refs: None,
        in_specs=[anywhere] * (1 + len(deps)),
        out_specs=anywhere,
        out_shape=jax.ShapeDtypeStruct(array.shape, array.dtype),
        input_output_aliases={0: 0},
    )(*(in_vmem((array,)) if close or small(array, 700) else (array,)), *[a if small(a, 1000) else in_hbm((a,))[0] for a in deps])


def all_states(local, backward):
    everything = lax.all_gather(local, "seq").astype(f32)
    count, place = lax.axis_size("seq"), lax.axis_index("seq")
    at = jnp.arange(count)
    wanted = (at > place) if backward else (at < place)
    total = jnp.sum(jnp.where(wanted[:, None, None, None], everything, 0.0), axis=0)
    return (total.astype(bf16),)


def chip_half(local, near):
    core = lax.rem(lax.axis_index("seq"), 2)
    half = local.shape[0] // 2
    low, high = [
        (local[rows].astype(f32) + near[rows].astype(f32)).astype(bf16) for rows in (slice(0, half), slice(half, None))
    ]
    return jnp.where(core == 0, low, high)


def sums_kernel(n_terms, plan, *refs):
    terms, outs = refs[:n_terms], refs[n_terms:]
    for out, pieces in zip(outs, plan):
        to = 0
        for names, first, size in pieces:
            total = terms[names[0]][first : first + size].astype(f32)
            for name in names[1:]:
                total = total + terms[name][first : first + size].astype(f32)
            out[to : to + size] = total.astype(out.dtype)
            to += size


def sums(terms, plan, kinds=None, close=()):
    model = terms[0].shape[-1]
    kinds = kinds or [bf16] * len(plan)
    shapes = [
        jax.ShapeDtypeStruct((sum(size for _, _, size in pieces), model), kind)
        for pieces, kind in zip(plan, kinds)
    ]
    return pl.pallas_call(
        functools.partial(sums_kernel, len(terms), plan),
        out_shape=shapes,
        compiler_params=params(),
        cost_estimate=cost(sum(t.size for t in terms), 3 * sum(t.size for t in terms)),
    )(*[in_vmem((t,))[0] if at in close else t for at, t in enumerate(terms)])


def split_kernel(near_ref, got_ref, low_ref, high_ref):
    for at, out_ref in enumerate((low_ref, high_ref)):
        out_ref[...] = (near_ref[at].astype(f32) + got_ref[at].astype(f32)).astype(bf16)


def split_sum(near, got):
    rows, model = near.shape
    half = rows // 2
    block = half // 2
    both = pl.BlockSpec((2, block, model), lambda i: (0, i, 0))
    one = pl.BlockSpec((block, model), lambda i: (i, 0))
    return pl.pallas_call(
        split_kernel,
        grid=(2,),
        in_specs=[both, both],
        out_specs=[one, one],
        out_shape=[jax.ShapeDtypeStruct((half, model), bf16)] * 2,
        compiler_params=params(),
        cost_estimate=cost(near.size, 6 * near.size),
    )(near.reshape(2, half, model), got.reshape(2, half, model))


def along_x(mine):
    return swap(mine, (2, 2))


def assemble_kernel(*refs):
    pieces = refs[:8]
    wqkv_ref, gains_ref, gw_ref, gwout_ref, ggain_ref = refs[8:]
    model = gwout_ref.shape[0]
    rows = model // 8
    for far in range(2):
        for plane in range(4):
            owner = row_owner(far, plane // 2, plane % 2)
            at = pl.ds(pl.multiple_of(owner * rows, rows), rows)
            piece = pieces[4 * far + plane]
            for part in range(3):
                gw_ref[at, part * model : (part + 1) * model] = piece[part * rows : (part + 1) * rows].astype(f32)
            gwout_ref[at, :] = piece[3 * rows : 4 * rows].astype(f32)

            @pl.when(owner == 0)
            def _():
                ggain_ref[1:2, :] = piece[4 * rows : 4 * rows + EXTRA].astype(f32)[0:1]

    ggain_ref[0:1, :] = first_gain(gw_ref, wqkv_ref, gains_ref)


def first_gain(gw_ref, wqkv_ref, gains_ref):
    along = jnp.sum(gw_ref[...] * wqkv_ref[...].astype(f32), axis=1, keepdims=True)
    return jnp.broadcast_to(along, (along.shape[0], 128)).T[0:1, :] / gains_ref[0:1, :]


def assemble_call(pieces, w_qkv, gains):
    model = w_qkv.shape[0]
    return pl.pallas_call(
        assemble_kernel,
        out_shape=[
            jax.ShapeDtypeStruct(w_qkv.shape, f32),
            jax.ShapeDtypeStruct((model, model), f32),
            jax.ShapeDtypeStruct(gains.shape, f32),
        ],
        compiler_params=params(40),
    )(*in_vmem(pieces), w_qkv, gains)


def gains_kernel(gw_ref, gain_ref, wqkv_ref, gains_ref, ggain_ref):
    ggain_ref[0:1, :] = first_gain(gw_ref, wqkv_ref, gains_ref)
    ggain_ref[1:2, :] = gain_ref[0:1, :]


def plane_kernel(far_ref, *refs):
    for at in range(4):
        refs[4 + at][...] = (far_ref[at].astype(f32) + refs[at][...].astype(f32)).astype(bf16)


def plane_sums(far, near):
    return pl.pallas_call(
        plane_kernel,
        out_shape=[jax.ShapeDtypeStruct(a.shape, bf16) for a in near],
        compiler_params=params(),
        cost_estimate=cost(far.size, 6 * far.size),
    )(far, *near)


def next_halves(low, got, n_shard, shards, whole_pieces):
    cut = shards * n_shard
    n_pieces = low.shape[0] - cut
    pieces = [(cut, n_pieces)] * 2 if whole_pieces else [(cut, n_pieces // 2), (cut + n_pieces // 2, n_pieces // 2)]
    return sums(
        [low, got],
        [[((0, 1), at * cut // 2, cut // 2), ((0, 1),) + pieces[at]] for at in range(2)],
        None,
        (1,) if small(got, 700) else (),
    )


def planned(inputs, gains, w_qkv, w_out, shard, omega, cotangent):
    batch, rows, model = inputs.shape
    heads, hd, _ = omega.shape
    pairs = heads // 2
    n_shard, n_piece = 2 * shard.shape[1], model // 8 + EXTRA

    held = shard[None]
    got = swap(held, GATHER[0])
    made = features_call(0, 0, 2, inputs, gains, w_qkv, omega, None)
    held = jnp.concatenate([held, gate(got, made[0])])
    got = swap(held, GATHER[1])
    made = features_call(1, 1, 2, inputs, gains, w_qkv, omega, made, in_vmem((held,)))
    got = gate(got, made[0])
    local = gate(made[4], got)
    near = swap(local, CORE)
    mine = chip_half(local, near)
    held = jnp.concatenate([held, got])
    got = swap(held, GATHER[2])
    far = along_x(mine)
    made = features_call(2, 0, 1, inputs, gains, w_qkv, omega, made, in_hbm((held,)) + in_vmem((mine,)))
    far, got = gate(far, made[0]), gate(got, made[0])
    first = (near, far, swap(far, CORE))
    local = gate(made[4], far, got)
    near = swap(local, CORE)
    mine = chip_half(local, near)
    held = jnp.concatenate([held, got])
    got = swap(held, GATHER[3])
    far = along_x(mine)
    beside = swap(held, CORE)
    qkv, phi_q, phi_k, h1 = made[:4]
    made = mix_call(
        0, 2, inputs, gains, w_out, phi_q, phi_k, qkv, (first, 0, 2 * pairs), None, hd, in_hbm((held,)) + in_vmem((mine,))
    )
    far = gate(far, made[0])
    got, beside = gate(got, far), gate(beside, far)
    second = (near, far, swap(far, CORE))
    made = mix_call(
        2, 1, inputs, gains, w_out, phi_q, phi_k, qkv, (second, 0, pairs), made, hd, in_hbm((got,))
    )
    weights = [beside, gate(swap(got, CORE), made[0]), held, got]
    mixed, rden, x1, h2 = made
    carried = [(first, 0, 2 * pairs), (first, 1, 2 * pairs), (second, 0, pairs)]

    act, pre, g1, ga, gain, side, local = ffn_call(
        h2, cotangent, x1, mixed, rden, phi_q, w_out, gains, weights, hd
    )
    near = swap(local, CORE)
    mine = chip_half(local, near)
    far = along_x(mine)
    send, low = ffn_weight_call(act, pre, cotangent, h2, gain, mixed, ga, n_shard // 2, True, (mine,))
    far = gate(far, low)
    other = swap(far, CORE)
    send = gate(send, other)
    later = (near, far, other)

    def back(b, before, *after):
        return attention_back_call(
            b, side, phi_q, phi_k, qkv, omega, carried[b], (later, b, batch * pairs), before, in_hbm(after)
        )

    def into(b, members, before, *after):
        return inputs_back_call(b, members, grads, w_qkv, inputs, g1, gains, before, in_hbm(after))

    def onto(b, before, *after):
        return outputs_call(b, act, x1, weights, before, in_hbm(after))

    got = swap(send, CORE)
    made = back(0, None)
    got = gate(got, made[0])
    low, high = split_sum(low, got)
    got = swap(high, GATHER[3])
    made = back(1, made, high)
    onto_made = onto(0, None, made[0])
    low, high = next_halves(low, gate(got, onto_made[0]), n_shard, 8, False)
    got = swap(high, GATHER[2])
    made = back(2, made, high)
    low, high = next_halves(low, gate(got, made[0]), n_shard, 4, True)
    got = swap(high, GATHER[1])
    (grads,) = made
    late = qkv_weight_call(h1, grads, True, (high,))

    send, *keep = [a.reshape(a.shape[:-3] + (-1, model)) for a in late]
    keep = plane_sums(swap(send, CORE), keep)
    far = [swap(keep[plane], PLANE[plane - 1]) for plane in (1, 2, 3)]
    into_made = into(0, 2, None, *keep)
    far = [gate(a, into_made[0], close=True) for a in far]
    got = gate(got, *far)
    n_late = keep[0].shape[0]
    (keep,) = sums([keep[0]] + far, [[((0, 1, 2, 3), 0, n_late)]], None, (1, 2, 3))
    line = swap(keep, LINE[0])
    low, high = next_halves(low, got, n_shard, 2, True)
    last = swap(high, GATHER[0])
    into_made = into(2, 1, into_made, keep, high)
    line = gate(line, into_made[0], close=True)
    last = gate(last, line)
    (keep,) = sums([keep, line], [[((0, 1), 0, n_late)]], None, (1,))
    got = swap(keep, LINE[1])
    onto_made = onto(1, onto_made, keep)
    grad_ffn, piece = sums(
        [low, last], [[((0, 1), 0, n_shard)], [((0, 1), n_shard, n_piece)]], [f32, bf16], (1,)
    )
    (keep,) = sums(
        [keep, gate(got, onto_made[0], close=True), piece], [[((0, 1), 0, n_late), ((2,), 0, n_piece)]], None, (1,)
    )
    got = [swap(keep, masks) for masks in PLANE]
    beside = swap(keep, CORE)
    onto_made = onto(2, onto_made, keep)
    near = [keep] + [gate(a, onto_made[0], close=True) for a in got]
    far = [gate(beside, onto_made[0], close=True)] + [swap(a, CORE) for a in near[1:]]
    grad_wqkv, grad_wout, grad_gains = assemble_call(near + far, w_qkv, gains)
    return onto_made[0], into_made[0], grad_gains, grad_wqkv, grad_wout, grad_ffn


def plain(inputs, gains, w_qkv, w_out, shard, omega, cotangent):
    batch, rows, model = inputs.shape
    heads, hd, _ = omega.shape
    pairs = heads // 2
    pair = lax.all_gather(shard, AXES, axis=1, tiled=True)
    hidden = pair.shape[1]
    unit = min(256, hidden)
    weights = [jnp.swapaxes(pair.reshape(2, hidden // unit, unit, model), 0, 1)]
    made = None
    for b in range(batch):
        made = features_call(b, b, batch, inputs, gains, w_qkv, omega, made)
    qkv, phi_q, phi_k, h1, local = made
    sums = all_states(local, False)
    mixed, rden, x1, h2 = mix_call(
        0, batch, inputs, gains, w_out, phi_q, phi_k, qkv, (sums, 0, batch * pairs), None, hd
    )
    act, pre, g1, ga, gain, side, local = ffn_call(
        h2, cotangent, x1, mixed, rden, phi_q, w_out, gains, weights, hd
    )
    later = all_states(local, True)
    both, grad_wout = ffn_weight_call(act, pre, cotangent, h2, gain, mixed, ga, unit, False)
    both = jnp.swapaxes(both.reshape(-1, 2, unit, model), 0, 1).reshape(2, -1, model)
    grad_ffn = lax.psum_scatter(both, AXES, scatter_dimension=1, tiled=True).astype(f32)
    made = None
    for b in range(batch):
        spot = (b, batch * pairs)
        made = attention_back_call(b, side, phi_q, phi_k, qkv, omega, (sums,) + spot, (later,) + spot, made)
    (grads,) = made
    (grad_wqkv,) = qkv_weight_call(h1, grads, False)
    into_made = onto_made = None
    for b in range(batch):
        into_made = inputs_back_call(b, 1, grads, w_qkv, inputs, g1, gains, into_made)
        onto_made = outputs_call(b, act, x1, weights, onto_made)
    grad_wqkv, grad_wout, gain = lax.psum((grad_wqkv, grad_wout, gain), AXES)
    grad_gains = pl.pallas_call(
        gains_kernel,
        out_shape=jax.ShapeDtypeStruct(gains.shape, f32),
        compiler_params=params(),
    )(grad_wqkv, gain, w_qkv, gains)
    return onto_made[0], into_made[0], grad_gains, grad_wqkv, grad_wout, grad_ffn


def on_device(inputs, gains, w_qkv, w_out, ffn_weight, omega, cotangent):
    fast = lax.axis_size("dp") == 8 and lax.axis_size("seq") == 4 and inputs.shape[0] == 3
    outputs, grad_inputs, *grads = (planned if fast else plain)(
        inputs, gains[0], w_qkv[0], w_out[0], ffn_weight[0], jnp.swapaxes(omega[0], 1, 2), cotangent
    )
    grad_gains, grad_wqkv, grad_wout, grad_ffn = grads
    grad_ffn = grad_ffn.reshape(ffn_weight.shape)
    return (outputs, grad_inputs, grad_gains[None], grad_wqkv[None], grad_wout[None], grad_ffn)


def solution(mesh):
    in_specs = (
        P("dp", "seq", None),
        P(),
        P(),
        P(),
        P(None, None, ("dp", "seq"), None),
        P(),
        P("dp", "seq", None),
    )
    out_specs = (
        P("dp", "seq", None),
        P("dp", "seq", None),
        P(),
        P(),
        P(),
        P(None, None, ("dp", "seq"), None),
    )
    return jax.shard_map(
        on_device, mesh=mesh, in_specs=in_specs, out_specs=out_specs, check_vma=False
    )
```

```python
import functools
import math

import jax
import jax.numpy as jnp
from jax import lax
from jax.experimental import pallas as pl
from jax.experimental.pallas import tpu as pltpu
from jax.sharding import PartitionSpec as P

epsilon = 1e-05
bf16 = jnp.bfloat16
f32 = jnp.float32
AXES = ("dp", "seq")
MIB = 2**20


def nn(a, b):
    return lax.dot_general(a, b, (((1,), (0,)), ((), ())), preferred_element_type=f32)


def nt(a, b):
    return lax.dot_general(a, b, (((1,), (1,)), ((), ())), preferred_element_type=f32)


def tn(a, b):
    return lax.dot_general(a, b, (((0,), (0,)), ((), ())), preferred_element_type=f32)


def lanes_of(shape):
    return lax.broadcasted_iota(jnp.int32, shape, len(shape) - 1)


def params(mib=62):
    return pltpu.CompilerParams(vmem_limit_bytes=mib * MIB)


def cost(flops, nbytes, trans=0):
    return pl.CostEstimate(flops=int(flops), bytes_accessed=int(nbytes), transcendentals=int(trans))


def in_hbm(arrays):
    return [pltpu.with_memory_space_constraint(a, pltpu.HBM) for a in arrays]


def in_vmem(arrays):
    return [pltpu.with_memory_space_constraint(a, pltpu.VMEM) for a in arrays]


def const_block(shape):
    return pl.BlockSpec(shape, lambda *_: (0,) * len(shape))


def stacked_call(kernel, grid, in_specs, out_specs, out_shapes, stacked, before, args, scratch, estimate, after=(), mib=62):
    n_in = len(args)
    aliases = {}
    extra = list(after)
    if before is not None:
        for at, (flag, buffer) in enumerate(zip(stacked, before)):
            if flag:
                aliases[n_in + len(extra)] = at
                extra += in_hbm((buffer,))
    n_extra = len(extra)

    def body(*refs):
        kernel(*refs[:n_in], *refs[n_in + n_extra :])

    return pl.pallas_call(
        body,
        grid=grid,
        in_specs=list(in_specs) + [pl.BlockSpec(memory_space=pl.ANY)] * n_extra,
        out_specs=out_specs,
        out_shape=out_shapes,
        scratch_shapes=scratch,
        input_output_aliases=aliases,
        compiler_params=params(mib),
        cost_estimate=estimate,
    )(*args, *extra)


def normed(values):
    center = values - jnp.mean(values, axis=-1, keepdims=True)
    spread = jnp.mean(center * center, axis=-1, keepdims=True)
    scale = lax.rsqrt(spread + epsilon)
    return center * scale, scale


def norm_back(grad, xhat, scale, gain):
    gy = grad * gain
    return scale * (
        gy - jnp.mean(gy, axis=-1, keepdims=True) - xhat * jnp.mean(gy * xhat, axis=-1, keepdims=True)
    )


def causal_tile(rows):
    return lax.broadcasted_iota(jnp.int32, (rows, rows), 0) >= lax.broadcasted_iota(
        jnp.int32, (rows, rows), 1
    )


def feature_weights(omega, odd):
    ones = jnp.full(omega.shape, -1.0, omega.dtype)
    zeros = jnp.zeros_like(ones)
    parts = [ones, omega, zeros, ones] if odd else [omega, ones, ones, zeros]
    return jnp.concatenate(parts, axis=0)


PER = 2
BACK_PER = 1


def features_kernel(hd, x_ref, gains_ref, w_ref, omega_ref, qkv_ref, phiq_ref, phik_ref, h1_ref, state_ref, qkv_scr):
    step = pl.program_id(0)
    width = 2 * hd
    rows, model = x_ref.shape[1:]
    s = hd ** (-0.25)
    feats = omega_ref.shape[2]
    per = omega_ref.shape[0] // 2

    @pl.when(step == 0)
    def _():
        xhat, _ = normed(x_ref[0].astype(f32))
        hidden = (xhat * gains_ref[0:1, :]).astype(bf16)
        h1_ref[0] = hidden
        for part in range(3):
            cols = slice(part * model, (part + 1) * model)
            made = nn(hidden, w_ref[:, cols]).astype(bf16)
            qkv_ref[0, :, cols] = made
            qkv_scr[part] = made

    low = lanes_of((rows, width)) < hd
    lefts = []
    for at in range(per):
        column = pl.ds(pl.multiple_of((step * per + at) * width, width), width)
        for part in range(2):
            points = qkv_scr[part, :, column].astype(f32)
            energy = points * points * (0.5 * s)
            high = energy.astype(bf16).astype(f32)
            rest = (energy - high).astype(bf16)
            turned = pltpu.roll(high, hd, 1)
            for odd in range(2):
                first = jnp.where(low, turned, points) if odd else jnp.where(low, points, turned)
                lefts.append((at, part, odd, jnp.concatenate([first.astype(bf16), rest], axis=1)))
    made = {}
    for at, part, odd, left in lefts:
        proj = nn(left, feature_weights(omega_ref[2 * at + odd], odd))
        phi = jnp.exp2(proj * (s * math.log2(math.e)) - 0.5 * math.log2(feats)).astype(bf16)
        head = 2 * at + odd
        (phik_ref if part else phiq_ref)[0, :, head * feats : (head + 1) * feats] = phi
        if part:
            made[at, odd] = phi
    for at in range(per):
        column = pl.ds(pl.multiple_of((step * per + at) * width, width), width)
        values = qkv_scr[2, :, column]
        state_ref[at, 0:hd, :] = tn(values, made[at, 0])[0:hd].astype(bf16)
        state_ref[at, hd:width, :] = tn(values, made[at, 1])[hd:width].astype(bf16)
        sums = jnp.concatenate(
            [
                jnp.sum(made[at, 0].astype(f32), axis=0, keepdims=True),
                jnp.sum(made[at, 1].astype(f32), axis=0, keepdims=True),
                jnp.zeros((14, feats), f32),
            ],
            axis=0,
        )
        state_ref[at, width : width + 16, :] = sums.astype(bf16)


def features_call(index, at, count, inputs, gains, w_qkv, omega, before, after=()):
    batch, rows, model = inputs.shape
    heads, hd, feats = omega.shape
    pairs = heads // 2
    per = pairs
    steps = pairs // per
    n_rows = 2 * hd + 16
    phi_spec = pl.BlockSpec((1, rows, 2 * per * feats), lambda g: (index, 0, g))
    return stacked_call(
        functools.partial(features_kernel, hd),
        (steps,),
        [
            pl.BlockSpec((1, rows, model), lambda g: (index, 0, 0)),
            const_block(gains.shape),
            const_block(w_qkv.shape),
            pl.BlockSpec((2 * per, hd, feats), lambda g: (g, 0, 0)),
        ],
        [
            pl.BlockSpec((1, rows, 3 * model), lambda g: (index, 0, 0)),
            phi_spec,
            phi_spec,
            pl.BlockSpec((1, rows, model), lambda g: (index, 0, 0)),
            pl.BlockSpec((per, n_rows, feats), lambda g: (at * steps + g, 0, 0)),
        ],
        [
            jax.ShapeDtypeStruct((batch, rows, 3 * model), bf16),
            jax.ShapeDtypeStruct((batch, rows, heads * feats), bf16),
            jax.ShapeDtypeStruct((batch, rows, heads * feats), bf16),
            jax.ShapeDtypeStruct((batch, rows, model), bf16),
            jax.ShapeDtypeStruct((count * pairs, n_rows, feats), bf16),
        ],
        (True, True, True, True, at > 0),
        before,
        (inputs, gains, w_qkv, omega),
        [pltpu.VMEM((3, rows, model), bf16)],
        cost(2 * rows * model * 3 * model + 4 * heads * rows * 256 * feats, 9 * MIB, 2 * rows * heads * feats),
        after,
    )


def state_block(state_refs, backward, at, step, per, hd, first, count):
    if len(state_refs) == 1:
        total = state_refs[0][at].astype(f32)
    else:
        near, got, other = state_refs
        seq = lax.axis_index("seq")
        core = lax.rem(seq, 2)
        own_half = (first + step * per + at) // (count // 2) == core
        beyond = (seq // 2) == (0 if backward else 1)
        beside = core == (0 if backward else 1)
        total = jnp.where(own_half, got[at].astype(f32), other[at].astype(f32))
        total = jnp.where(beyond, total, 0.0) + jnp.where(beside, near[at].astype(f32), 0.0)
    feats = total.shape[-1]
    width = 2 * hd
    zeros = jnp.zeros((hd, feats), bf16)
    low = total.astype(bf16)
    even_norm = jnp.broadcast_to(total[width : width + 1], (hd, feats)).astype(bf16)
    odd_norm = jnp.broadcast_to(total[width + 1 : width + 2], (hd, feats)).astype(bf16)
    even = jnp.concatenate([low[0:hd], zeros, even_norm, zeros], axis=0)
    odd = jnp.concatenate([zeros, low[hd:width], zeros, odd_norm], axis=0)
    return even, odd


def state_specs(carried, pairs, per):
    states, at, count = carried
    shape = (per,) + states[0].shape[1:]
    first = at * pairs // per
    specs = [pl.BlockSpec(shape, lambda g: (first + g, 0, 0))]
    if len(states) > 1:
        specs += [pl.BlockSpec(shape, lambda g: (lax.rem(first + g, count // 2 // per), 0, 0))] * 2
    return specs


def mix_kernel(hd, n_states, first, count, tile, *refs):
    x_ref, gains_ref, wout_ref, phiq_ref, phik_ref, v_ref = refs[:6]
    state_refs = refs[6 : 6 + n_states]
    mixed_ref, rden_ref, x1_ref, h2_ref, mixed_scr = refs[6 + n_states :]
    step = pl.program_id(0)
    width = 2 * hd
    rows, model = x_ref.shape[1:]
    steps = model // width // PER
    feats = phiq_ref.shape[-1] // (2 * PER)
    causal = causal_tile(tile)
    low = lanes_of((rows, width)) < hd
    ones = jnp.where(low, 1.0, 0.0)
    spans = [(slice(at * tile, (at + 1) * tile), (at + 1) * tile) for at in range(rows // tile)]
    scores = {}
    for at in range(PER):
        for odd in range(2):
            cols = slice((2 * at + odd) * feats, (2 * at + odd + 1) * feats)
            for t, (here, end) in enumerate(spans):
                scores[at, odd, t] = masked(nt(phiq_ref[0, here, cols], phik_ref[0, 0:end, cols]), causal, t, tile)
    for at in range(PER):
        even, odd = state_block(state_refs, False, at, step, PER, hd, first, count)
        both_state = jnp.concatenate([even, odd], axis=1)
        values = v_ref[0, :, at * width : (at + 1) * width].astype(f32)
        sides = [
            jnp.concatenate([jnp.where(low, values, 0.0), ones], axis=1).astype(bf16),
            jnp.concatenate([jnp.where(low, 0.0, values), 1.0 - ones], axis=1).astype(bf16),
        ]
        cols = slice(2 * at * feats, 2 * (at + 1) * feats)
        lanes = slice(at * width, (at + 1) * width)
        column = pl.ds(pl.multiple_of((lax.rem(step, steps) * PER + at) * width, width), width)
        for t, (here, end) in enumerate(spans):
            total = nt(phiq_ref[0, here, cols], both_state)
            for odd in range(2):
                total = total + nn(scores[at, odd, t], sides[odd][0:end])
            rden = 1.0 / total[:, width:]
            mixed = (total[:, :width] * rden).astype(bf16)
            rden_ref[0, here, lanes] = rden
            mixed_ref[0, here, lanes] = mixed
            mixed_scr[here, column] = mixed

    @pl.when(lax.rem(step, steps) == steps - 1)
    def _():
        x1 = x_ref[0].astype(f32) + nn(mixed_scr[...], wout_ref[...])
        x1_ref[0] = x1
        xhat, _ = normed(x1)
        h2_ref[0] = (xhat * gains_ref[1:2, :]).astype(bf16)


def masked(made, causal, at, tile):
    last = jnp.where(causal, made[:, at * tile :], 0.0)
    if at > 0:
        last = jnp.concatenate([made[:, : at * tile], last], axis=1)
    return last.astype(bf16)


def mix_call(index, members, inputs, gains, w_out, phi_q, phi_k, qkv, carried, before, hd, after=()):
    batch, rows, model = inputs.shape
    width = 2 * hd
    pairs = model // width
    steps = pairs // PER
    states, at, count = carried
    heads = 2 * pairs
    feats = phi_q.shape[-1] // heads
    tile = min(256, rows)
    whole = pl.BlockSpec((1, rows, model), lambda g: (index + g // steps, 0, 0))
    narrow = pl.BlockSpec((1, rows, PER * width), lambda g: (index + g // steps, 0, lax.rem(g, steps)))
    phi_spec = pl.BlockSpec((1, rows, 2 * PER * feats), lambda g: (index + g // steps, 0, lax.rem(g, steps)))
    return stacked_call(
        functools.partial(mix_kernel, hd, len(states), at * pairs, count, tile),
        (members * steps,),
        [
            whole,
            const_block(gains.shape),
            const_block(w_out.shape),
            phi_spec,
            phi_spec,
            pl.BlockSpec((1, rows, PER * width), lambda g: (index + g // steps, 0, 2 * steps + lax.rem(g, steps))),
        ]
        + state_specs(carried, pairs, PER),
        [narrow, narrow, whole, whole],
        [
            jax.ShapeDtypeStruct((batch, rows, model), bf16),
            jax.ShapeDtypeStruct((batch, rows, model), f32),
            jax.ShapeDtypeStruct((batch, rows, model), f32),
            jax.ShapeDtypeStruct((batch, rows, model), bf16),
        ],
        (True,) * 4,
        before,
        (inputs, gains, w_out, phi_q, phi_k, qkv) + tuple(states),
        [pltpu.VMEM((rows, model), bf16)],
        cost(members * (heads * 2 * rows * rows * 512 + 2 * rows * model * model), members * 9 * MIB),
        after,
    )


def ffn_kernel(groups, batch, hd, *refs):
    h2_ref, gf_ref, wout_ref, gains_ref = refs[:4]
    late_any = refs[4:8]
    weights = refs[8 : 8 + groups]
    act_ref, pre_ref, g1_any, ga_any, gain_ref, side_any, gstate_ref = refs[8 + groups : 15 + groups]
    up_scr, down_scr, pre_scr, x1_scr, mixed_scr, rden_scr, phiq_scr, g1_scr, ga_scr, side_scr = refs[
        15 + groups : 25 + groups
    ]
    sems, late_sems, out_sems = refs[25 + groups :]
    step = pl.program_id(0)
    n_blocks = pl.num_programs(0) - 1
    each = n_blocks // groups
    block = act_ref.shape[-1]
    rows = h2_ref.shape[1]
    model = h2_ref.shape[2]
    shards, unit = up_scr.shape[1:3]
    taken = block // unit
    started = []
    for group in range(groups):
        started.append(pltpu.make_async_copy(weights[group].at[:, 0], up_scr.at[group], sems.at[2 * group]))
        started.append(pltpu.make_async_copy(weights[group].at[:, 1], down_scr.at[group], sems.at[2 * group + 1]))
    late = [
        pltpu.make_async_copy(src, dst, late_sems.at[at])
        for at, (src, dst) in enumerate(zip(late_any, (x1_scr, mixed_scr, rden_scr, phiq_scr)))
    ]
    leaving = [
        [
            pltpu.make_async_copy(scr.at[b], out.at[b], out_sems.at[b, at])
            for at, (scr, out) in enumerate(((g1_scr, g1_any), (ga_scr, ga_any), (side_scr, side_any)))
        ]
        for b in range(batch)
    ]

    @pl.when(step == 0)
    def _():
        for copy in started:
            copy.start()

    @pl.when(step == n_blocks // 2)
    def _():
        for copy in late:
            copy.start()

    for group in range(groups):

        @pl.when(step == group * each)
        def _():
            started[2 * group].wait()
            started[2 * group + 1].wait()

    @pl.when(step < n_blocks)
    def _():
        here = pl.ds(pl.multiple_of(lax.rem(step, each) * taken, taken), taken)
        up = up_scr[step // each, here].reshape(block, model)
        down = down_scr[step // each, here].reshape(block, model)
        cols = pl.ds(pl.multiple_of(step * block, block), block)
        for b in range(batch):
            pre = nt(h2_ref[b], up)
            part = 0.5 * lax.erf(pre * math.sqrt(0.5)) + 0.5
            act_ref[b] = (pre * part).astype(bf16)
            slope = part + pre * (
                jnp.exp2(pre * pre * (-0.5 * math.log2(math.e))) * (1.0 / math.sqrt(2.0 * math.pi))
            )
            grad_pre = (nt(gf_ref[b], down) * slope).astype(bf16)
            pre_ref[b] = grad_pre
            pre_scr[b, :, cols] = grad_pre

    @pl.when(step == n_blocks)
    def _():
        width = 2 * hd
        pairs = model // width
        feats = phiq_scr.shape[-1] // (2 * pairs)
        up = up_scr[...].reshape(n_blocks * block, model)
        same = lax.div(lax.rem(lax.broadcasted_iota(jnp.int32, (2 * width, width), 0), width), hd) == lax.div(
            lax.broadcasted_iota(jnp.int32, (2 * width, width), 1), hd
        )
        minus = jnp.where(same, -1.0, 0.0).astype(bf16)
        inner = lax.rem(lanes_of((rows, width)), hd)
        grads = [nn(pre_scr[b], up) for b in range(batch)]
        for copy in late:
            copy.wait()
        gain = jnp.zeros((1, model), f32)
        for b in range(batch):
            xhat, scale = normed(x1_scr[b])
            g1 = gf_ref[b].astype(f32) + norm_back(grads[b], xhat, scale, gains_ref[1:2, :])
            gain = gain + jnp.sum(grads[b] * xhat, axis=0, keepdims=True)
            g1_scr[b] = g1
            ga_scr[b] = g1.astype(bf16)
            leaving[b][0].start()
            leaving[b][1].start()
        gain_ref[...] = jnp.broadcast_to(gain, gain_ref.shape)
        for b in range(batch):
            x1_scr[b] = nt(ga_scr[b], wout_ref[...])

        def sides(b, carry):
            gn_full = x1_scr[b] * rden_scr[b]
            gn_low = gn_full.astype(bf16)
            product = gn_full * mixed_scr[b].astype(f32)
            high = product.astype(bf16)
            rest = (product - high.astype(f32)).astype(bf16)
            made = []
            for at in range(pairs):
                cols = slice(at * width, (at + 1) * width)
                gd = nn(jnp.concatenate([high[:, cols], rest[:, cols]], axis=1), minus)
                gd_high = gd.astype(bf16).astype(f32)
                gdx = jnp.where(inner == 0, gd_high, jnp.where(inner == 1, gd - gd_high, 0.0))
                made.append(jnp.concatenate([gn_low[:, cols], gdx.astype(bf16)], axis=1))
            for at in range(pairs):
                side_scr[b, at] = made[at]
            found = [
                [tn(made[at], phiq_scr[b, :, (2 * at + odd) * feats : (2 * at + odd + 1) * feats]) for odd in range(2)]
                for at in range(pairs)
            ]
            for at, (even, odd) in enumerate(found):
                to = b * pairs + at
                gstate_ref[to, 0:hd] = even[0:hd].astype(bf16)
                gstate_ref[to, hd:width] = odd[hd:width].astype(bf16)
                norms = jnp.concatenate(
                    [
                        even[width : width + 1] + even[width + 1 : width + 2],
                        odd[width + hd : width + hd + 1] + odd[width + hd + 1 : width + hd + 2],
                        jnp.zeros((14, feats), f32),
                    ],
                    axis=0,
                )
                gstate_ref[to, width : width + 16] = norms.astype(bf16)
            return carry

        lax.fori_loop(0, batch, sides, 0)
        for b in range(batch):
            leaving[b][2].start()
        for copies in leaving:
            for copy in copies:
                copy.wait()


def ffn_call(h2, gf, x1, mixed, rden, phi_q, w_out, gains, weights, hd):
    batch, rows, model = h2.shape
    groups = len(weights)
    shards, _, unit, _ = weights[0].shape
    hidden = groups * shards * unit
    block = min(512, shards * unit)
    n_blocks = hidden // block
    pairs = model // (2 * hd)
    feats = phi_q.shape[-1] // (2 * pairs)
    n_rows = 2 * hd + 16
    wide = pl.BlockSpec((batch, rows, block), lambda j: (0, 0, jnp.minimum(j, n_blocks - 1)))
    anywhere = pl.BlockSpec(memory_space=pl.ANY)
    scratch = (groups, shards, unit, model)
    return pl.pallas_call(
        functools.partial(ffn_kernel, groups, batch, hd),
        grid=(n_blocks + 1,),
        in_specs=[
            const_block(h2.shape),
            const_block(gf.shape),
            const_block(w_out.shape),
            const_block(gains.shape),
        ]
        + [anywhere] * (4 + groups),
        out_specs=[
            wide,
            wide,
            anywhere,
            anywhere,
            const_block((16, model)),
            anywhere,
            const_block((batch * pairs, n_rows, feats)),
        ],
        out_shape=[
            jax.ShapeDtypeStruct((batch, rows, hidden), bf16),
            jax.ShapeDtypeStruct((batch, rows, hidden), bf16),
            jax.ShapeDtypeStruct((batch, rows, model), f32),
            jax.ShapeDtypeStruct((batch, rows, model), bf16),
            jax.ShapeDtypeStruct((16, model), f32),
            jax.ShapeDtypeStruct((batch, pairs, rows, 4 * hd), bf16),
            jax.ShapeDtypeStruct((batch * pairs, n_rows, feats), bf16),
        ],
        scratch_shapes=[
            pltpu.VMEM(scratch, bf16),
            pltpu.VMEM(scratch, bf16),
            pltpu.VMEM((batch, rows, hidden), bf16),
            pltpu.VMEM((batch, rows, model), f32),
            pltpu.VMEM((batch, rows, model), bf16),
            pltpu.VMEM((batch, rows, model), f32),
            pltpu.VMEM(phi_q.shape, bf16),
            pltpu.VMEM((batch, rows, model), f32),
            pltpu.VMEM((batch, rows, model), bf16),
            pltpu.VMEM((batch, pairs, rows, 4 * hd), bf16),
            pltpu.SemaphoreType.DMA((2 * groups,)),
            pltpu.SemaphoreType.DMA((4,)),
            pltpu.SemaphoreType.DMA((batch, 3)),
        ],
        compiler_params=params(),
        cost_estimate=cost(6 * batch * rows * hidden * model, 30 * MIB, 2 * batch * rows * hidden),
    )(h2, gf, w_out, gains, x1, mixed, rden, phi_q, *weights)


def row_owner(far, y_bit, x_bit):
    seq = lax.axis_index("seq")
    y, x, core = lax.rem(lax.axis_index("dp"), 2), seq // 2, lax.rem(seq, 2)
    return (core ^ far) * 4 + (y ^ y_bit) * 2 + (x ^ x_bit)


def plane_of(far, first, second):
    turned = (lax.rem(lax.axis_index("seq"), 2) ^ far) == 1
    return jnp.where(turned, second, first), jnp.where(turned, first, second)


EXTRA = 16


def ffn_weight_kernel(unit, n_pieces, n_after, *refs):
    act_ref, pre_ref, gf_ref, h2_ref, gain_ref, mixed_any, ga_any = refs[:7]
    outs = refs[7 + n_after : 9 + n_after]
    mixed_scr, ga_scr, sum_scr, row_scr, piece_scr, in_sems, row_sems, piece_sems = refs[9 + n_after :]
    step = pl.program_id(0)
    n_blocks = pl.num_programs(0)
    batch, rows, block = act_ref.shape
    model = gf_ref.shape[2]
    n_rows = row_scr.shape[1]
    slot = lax.rem(step, 2)
    copies = [
        pltpu.make_async_copy(mixed_any, mixed_scr, in_sems.at[0]),
        pltpu.make_async_copy(ga_any, ga_scr, in_sems.at[1]),
    ]

    def row_copy(out, row, slot):
        row = pl.multiple_of(row, 16)
        return pltpu.make_async_copy(row_scr.at[slot], out.at[pl.ds(row, n_rows)], row_sems.at[slot])

    @pl.when(step == 0)
    def _():
        for copy in copies:
            copy.start()

    down = tn(act_ref[...].reshape(batch * rows, block), gf_ref[...].reshape(batch * rows, model)).astype(bf16)
    up = tn(pre_ref[...].reshape(batch * rows, block), h2_ref[...].reshape(batch * rows, model)).astype(bf16)

    @pl.when(step >= 2)
    def _():
        row_copy(outs[0], 0, slot).wait()

    for at in range(block // unit):
        here = slice(at * unit, (at + 1) * unit)
        row_scr[slot, 2 * at * unit : (2 * at + 1) * unit] = up[here]
        row_scr[slot, (2 * at + 1) * unit : (2 * at + 2) * unit] = down[here]
    if n_pieces:
        half = n_blocks // 2
        quarter = n_blocks // 4
        held = outs[0].shape[0] // 2
        inside = lax.rem(step, half)
        row = (inside // quarter) * held + lax.rem(inside, quarter) * n_rows
        for at in range(2):

            @pl.when(step // half == at)
            def _():
                row_copy(outs[at], row, slot).start()
    else:
        row_copy(outs[0], step * n_rows, slot).start()

    def piece_copies():
        if not n_pieces:
            return [pltpu.make_async_copy(sum_scr, outs[1], piece_sems.at[0])]
        held = outs[0].shape[0] // 2
        n_piece = piece_scr.shape[1]
        return [
            pltpu.make_async_copy(
                piece_scr.at[2 * at + first],
                outs[at].at[(first + 1) * held - n_piece : (first + 1) * held],
                piece_sems.at[2 * at + first],
            )
            for at in range(2)
            for first in range(2)
        ]

    @pl.when(step == n_blocks // 2)
    def _():
        for copy in copies:
            copy.wait()
        sum_scr[...] = tn(
            mixed_scr[...].reshape(batch * rows, model), ga_scr[...].reshape(batch * rows, model)
        )
        if n_pieces:
            piece = model // 8
            gain = gain_ref[...].astype(bf16)
            for at in range(2):
                for first in range(2):
                    for second in range(2):
                        owner = row_owner(1 - at, *plane_of(1 - at, first, second))
                        taken = sum_scr[pl.ds(pl.multiple_of(owner * piece, piece), piece), :].astype(bf16)
                        row = second * (piece + EXTRA)
                        piece_scr[2 * at + first, row : row + piece] = taken
                        piece_scr[2 * at + first, row + piece : row + piece + EXTRA] = gain
        for copy in piece_copies():
            copy.start()

    @pl.when(step == n_blocks - 1)
    def _():
        row_copy(outs[0], 0, 1 - slot).wait()
        row_copy(outs[0], 0, slot).wait()
        for copy in piece_copies():
            copy.wait()


def ffn_weight_call(act, pre, gf, h2, gain, mixed, ga, unit, fast, after=()):
    batch, rows, model = h2.shape
    hidden = act.shape[-1]
    block = min(512, hidden)
    n_blocks = hidden // block
    wide = pl.BlockSpec((batch, rows, block), lambda j: (0, 0, j))
    n_piece = 2 * (model // 8 + EXTRA)
    if fast:
        out_shapes = [jax.ShapeDtypeStruct((hidden + 2 * n_piece, model), bf16)] * 2
    else:
        out_shapes = [jax.ShapeDtypeStruct((2 * hidden, model), bf16), jax.ShapeDtypeStruct((model, model), f32)]
    anywhere = pl.BlockSpec(memory_space=pl.ANY)
    return pl.pallas_call(
        functools.partial(ffn_weight_kernel, unit, 8 if fast else 0, len(after)),
        grid=(n_blocks,),
        in_specs=[wide, wide, const_block(gf.shape), const_block(h2.shape), const_block(gain.shape), anywhere, anywhere]
        + [anywhere] * len(after),
        out_specs=[anywhere] * 2,
        out_shape=out_shapes,
        scratch_shapes=[
            pltpu.VMEM(mixed.shape, bf16),
            pltpu.VMEM(ga.shape, bf16),
            pltpu.VMEM((model, model), f32),
            pltpu.VMEM((2, 2 * block, model), bf16),
            pltpu.VMEM((4, n_piece, model), bf16),
            pltpu.SemaphoreType.DMA((2,)),
            pltpu.SemaphoreType.DMA((2,)),
            pltpu.SemaphoreType.DMA((4,)),
        ],
        compiler_params=params(),
        cost_estimate=cost(4 * batch * rows * hidden * model, 22 * MIB),
    )(act, pre, gf, h2, gain, mixed, ga, *in_hbm(after))


def attention_back_kernel(hd, n_prev, n_later, spots, tile, *refs):
    side_ref, phiq_ref, phik_ref, q_ref, k_ref, v_ref, omega_ref = refs[:7]
    prev_refs = refs[7 : 7 + n_prev]
    later_refs = refs[7 + n_prev : 7 + n_prev + n_later]
    (out_ref,) = refs[7 + n_prev + n_later :]
    step = pl.program_id(0)
    width = 2 * hd
    rows = q_ref.shape[1]
    feats = phiq_ref.shape[-1] // (2 * BACK_PER)
    tiles = rows // tile
    s = hd ** (-0.25)
    low = lanes_of((rows, width)) < hd
    low_tile = low[0:tile]
    inner = lax.rem(lanes_of((rows, width)), hd)
    ones = jnp.where(inner < 2, 1.0, 0.0)
    one = jnp.where(inner == 0, 1.0, 0.0).astype(bf16)
    causal = causal_tile(tile)
    spans = [(slice(t * tile, (t + 1) * tile), (t + 1) * tile) for t in range(tiles)]
    heads = [(at, odd) for at in range(BACK_PER) for odd in range(2)]
    each = [(at, odd, t) for at, odd in heads for t in range(tiles)]
    cols = {(at, odd): slice((2 * at + odd) * feats, (2 * at + odd + 1) * feats) for at, odd in heads}
    lanes = [slice(at * width, (at + 1) * width) for at in range(BACK_PER)]

    def column(made, at, odd, t):
        return jnp.concatenate([made[at, odd, i][:, t * tile : (t + 1) * tile] for i in range(t, tiles)], axis=0)

    made, scores, weights, value_sides = {}, {}, {}, {}
    for at in range(BACK_PER):
        values = v_ref[0, :, lanes[at]].astype(f32)
        value_sides[at, 0] = jnp.concatenate(
            [jnp.where(low, values, 0.0), jnp.where(low, ones, 0.0)], axis=1
        ).astype(bf16)
        value_sides[at, 1] = jnp.concatenate(
            [jnp.where(low, 0.0, values), jnp.where(low, 0.0, ones)], axis=1
        ).astype(bf16)
    for at, odd, t in each:
        here, end = spans[t]
        made[at, odd, t] = masked(nt(side_ref[0, at, here], value_sides[at, odd][0:end]), causal, t, tile)
    for at, odd, t in each:
        here, end = spans[t]
        scores[at, odd, t] = masked(
            nt(phiq_ref[0, here, cols[at, odd]], phik_ref[0, 0:end, cols[at, odd]]), causal, t, tile
        )
    prev = [state_block(prev_refs, False, at, step, BACK_PER, hd, *spots[0]) for at in range(BACK_PER)]
    later = [state_block(later_refs, True, at, step, BACK_PER, hd, *spots[1]) for at in range(BACK_PER)]
    for at, odd in heads:
        weights[at, odd] = feature_weights(omega_ref[2 * at + odd], odd)
    proj_q, proj_k = {}, {}
    for at, odd, t in each:
        here, end = spans[t]
        grad_phi = nn(side_ref[0, at, here], prev[at][odd]) + nn(made[at, odd, t], phik_ref[0, 0:end, cols[at, odd]])
        proj_q[at, odd, t] = (grad_phi * phiq_ref[0, here, cols[at, odd]].astype(f32)).astype(bf16)
    for at, odd, t in each:
        here = spans[t][0]
        beside = jnp.concatenate([v_ref[0, here, lanes[at]], one[here]], axis=1)
        grad_phi = nn(beside, later[at][odd]) + tn(column(made, at, odd, t), phiq_ref[0, t * tile :, cols[at, odd]])
        proj_k[at, odd, t] = (grad_phi * phik_ref[0, here, cols[at, odd]].astype(f32)).astype(bf16)
    back_q = {key: nt(proj_q[key], weights[key[:2]]) for key in each}
    back_k = {key: nt(proj_k[key], weights[key[:2]]) for key in each}
    for at in range(BACK_PER):
        both = jnp.concatenate([later[at][0][0:width], later[at][1][0:width]], axis=1)
        gn_pair = side_ref[0, at, :, 0:width].astype(f32)
        gn_sides = [jnp.where(low, gn_pair, 0.0).astype(bf16), jnp.where(low, 0.0, gn_pair).astype(bf16)]
        for t in range(tiles):
            here = spans[t][0]
            grad_v = nt(phik_ref[0, here, 2 * at * feats : 2 * (at + 1) * feats], both)
            for odd in range(2):
                grad_v = grad_v + tn(column(scores, at, odd, t), gn_sides[odd][t * tile :])
            out_ref[0, 2, here, lanes[at]] = grad_v.astype(bf16)
    for part, back, points_ref in ((0, back_q, q_ref), (1, back_k, k_ref)):
        for at in range(BACK_PER):
            for t in range(tiles):
                here = spans[t][0]
                even, odd = back[at, 0, t], back[at, 1, t]
                along = jnp.where(low_tile, even[:, :width], odd[:, :width])
                total = jnp.where(low_tile, even[:, width:], odd[:, width:])
                points = points_ref[0, here, lanes[at]].astype(f32)
                out_ref[0, part, here, lanes[at]] = (s * along + (s * s) * points * total).astype(bf16)


def attention_back_call(index, side, phi_q, phi_k, qkv, omega, carried, later, before, after=()):
    batch, pairs, rows, wide = side.shape
    heads, hd, feats = omega.shape
    steps = pairs // BACK_PER
    model = pairs * 2 * hd
    tile = min(256, rows)
    phi_spec = pl.BlockSpec((1, rows, 2 * BACK_PER * feats), lambda g: (index, 0, g))
    spots = tuple((at * pairs, count) for _, at, count in (carried, later))

    def part(n):
        return pl.BlockSpec((1, rows, 2 * BACK_PER * hd), lambda g: (index, 0, n * steps + g))

    return stacked_call(
        functools.partial(attention_back_kernel, hd, len(carried[0]), len(later[0]), spots, tile),
        (steps,),
        [
            pl.BlockSpec((1, BACK_PER, rows, wide), lambda g: (index, g, 0, 0)),
            phi_spec,
            phi_spec,
            part(0),
            part(1),
            part(2),
            pl.BlockSpec((2 * BACK_PER, hd, feats), lambda g: (g, 0, 0)),
        ]
        + state_specs(carried, pairs, BACK_PER)
        + state_specs(later, pairs, BACK_PER),
        [pl.BlockSpec((1, 3, rows, 2 * BACK_PER * hd), lambda g: (index, 0, 0, g))],
        [jax.ShapeDtypeStruct((batch, 3, rows, model), bf16)],
        (True,),
        before,
        (side, phi_q, phi_k, qkv, qkv, qkv, omega) + tuple(carried[0]) + tuple(later[0]),
        [],
        cost(heads * 2 * rows * (rows * 1024 + 6 * 65536), 12 * MIB),
        after,
    )


def qkv_weight_kernel(fast, n_after, *refs):
    h1_ref, grad_ref = refs[:2]
    outs = refs[2 + n_after :]
    batch, rows, model = h1_ref.shape
    total = tn(h1_ref[...].reshape(batch * rows, model), grad_ref[...].reshape(batch * rows, model))
    if not fast:
        outs[0][...] = total
        return
    far_ref, *near_refs, sum_scr = outs
    sum_scr[...] = total
    piece = model // 8
    for far in range(2):
        for plane in range(4):
            owner = row_owner(far, plane // 2, plane % 2)
            taken = sum_scr[pl.ds(pl.multiple_of(owner * piece, piece), piece), :].astype(bf16)
            if far:
                far_ref[plane, 0] = taken
            else:
                near_refs[plane][0] = taken


def qkv_weight_call(h1, grads, fast, after=()):
    batch, rows, model = h1.shape
    if fast:
        out_specs = [pl.BlockSpec((4, 1, model // 8, model), lambda p: (0, p, 0, 0))]
        out_shapes = [jax.ShapeDtypeStruct((4, 3, model // 8, model), bf16)]
        out_specs += [pl.BlockSpec((1, model // 8, model), lambda p: (p, 0, 0))] * 4
        out_shapes += [jax.ShapeDtypeStruct((3, model // 8, model), bf16)] * 4
    else:
        out_specs = [pl.BlockSpec((model, model), lambda p: (0, p))]
        out_shapes = [jax.ShapeDtypeStruct((model, 3 * model), f32)]
    return pl.pallas_call(
        functools.partial(qkv_weight_kernel, fast, len(after)),
        grid=(3,),
        in_specs=[const_block(h1.shape), pl.BlockSpec((batch, 1, rows, model), lambda p: (0, p, 0, 0))]
        + [pl.BlockSpec(memory_space=pl.ANY)] * len(after),
        out_specs=out_specs,
        out_shape=out_shapes,
        scratch_shapes=[pltpu.VMEM((model, model), f32)] if fast else [],
        compiler_params=params(),
        cost_estimate=cost(6 * batch * rows * model * model, 8 * MIB),
    )(h1, grads, *in_hbm(after))


def inputs_back_kernel(grads_ref, w_ref, x_ref, g1_ref, gains_ref, grad_ref):
    model = x_ref.shape[2]
    grad = nt(grads_ref[0, 0], w_ref[:, :model])
    for part in (1, 2):
        grad = grad + nt(grads_ref[0, part], w_ref[:, part * model : (part + 1) * model])
    xhat, scale = normed(x_ref[0].astype(f32))
    grad_ref[0] = g1_ref[0] + norm_back(grad, xhat, scale, gains_ref[0:1, :])


def inputs_back_call(index, members, grads, w_qkv, inputs, g1, gains, before, after=()):
    batch, rows, model = inputs.shape
    whole = pl.BlockSpec((1, rows, model), lambda j: (index + j, 0, 0))
    return stacked_call(
        inputs_back_kernel,
        (members,),
        [
            pl.BlockSpec((1, 3, rows, model), lambda j: (index + j, 0, 0, 0)),
            const_block(w_qkv.shape),
            whole,
            whole,
            const_block(gains.shape),
        ],
        [whole],
        [jax.ShapeDtypeStruct((batch, rows, model), f32)],
        (True,),
        before,
        (grads, w_qkv, inputs, g1, gains),
        [],
        cost(6 * members * rows * model * model, 6 * members * MIB),
        after,
        62,
    )


def outputs_kernel(groups, *refs):
    act_ref, x1_ref = refs[:2]
    weights = refs[2 : 2 + groups]
    out_ref, down_scr, sems = refs[2 + groups :]
    copies = [
        pltpu.make_async_copy(weights[group].at[:, 1], down_scr.at[group], sems.at[group]) for group in range(groups)
    ]
    for copy in copies:
        copy.start()
    for copy in copies:
        copy.wait()
    down = down_scr[...].reshape(act_ref.shape[2], x1_ref.shape[2])
    out_ref[0] = (x1_ref[0] + nn(act_ref[0], down)).astype(bf16)


def outputs_call(index, act, x1, weights, before, after=()):
    batch, rows, model = x1.shape
    hidden = act.shape[2]
    groups = len(weights)
    shards, _, unit, _ = weights[0].shape
    one = lambda j: (index, 0, 0)
    return stacked_call(
        functools.partial(outputs_kernel, groups),
        (1,),
        [pl.BlockSpec((1, rows, hidden), one), pl.BlockSpec((1, rows, model), one)]
        + [pl.BlockSpec(memory_space=pl.ANY)] * groups,
        [pl.BlockSpec((1, rows, model), one)],
        [jax.ShapeDtypeStruct((batch, rows, model), bf16)],
        (True,),
        before,
        (act, x1) + tuple(weights),
        [pltpu.VMEM((groups, shards, unit, model), bf16), pltpu.SemaphoreType.DMA((groups,))],
        cost(2 * rows * model * hidden, 6 * MIB),
        after,
        62,
    )


CORE = (1, 1)
GATHER = ((16, 8), (8, 16), (2, 4), (4, 2))
PLANE = ((2, 2), (4, 4), (6, 6))
LINE = ((16, 8), (8, 16))


def swap(array, masks):
    return lax.ppermute(array, AXES, [(i, i ^ masks[i & 1]) for i in range(32)])


def small(array, kib):
    return array.size * array.dtype.itemsize <= kib * 1024


def gate(array, *deps, close=False):
    anywhere = pl.BlockSpec(memory_space=pl.ANY)
    return pl.pallas_call(
        lambda *refs: None,
        in_specs=[anywhere] * (1 + len(deps)),
        out_specs=anywhere,
        out_shape=jax.ShapeDtypeStruct(array.shape, array.dtype),
        input_output_aliases={0: 0},
    )(*(in_vmem((array,)) if close or small(array, 700) else (array,)), *[a if small(a, 1000) else in_hbm((a,))[0] for a in deps])


def all_states(local, backward):
    everything = lax.all_gather(local, "seq").astype(f32)
    count, place = lax.axis_size("seq"), lax.axis_index("seq")
    at = jnp.arange(count)
    wanted = (at > place) if backward else (at < place)
    total = jnp.sum(jnp.where(wanted[:, None, None, None], everything, 0.0), axis=0)
    return (total.astype(bf16),)


def chip_half(local, near):
    core = lax.rem(lax.axis_index("seq"), 2)
    half = local.shape[0] // 2
    low, high = [
        (local[rows].astype(f32) + near[rows].astype(f32)).astype(bf16) for rows in (slice(0, half), slice(half, None))
    ]
    return jnp.where(core == 0, low, high)


def sums_kernel(n_terms, plan, *refs):
    terms, outs = refs[:n_terms], refs[n_terms:]
    for out, pieces in zip(outs, plan):
        to = 0
        for names, first, size in pieces:
            total = terms[names[0]][first : first + size].astype(f32)
            for name in names[1:]:
                total = total + terms[name][first : first + size].astype(f32)
            out[to : to + size] = total.astype(out.dtype)
            to += size


def sums(terms, plan, kinds=None, close=()):
    model = terms[0].shape[-1]
    kinds = kinds or [bf16] * len(plan)
    shapes = [
        jax.ShapeDtypeStruct((sum(size for _, _, size in pieces), model), kind)
        for pieces, kind in zip(plan, kinds)
    ]
    return pl.pallas_call(
        functools.partial(sums_kernel, len(terms), plan),
        out_shape=shapes,
        compiler_params=params(),
        cost_estimate=cost(sum(t.size for t in terms), 3 * sum(t.size for t in terms)),
    )(*[in_vmem((t,))[0] if at in close else t for at, t in enumerate(terms)])


def split_kernel(near_ref, got_ref, low_ref, high_ref):
    for at, out_ref in enumerate((low_ref, high_ref)):
        out_ref[...] = (near_ref[at].astype(f32) + got_ref[at].astype(f32)).astype(bf16)


def split_sum(near, got):
    rows, model = near.shape
    half = rows // 2
    block = half // 2
    both = pl.BlockSpec((2, block, model), lambda i: (0, i, 0))
    one = pl.BlockSpec((block, model), lambda i: (i, 0))
    return pl.pallas_call(
        split_kernel,
        grid=(2,),
        in_specs=[both, both],
        out_specs=[one, one],
        out_shape=[jax.ShapeDtypeStruct((half, model), bf16)] * 2,
        compiler_params=params(),
        cost_estimate=cost(near.size, 6 * near.size),
    )(near.reshape(2, half, model), got.reshape(2, half, model))


def along_x(mine):
    return swap(mine, (2, 2))


def assemble_kernel(*refs):
    pieces = refs[:8]
    wqkv_ref, gains_ref, gw_ref, gwout_ref, ggain_ref = refs[8:]
    model = gwout_ref.shape[0]
    rows = model // 8
    for far in range(2):
        for plane in range(4):
            owner = row_owner(far, plane // 2, plane % 2)
            at = pl.ds(pl.multiple_of(owner * rows, rows), rows)
            piece = pieces[4 * far + plane]
            for part in range(3):
                gw_ref[at, part * model : (part + 1) * model] = piece[part * rows : (part + 1) * rows].astype(f32)
            gwout_ref[at, :] = piece[3 * rows : 4 * rows].astype(f32)

            @pl.when(owner == 0)
            def _():
                ggain_ref[1:2, :] = piece[4 * rows : 4 * rows + EXTRA].astype(f32)[0:1]

    ggain_ref[0:1, :] = first_gain(gw_ref, wqkv_ref, gains_ref)


def first_gain(gw_ref, wqkv_ref, gains_ref):
    along = jnp.sum(gw_ref[...] * wqkv_ref[...].astype(f32), axis=1, keepdims=True)
    return jnp.broadcast_to(along, (along.shape[0], 128)).T[0:1, :] / gains_ref[0:1, :]


def assemble_call(pieces, w_qkv, gains):
    model = w_qkv.shape[0]
    return pl.pallas_call(
        assemble_kernel,
        out_shape=[
            jax.ShapeDtypeStruct(w_qkv.shape, f32),
            jax.ShapeDtypeStruct((model, model), f32),
            jax.ShapeDtypeStruct(gains.shape, f32),
        ],
        compiler_params=params(40),
    )(*in_vmem(pieces), w_qkv, gains)


def gains_kernel(gw_ref, gain_ref, wqkv_ref, gains_ref, ggain_ref):
    ggain_ref[0:1, :] = first_gain(gw_ref, wqkv_ref, gains_ref)
    ggain_ref[1:2, :] = gain_ref[0:1, :]


def plane_kernel(far_ref, *refs):
    for at in range(4):
        refs[4 + at][...] = (far_ref[at].astype(f32) + refs[at][...].astype(f32)).astype(bf16)


def plane_sums(far, near):
    return pl.pallas_call(
        plane_kernel,
        out_shape=[jax.ShapeDtypeStruct(a.shape, bf16) for a in near],
        compiler_params=params(),
        cost_estimate=cost(far.size, 6 * far.size),
    )(far, *near)


def next_halves(low, got, n_shard, shards, whole_pieces):
    cut = shards * n_shard
    n_pieces = low.shape[0] - cut
    pieces = [(cut, n_pieces)] * 2 if whole_pieces else [(cut, n_pieces // 2), (cut + n_pieces // 2, n_pieces // 2)]
    return sums(
        [low, got],
        [[((0, 1), at * cut // 2, cut // 2), ((0, 1),) + pieces[at]] for at in range(2)],
        None,
        (1,) if small(got, 700) else (),
    )


def planned(inputs, gains, w_qkv, w_out, shard, omega, cotangent):
    batch, rows, model = inputs.shape
    heads, hd, _ = omega.shape
    pairs = heads // 2
    n_shard, n_piece = 2 * shard.shape[1], model // 8 + EXTRA

    held = shard[None]
    got = swap(held, GATHER[0])
    made = features_call(0, 0, 2, inputs, gains, w_qkv, omega, None)
    held = jnp.concatenate([held, gate(got, made[0])])
    got = swap(held, GATHER[1])
    made = features_call(1, 1, 2, inputs, gains, w_qkv, omega, made, in_vmem((held,)))
    got = gate(got, made[0])
    local = gate(made[4], got)
    near = swap(local, CORE)
    mine = chip_half(local, near)
    held = jnp.concatenate([held, got])
    got = swap(held, GATHER[2])
    far = along_x(mine)
    made = features_call(2, 0, 1, inputs, gains, w_qkv, omega, made, in_hbm((held,)) + in_vmem((mine,)))
    far, got = gate(far, made[0]), gate(got, made[0])
    first = (near, far, swap(far, CORE))
    local = gate(made[4], far, got)
    near = swap(local, CORE)
    mine = chip_half(local, near)
    held = jnp.concatenate([held, got])
    got = swap(held, GATHER[3])
    far = along_x(mine)
    beside = swap(held, CORE)
    qkv, phi_q, phi_k, h1 = made[:4]
    made = mix_call(
        0, 2, inputs, gains, w_out, phi_q, phi_k, qkv, (first, 0, 2 * pairs), None, hd, in_hbm((held,)) + in_vmem((mine,))
    )
    far = gate(far, made[0])
    got, beside = gate(got, far), gate(beside, far)
    second = (near, far, swap(far, CORE))
    made = mix_call(
        2, 1, inputs, gains, w_out, phi_q, phi_k, qkv, (second, 0, pairs), made, hd, in_hbm((got,))
    )
    weights = [beside, gate(swap(got, CORE), made[0]), held, got]
    mixed, rden, x1, h2 = made
    carried = [(first, 0, 2 * pairs), (first, 1, 2 * pairs), (second, 0, pairs)]

    act, pre, g1, ga, gain, side, local = ffn_call(
        h2, cotangent, x1, mixed, rden, phi_q, w_out, gains, weights, hd
    )
    near = swap(local, CORE)
    mine = chip_half(local, near)
    far = along_x(mine)
    send, low = ffn_weight_call(act, pre, cotangent, h2, gain, mixed, ga, n_shard // 2, True, (mine,))
    far = gate(far, low)
    other = swap(far, CORE)
    send = gate(send, other)
    later = (near, far, other)

    def back(b, before, *after):
        return attention_back_call(
            b, side, phi_q, phi_k, qkv, omega, carried[b], (later, b, batch * pairs), before, in_hbm(after)
        )

    def into(b, members, before, *after):
        return inputs_back_call(b, members, grads, w_qkv, inputs, g1, gains, before, in_hbm(after))

    def onto(b, before, *after):
        return outputs_call(b, act, x1, weights, before, in_hbm(after))

    got = swap(send, CORE)
    made = back(0, None)
    got = gate(got, made[0])
    low, high = split_sum(low, got)
    got = swap(high, GATHER[3])
    made = back(1, made, high)
    onto_made = onto(0, None, made[0])
    low, high = next_halves(low, gate(got, onto_made[0]), n_shard, 8, False)
    got = swap(high, GATHER[2])
    made = back(2, made, high)
    low, high = next_halves(low, gate(got, made[0]), n_shard, 4, True)
    got = swap(high, GATHER[1])
    (grads,) = made
    late = qkv_weight_call(h1, grads, True, (high,))

    send, *keep = [a.reshape(a.shape[:-3] + (-1, model)) for a in late]
    keep = plane_sums(swap(send, CORE), keep)
    far = [swap(keep[plane], PLANE[plane - 1]) for plane in (1, 2, 3)]
    into_made = into(0, 2, None, *keep)
    far = [gate(a, into_made[0], close=True) for a in far]
    got = gate(got, *far)
    n_late = keep[0].shape[0]
    (keep,) = sums([keep[0]] + far, [[((0, 1, 2, 3), 0, n_late)]], None, (1, 2, 3))
    line = swap(keep, LINE[0])
    low, high = next_halves(low, got, n_shard, 2, True)
    last = swap(high, GATHER[0])
    into_made = into(2, 1, into_made, keep, high)
    line = gate(line, into_made[0], close=True)
    last = gate(last, line)
    (keep,) = sums([keep, line], [[((0, 1), 0, n_late)]], None, (1,))
    got = swap(keep, LINE[1])
    onto_made = onto(1, onto_made, keep)
    grad_ffn, piece = sums(
        [low, last], [[((0, 1), 0, n_shard)], [((0, 1), n_shard, n_piece)]], [f32, bf16], (1,)
    )
    (keep,) = sums(
        [keep, gate(got, onto_made[0], close=True), piece], [[((0, 1), 0, n_late), ((2,), 0, n_piece)]], None, (1,)
    )
    got = [swap(keep, masks) for masks in PLANE]
    beside = swap(keep, CORE)
    onto_made = onto(2, onto_made, keep)
    near = [keep] + [gate(a, onto_made[0], close=True) for a in got]
    far = [gate(beside, onto_made[0], close=True)] + [swap(a, CORE) for a in near[1:]]
    grad_wqkv, grad_wout, grad_gains = assemble_call(near + far, w_qkv, gains)
    return onto_made[0], into_made[0], grad_gains, grad_wqkv, grad_wout, grad_ffn


def plain(inputs, gains, w_qkv, w_out, shard, omega, cotangent):
    batch, rows, model = inputs.shape
    heads, hd, _ = omega.shape
    pairs = heads // 2
    pair = lax.all_gather(shard, AXES, axis=1, tiled=True)
    hidden = pair.shape[1]
    unit = min(256, hidden)
    weights = [jnp.swapaxes(pair.reshape(2, hidden // unit, unit, model), 0, 1)]
    made = None
    for b in range(batch):
        made = features_call(b, b, batch, inputs, gains, w_qkv, omega, made)
    qkv, phi_q, phi_k, h1, local = made
    sums = all_states(local, False)
    mixed, rden, x1, h2 = mix_call(
        0, batch, inputs, gains, w_out, phi_q, phi_k, qkv, (sums, 0, batch * pairs), None, hd
    )
    act, pre, g1, ga, gain, side, local = ffn_call(
        h2, cotangent, x1, mixed, rden, phi_q, w_out, gains, weights, hd
    )
    later = all_states(local, True)
    both, grad_wout = ffn_weight_call(act, pre, cotangent, h2, gain, mixed, ga, unit, False)
    both = jnp.swapaxes(both.reshape(-1, 2, unit, model), 0, 1).reshape(2, -1, model)
    grad_ffn = lax.psum_scatter(both, AXES, scatter_dimension=1, tiled=True).astype(f32)
    made = None
    for b in range(batch):
        spot = (b, batch * pairs)
        made = attention_back_call(b, side, phi_q, phi_k, qkv, omega, (sums,) + spot, (later,) + spot, made)
    (grads,) = made
    (grad_wqkv,) = qkv_weight_call(h1, grads, False)
    into_made = onto_made = None
    for b in range(batch):
        into_made = inputs_back_call(b, 1, grads, w_qkv, inputs, g1, gains, into_made)
        onto_made = outputs_call(b, act, x1, weights, onto_made)
    grad_wqkv, grad_wout, gain = lax.psum((grad_wqkv, grad_wout, gain), AXES)
    grad_gains = pl.pallas_call(
        gains_kernel,
        out_shape=jax.ShapeDtypeStruct(gains.shape, f32),
        compiler_params=params(),
    )(grad_wqkv, gain, w_qkv, gains)
    return onto_made[0], into_made[0], grad_gains, grad_wqkv, grad_wout, grad_ffn


def on_device(inputs, gains, w_qkv, w_out, ffn_weight, omega, cotangent):
    fast = lax.axis_size("dp") == 8 and lax.axis_size("seq") == 4 and inputs.shape[0] == 3
    outputs, grad_inputs, *grads = (planned if fast else plain)(
        inputs, gains[0], w_qkv[0], w_out[0], ffn_weight[0], jnp.swapaxes(omega[0], 1, 2), cotangent
    )
    grad_gains, grad_wqkv, grad_wout, grad_ffn = grads
    grad_ffn = grad_ffn.reshape(ffn_weight.shape)
    return (outputs, grad_inputs, grad_gains[None], grad_wqkv[None], grad_wout[None], grad_ffn)


def solution(mesh):
    in_specs = (
        P("dp", "seq", None),
        P(),
        P(),
        P(),
        P(None, None, ("dp", "seq"), None),
        P(),
        P("dp", "seq", None),
    )
    out_specs = (
        P("dp", "seq", None),
        P("dp", "seq", None),
        P(),
        P(),
        P(),
        P(None, None, ("dp", "seq"), None),
    )
    return jax.shard_map(
        on_device, mesh=mesh, in_specs=in_specs, out_specs=out_specs, check_vma=False
    )
```
